256 devices in a mesh: batch: 32 (over y, z), hist: 4 (over x), rep: 2 (over core).
Axes of the slice: x: 4, y: 4, z: 8, core: 2. Of those that a mesh axis runs over, the one named last changes fastest.
Arguments:
- node_input: float32 [131072, 512], P(('batch', 'hist', 'rep')), may hold values from -6 to 6
- initial: float32 [131072, 512], P(('batch', 'hist', 'rep')), may hold values from -12 to 12
- cotangent: float32 [131072, 512], P(('batch', 'hist', 'rep')), may hold values from -6 to 6
- weight: float32 [512, 512], replicated, may hold values from -0.25 to 0.25
- edge_weight: float32 [131072, 8], P(('batch', 'hist', 'rep')), may hold values from 0.05 to 0.3
- neighbors: int32 [131072, 8], P(('batch', 'hist', 'rep')), may hold values from 0 to 2815, as said below
- halo_rows: int32 [256, 128, 2], P(('batch', 'hist', 'rep')), may hold values from 0 to 1279
- cold_history: float32 [163840, 512], P(('batch', 'hist')), may hold values from -6 to 6
- hot_history: float32 [2048, 512], P('rep'), may hold values from -6 to 6
- dest_rows: int32 [128, 1024], P(('batch', 'hist')), may hold values from 0 to 1279, as said below
Outputs:
- grad_weight: float32 [512, 512], replicated
- grad_input: float32 [131072, 512], P(('batch', 'hist', 'rep'))
- new_history: float32 [163840, 512], P(('batch', 'hist'))
The draws below stay inside these ranges and needn't reach their ends.
Inputs may be any that keep to these rules, and one draw needn't show every extreme that they name: `neighbors`: column 0 of each node lies in the halo range [512, 768), column 1 in the hot range from 768, the others name nodes of the same device below 512. `dest_rows`: each row of an owner names 1024 distinct rows.
All inputs are finite; a program needn't handle non-finite values.
Results may differ from the reference program's by a relative error of at most 0.0003.
Values sent between devices are 32-bit elements; how exact they have to be, the bound alone decides.
No kernel may reach another device: no remote copies, remote signals or barrier semaphores. Data moves between devices by JAX's collectives and lax.ppermute only.
A program may use at most 128 MiB of HBM per device.

```python
import math
import jax
import jax.numpy as jnp
from jax import lax

D = 512
NB = 512
CAP = 2
HOT = 2048
K = 8
OWNERS = 128
HALO = 256
COLD_DEV = 1280
COLD = 163840
NODES = 131072
N_REP = 2
DEVICES = 256


def draw_neighbors(key, part):
    key = jax.random.fold_in(key, 11)
    first, second, third = jax.random.split(key, 3)
    total = NB * DEVICES
    halo_col = NB + jax.random.randint(first, (total, 1), 0, OWNERS * CAP)
    hot_col = NB + OWNERS * CAP + jax.random.randint(second, (total, 1), 0, HOT)
    local_col = jax.random.randint(third, (total, K - 2), 0, NB)
    return jnp.concatenate([halo_col, hot_col, local_col], axis=1).astype(jnp.int32)


def draw_dest_rows(key, part):
    key = jax.random.fold_in(key, 23)
    keys = jax.random.split(key, OWNERS)
    return jax.vmap(lambda single: jax.random.permutation(single, COLD_DEV)[:N_REP * NB])(keys).astype(jnp.int32)


def plant(entries, stream_key, smallest, high):
    index_at = [jax.random.randint(jax.random.fold_in(stream_key, axis), (), 0, length) for axis, length in enumerate(entries.shape)]
    longest = entries.shape.index(max(entries.shape))
    next_to = index_at[:longest] + [(index_at[longest] + 1) % entries.shape[longest]] + index_at[longest + 1:]
    return entries.at[tuple(index_at)].set(smallest).at[tuple(next_to)].set(high)


def steps_of(stream_key, extent, cuts, low, largest):
    def one(axis_at, blocks):
        steps = jax.random.uniform(jax.random.fold_in(jax.random.fold_in(stream_key, 6), axis_at), (blocks,), jnp.float32, low / len(cuts), largest / len(cuts))
        return jnp.repeat(jnp.exp(steps), extent[axis_at] // blocks).reshape((-1,) + (1,) * (len(extent) - axis_at - 1))

    factor_of = one(*cuts[0])
    for cut in cuts[1:]:
        factor_of = factor_of * one(*cut)
    return factor_of


def gaussian(rng, shape, width, bound, shards=(), held_as=jnp.bfloat16):
    loudness = steps_of(rng, shape, shards, -0.22, 0.18) if shards else 1.0
    values = jax.random.normal(rng, shape, jnp.float32) * width * loudness
    return jnp.minimum(jnp.maximum(values, -bound), bound).astype(held_as)


def setup_inputs(seed: int = 0) -> dict:
    key_list = jax.random.split(jax.random.key(seed), 11)
    return {
        "node_input": gaussian(key_list[0], (NODES, D), 1.0, 6.0, ((0, 256),), jnp.float32),
        "initial": gaussian(key_list[1], (NODES, D), 2.0, 12.0, ((0, 256),), jnp.float32),
        "cotangent": gaussian(key_list[2], (NODES, D), 1.0, 6.0, ((0, 256),), jnp.float32),
        "weight": gaussian(key_list[3], (D, D), D ** -0.5, 0.25, (), jnp.float32),
        "edge_weight": jnp.clip(jnp.exp(math.log(0.3) - 1.7917595 * jax.random.uniform(key_list[4], (NODES, K), jnp.float32) ** steps_of(key_list[4], (NODES, K), ((0, 256),), -0.2, 0.2)), 0.05, 0.3),
        "neighbors": draw_neighbors(jax.random.fold_in(key_list[10], 71), 0),
        "halo_rows": plant(jax.random.randint(key_list[6], (DEVICES, OWNERS, CAP), 0, COLD_DEV), jax.random.fold_in(key_list[6], 1), 0, COLD_DEV - 1).astype(jnp.int32),
        "cold_history": gaussian(key_list[7], (COLD, D), 1.0, 6.0, ((0, 128),), jnp.float32),
        "hot_history": gaussian(key_list[8], (HOT, D), 1.0, 6.0, ((0, 2),), jnp.float32),
        "dest_rows": draw_dest_rows(jax.random.fold_in(key_list[10], 71), 0),
    }


ALPHA = 0.1
BETA = math.log(1.5)
HIGH = lax.Precision.HIGHEST

def reference(node_input, initial, cotangent, weight, edge_weight, neighbors, halo_rows, cold_history, hot_history, dest_rows):
    total_dev = NODES // NB
    cold = cold_history.reshape(OWNERS, COLD_DEV, D)
    owner_ids = jnp.arange(OWNERS)[:, None]

    def per_device(carry, index):
        rows = lax.dynamic_slice_in_dim(node_input, index * NB, NB, 0)
        start_rows = lax.dynamic_slice_in_dim(initial, index * NB, NB, 0)
        grad_out = lax.dynamic_slice_in_dim(cotangent, index * NB, NB, 0)
        weights = lax.dynamic_slice_in_dim(edge_weight, index * NB, NB, 0)
        columns = lax.dynamic_slice_in_dim(neighbors, index * NB, NB, 0)
        wanted = lax.dynamic_index_in_dim(halo_rows, index, 0, keepdims=False)
        halo = cold[owner_ids, wanted].reshape(HALO, D)
        table = jnp.concatenate([rows, halo, hot_history], axis=0)
        agg = jnp.zeros((NB, D), jnp.float32)
        for slot in range(K):
            agg = agg + weights[:, slot:slot + 1] * table[columns[:, slot]]
        z = (1.0 - ALPHA) * agg + ALPHA * start_rows
        u = (1.0 - BETA) * z + BETA * jnp.dot(z, weight, precision=HIGH, preferred_element_type=jnp.float32)
        embed, pull = jax.vjp(lambda v: jax.nn.gelu(v, approximate=True), u)
        du = pull(grad_out)[0]
        dz = (1.0 - BETA) * du + BETA * jnp.dot(du, weight.T, precision=HIGH, preferred_element_type=jnp.float32)
        term = jnp.dot(z.T, du, precision=HIGH, preferred_element_type=jnp.float32)
        grad_rows = jnp.zeros((NB + 1, D), jnp.float32)
        for slot in range(K):
            target = jnp.where(columns[:, slot] < NB, columns[:, slot], NB).astype(jnp.int32)
            grad_rows = grad_rows + jax.ops.segment_sum(weights[:, slot:slot + 1] * dz, target, num_segments=NB + 1)
        return (carry + term, (embed, (1.0 - ALPHA) * grad_rows[:NB]))
    init = jnp.zeros((D, D), jnp.float32)
    summed, (embeds, grads) = lax.scan(per_device, init, jnp.arange(total_dev))
    grad_weight = summed * (BETA / math.sqrt(NODES))
    grad_input = grads.reshape(NODES, D)
    per_q = NB // OWNERS
    sent = embeds.reshape(OWNERS, N_REP, OWNERS, per_q, D)
    received = jnp.transpose(sent, (2, 1, 0, 3, 4)).reshape(OWNERS, 2 * NB, D)

    def write(shard, places, values):
        return shard.at[places].set(values)
    new_history = jax.vmap(write)(cold, dest_rows, received).reshape(COLD, D)
    return (grad_weight, grad_input, new_history)
```

```python
import math

import jax
import jax.numpy as jnp
from jax import lax
from jax.sharding import PartitionSpec as P

ALPHA = 0.1
BETA = math.log(1.5)
HIGH = lax.Precision.HIGH
OWN = ("batch", "hist")
SWAP = [(0, 1), (1, 0)]


def dot(a, b, dims=(((1,), (0,)), ((), ()))):
    return lax.dot_general(a, b, dims, precision=HIGH, preferred_element_type=jnp.float32)


def exchange(v):
    return lax.all_to_all(v, OWN, split_axis=0, concat_axis=0, tiled=True)


def pair(mine, core):
    other = lax.ppermute(mine, "rep", SWAP)
    first = jnp.where(core == 0, mine, other)
    second = jnp.where(core == 0, other, mine)
    return jnp.concatenate([first, second], axis=0)


def body(
    node_input,
    initial,
    cotangent,
    weight,
    edge_weight,
    neighbors,
    halo_rows,
    cold_history,
    hot_history,
    dest_rows,
):
    local_rows, width = node_input.shape
    owners = lax.axis_size(OWN)
    core = lax.axis_index("rep")
    halo_count = owners * halo_rows.shape[2]
    found = cold_history[exchange(halo_rows[0])]
    halo = exchange(found).reshape(halo_count, width)
    hot = pair(hot_history, core)
    ids = lax.broadcasted_iota(jnp.int32, (1, local_rows), 1)
    tile = jnp.zeros((local_rows, local_rows), jnp.float32)
    for slot in range(2, neighbors.shape[1]):
        tile = tile + jnp.where(
            neighbors[:, slot : slot + 1] == ids, edge_weight[:, slot : slot + 1], 0.0
        )
    hot_rows = hot[neighbors[:, 1] - local_rows - halo_count]
    agg = dot(tile, node_input) + edge_weight[:, 1:2] * hot_rows
    halo_ids = lax.broadcasted_iota(jnp.int32, (1, halo_count), 1) + local_rows
    halo_tile = jnp.where(neighbors[:, :1] == halo_ids, edge_weight[:, :1], 0.0)
    agg = agg + dot(halo_tile, halo)
    z = (1.0 - ALPHA) * agg + ALPHA * initial
    u = (1.0 - BETA) * z + BETA * dot(z, weight)
    embed, pull = jax.vjp(lambda v: jax.nn.gelu(v, approximate=True), u)
    du = pull(cotangent)[0]
    all_nodes = local_rows * lax.axis_size(("batch", "hist", "rep"))
    term = dot(z, du, (((0,), (0,)), ((), ()))) * (BETA / math.sqrt(all_nodes))
    half = width // 2
    keep = lax.dynamic_slice_in_dim(term, core * half, half, 0)
    give = lax.dynamic_slice_in_dim(term, (1 - core) * half, half, 0)
    keep = keep + lax.ppermute(give, "rep", SWAP)
    outgoing = jnp.concatenate(
        [embed.reshape(owners, -1, 128), keep.reshape(owners, -1, 128)], axis=1
    )
    arrived = exchange(outgoing)
    cut = local_rows * width // owners // 128
    piece = jnp.sum(arrived[:, cut:], axis=0)
    pieces = exchange(jnp.broadcast_to(piece[None], (owners,) + piece.shape))
    grad_weight = pair(pieces.reshape(half, width), core)
    dz = (1.0 - BETA) * du + BETA * dot(du, weight, (((1,), (1,)), ((), ())))
    grad_input = (1.0 - ALPHA) * dot(tile, dz, (((0,), (0,)), ((), ())))
    received = pair(arrived[:, :cut].reshape(local_rows, width), core)
    new_history = cold_history.at[dest_rows[0]].set(received, unique_indices=True)
    return (grad_weight, grad_input, new_history)


def solution(mesh):
    return jax.shard_map(
        body,
        mesh=mesh,
        in_specs=(
            P(("batch", "hist", "rep"), None),
            P(("batch", "hist", "rep"), None),
            P(("batch", "hist", "rep"), None),
            P(),
            P(("batch", "hist", "rep"), None),
            P(("batch", "hist", "rep"), None),
            P(("batch", "hist", "rep"), None, None),
            P(("batch", "hist"), None),
            P("rep", None),
            P(("batch", "hist"), None),
        ),
        out_specs=(P(), P(("batch", "hist", "rep"), None), P(("batch", "hist"), None)),
        check_vma=False,
    )
```

```python
import math

import jax
import jax.numpy as jnp
from jax import lax
from jax.experimental import pallas as pl
from jax.experimental.pallas import tpu as pltpu
from jax.sharding import PartitionSpec as P

ALPHA = 0.1
BETA = math.log(1.5)
OWN = ("batch", "hist")
SWAP = [(0, 1), (1, 0)]
F32 = jnp.float32
BF16 = jnp.bfloat16
GELU_C = math.sqrt(2.0 / math.pi)
GELU_A = 0.044715
VMEM = pl.BlockSpec(memory_space=pltpu.VMEM)
SMEM = pl.BlockSpec(memory_space=pltpu.SMEM)
MIB = 1 << 20


def dot(a, b, left=1, right=0):
    return lax.dot_general(a, b, (((left,), (right,)), ((), ())), preferred_element_type=F32)


def split(v):
    high = v.astype(BF16)
    return high, (v - high.astype(F32)).astype(BF16)


def dot3(a, b, left=1, right=0):
    return dot(a[0], b[0], left, right) + (dot(a[0], b[1], left, right) + dot(a[1], b[0], left, right))


def lanes(rows, columns):
    return lax.broadcasted_iota(jnp.int32, (rows, columns), 1)


def one_hot(column, count):
    return (column == lanes(column.shape[0], count)).astype(BF16)


def call(kernel, outs, args, scalars=0, scratch=(), limit=16, flops=0, aliases=None):
    count = sum(math.prod(o[0]) for o in outs) * 4 + sum(math.prod(a.shape) for a in args) * 4
    return pl.pallas_call(
        kernel,
        out_shape=[jax.ShapeDtypeStruct(*o) for o in outs],
        in_specs=[SMEM] * scalars + [VMEM] * (len(args) - scalars),
        out_specs=[VMEM] * len(outs),
        scratch_shapes=list(scratch),
        input_output_aliases=aliases or {},
        compiler_params=pltpu.CompilerParams(vmem_limit_bytes=limit * MIB),
        cost_estimate=pl.CostEstimate(flops=flops, bytes_accessed=count, transcendentals=0),
    )(*args)


def gather_kernel(idx_ref, cold_ref, out_ref):
    owners, per = idx_ref.shape
    high, low = split(cold_ref[...])
    pick = jnp.concatenate(
        [one_hot(idx_ref[:, s : s + 1], cold_ref.shape[0]) for s in range(per)], axis=0
    )
    found = dot(pick, high) + dot(pick, low)
    for s in range(per):
        for l in range(4):
            out_ref[pl.ds(s * 4 + l, owners, stride=per * 4), :] = found[
                s * owners : (s + 1) * owners, l * 128 : (l + 1) * 128
            ]


def prepare_kernel(
    core_ref, nbr_ref, ew_ref, node_ref, init_ref, mine_ref, other_ref,
    part_ref, high_ref, low_ref, pick_ref, *, halo_count,
):
    rows = node_ref.shape[0]
    core = core_ref[0]
    nbr = nbr_ref[...]
    ew = ew_ref[...]
    ids = lanes(rows, rows)
    tile = jnp.zeros((rows, rows), F32)
    for k in range(2, nbr.shape[1]):
        tile = tile + jnp.where(nbr[:, k : k + 1] == ids, ew[:, k : k + 1], 0.0)
    tiles = split(tile)
    high_ref[...] = tiles[0]
    low_ref[...] = tiles[1]
    half = mine_ref.shape[0]
    hot = nbr[:, 1:2] - (rows + halo_count)
    picked = jnp.zeros((rows, node_ref.shape[1]), F32)
    for ref, start in ((mine_ref, core * half), (other_ref, (1 - core) * half)):
        choose = one_hot(hot - start, half)
        for part in split(ref[...]):
            picked = picked + dot(choose, part)
    agg = dot3(tiles, split(node_ref[...])) + ew[:, 1:2] * picked
    part_ref[...] = (1.0 - ALPHA) * agg + ALPHA * init_ref[...]
    place = nbr[:, :1] - rows
    pick_ref[...] = one_hot((place & 1) * (halo_count // 2) + (place >> 1), halo_count)


def layer_kernel(
    core_ref, halo_ref, pick_ref, ew_ref, part_ref, weight_ref, cot_ref,
    embed_ref, keep_ref, give_ref, du_ref, term_ref,
):
    owners = halo_ref.shape[0] // 8
    halo = jnp.concatenate(
        [
            jnp.concatenate(
                [halo_ref[pl.ds(s * 4 + l, owners, stride=8), :] for l in range(4)], axis=1
            )
            for s in range(2)
        ],
        axis=0,
    )
    pick = pick_ref[...]
    high, low = split(halo)
    z = part_ref[...] + ((1.0 - ALPHA) * ew_ref[:, :1]) * (dot(pick, high) + dot(pick, low))
    zs = split(z)
    u = (1.0 - BETA) * z + BETA * dot3(zs, split(weight_ref[...]))
    square = u * u
    bent = jnp.tanh(GELU_C * (u + GELU_A * (square * u)))
    embed_ref[...] = (0.5 * u) * (1.0 + bent)
    slope = 0.5 * (1.0 + bent) + (0.5 * u) * (1.0 - bent * bent) * (
        GELU_C * (1.0 + (3.0 * GELU_A) * square)
    )
    du = cot_ref[...] * slope
    du_ref[...] = du
    term_ref[...] = dot3(zs, split(du), 0, 0)
    half = term_ref.shape[0] // 2
    core = core_ref[0]
    keep_ref[...] = term_ref[pl.ds(pl.multiple_of(core * half, half), half), :]
    give_ref[...] = term_ref[pl.ds(pl.multiple_of((1 - core) * half, half), half), :]


def pack_kernel(embed_ref, keep_ref, got_ref, out_ref):
    groups = out_ref.shape[0]
    top = lax.broadcasted_iota(jnp.int32, (groups, 2, 8, 128), 2) < 4
    for pair in range(2):
        x, y = (
            embed_ref[:, l * 128 : (l + 1) * 128].reshape(groups, 2, 8, 128)
            for l in (2 * pair, 2 * pair + 1)
        )
        even = jnp.where(top, x, pltpu.roll(y, 4, 2))
        odd = jnp.where(top, pltpu.roll(x, 4, 2), y)
        for h in range(2):
            out_ref[:, 2 * h, 8 * pair : 8 * pair + 8, :] = even[:, h]
            out_ref[:, 2 * h + 1, 8 * pair : 8 * pair + 8, :] = odd[:, h]
    for l in range(4):
        at = slice(l * 128, (l + 1) * 128)
        out_ref[:, l, 16:24, :] = (keep_ref[:, at] + got_ref[:, at]).reshape(groups, 8, 128)


def backward_kernel(du_ref, weight_ref, high_ref, low_ref, out_ref):
    du = du_ref[...]
    dz = (1.0 - BETA) * du + BETA * dot3(split(du), split(weight_ref[...]), 1, 1)
    out_ref[...] = (1.0 - ALPHA) * dot3((high_ref[...], low_ref[...]), split(dz), 0, 0)


def sum_kernel(arrived_ref, piece_ref, recv_ref, *, scale):
    piece = jnp.sum(arrived_ref[:, 16:24, :], axis=0) * scale
    piece_ref[...] = jnp.broadcast_to(piece[None], piece_ref.shape)
    recv_ref[...] = arrived_ref[:, :16, :]


def history_kernel(core_ref, dest_ref, mine_ref, other_ref, cold_ref, out_ref, high_ref, low_ref):
    core = core_ref[0]
    owners = mine_ref.shape[0] // 16
    rows = 4 * owners
    for r, ref in enumerate((mine_ref, other_ref)):
        for s in range(4):
            for l in range(4):
                high, low = split(ref[pl.ds(4 * l + s, owners, stride=16), :])
                at = pl.ds(r * rows + s * owners, owners)
                high_ref[at, l * 128 : (l + 1) * 128] = high
                low_ref[at, l * 128 : (l + 1) * 128] = low
    dest = jnp.concatenate(
        [dest_ref[pl.ds(core, 1), :], dest_ref[pl.ds(1 - core, 1), :]], axis=1
    )
    step = 256
    for start in range(0, cold_ref.shape[0], step):
        ids = lax.broadcasted_iota(jnp.int32, (step, 2 * rows), 0) + start
        hit = jnp.where(ids == dest, 1.0, 0.0)
        count = jnp.sum(hit, axis=1, keepdims=True)
        place = hit.astype(BF16)
        written = dot(place, high_ref[...]) + dot(place, low_ref[...])
        at = pl.ds(start, step)
        out_ref[at, :] = jnp.where(count > 0.5, written, cold_ref[at, :])


def assemble_kernel(core_ref, mine_ref, other_ref, out_ref):
    core = core_ref[0]
    half = out_ref.shape[0] // 2
    for ref, which in ((mine_ref, core), (other_ref, 1 - core)):
        at = pl.ds(pl.multiple_of(which * half, half), half)
        for l in range(4):
            out_ref[at, l * 128 : (l + 1) * 128] = ref[:, l].reshape(half, 128)


def exchange(v):
    return lax.all_to_all(v, OWN, split_axis=0, concat_axis=0, tiled=True)


def swap(v):
    return lax.ppermute(v, "rep", SWAP)


def body(
    node_input,
    initial,
    cotangent,
    weight,
    edge_weight,
    neighbors,
    halo_rows,
    cold_history,
    hot_history,
    dest_rows,
):
    rows, width = node_input.shape
    owners = lax.axis_size(OWN)
    halo_count = owners * halo_rows.shape[2]
    core = lax.axis_index("rep").astype(jnp.int32).reshape(1)
    full = (rows, width)
    wanted = exchange(halo_rows[0])
    part, high, low, pick = call(
        lambda *r: prepare_kernel(*r, halo_count=halo_count),
        [(full, F32), ((rows, rows), BF16), ((rows, rows), BF16), ((rows, halo_count), BF16)],
        (core, neighbors, edge_weight, node_input, initial, hot_history, swap(hot_history)),
        scalars=1,
        flops=6 * 10**9,
    )
    wanted, part = lax.optimization_barrier((wanted, part))
    (found,) = call(
        gather_kernel,
        [((halo_count * 4, 128), F32)],
        (wanted, cold_history),
        flops=10**9,
    )
    halo = exchange(found)
    half = (rows // 2, width)
    embed, keep, give, du = call(
        layer_kernel,
        [(full, F32), (half, F32), (half, F32), (full, F32)],
        (core, halo, pick, edge_weight, part, weight, cotangent),
        scalars=1,
        scratch=[pltpu.VMEM((width, width), F32)],
        flops=2 * 10**9,
    )
    (outgoing,) = call(
        pack_kernel, [((owners // 4, 4, 24, 128), F32)], (embed, keep, swap(give))
    )
    arrived = exchange(outgoing.reshape(owners * 24, 128)).reshape(owners, 24, 128)
    (grad_input,) = call(
        backward_kernel, [(full, F32)], (du, weight, high, low), flops=2 * 10**9
    )
    arrived, grad_input = lax.optimization_barrier((arrived, grad_input))
    all_nodes = rows * lax.axis_size(("batch", "hist", "rep"))
    piece, recv = call(
        lambda *r: sum_kernel(*r, scale=BETA / math.sqrt(all_nodes)),
        [((owners, 8, 128), F32), ((owners, 16, 128), F32)],
        (arrived,),
    )
    pieces = exchange(piece.reshape(owners * 8, 128))
    recv = recv.reshape(owners * 16, 128)
    dest = jnp.transpose(dest_rows.reshape(2, owners, 4), (0, 2, 1)).reshape(2, rows)
    (new_history,) = call(
        history_kernel,
        [(cold_history.shape, F32)],
        (core, dest, recv, swap(recv), cold_history),
        scalars=1,
        scratch=[pltpu.VMEM((2 * rows, width), BF16), pltpu.VMEM((2 * rows, width), BF16)],
        flops=4 * 10**9,
    )
    pieces, new_history = lax.optimization_barrier((pieces, new_history))
    shape = (owners // 4, 4, 8, 128)
    (grad_weight,) = call(
        assemble_kernel,
        [((width, width), F32)],
        (core, pieces.reshape(shape), swap(pieces).reshape(shape)),
        scalars=1,
    )
    return (grad_weight, grad_input, new_history)


def solution(mesh):
    return jax.shard_map(
        body,
        mesh=mesh,
        in_specs=(
            P(("batch", "hist", "rep"), None),
            P(("batch", "hist", "rep"), None),
            P(("batch", "hist", "rep"), None),
            P(),
            P(("batch", "hist", "rep"), None),
            P(("batch", "hist", "rep"), None),
            P(("batch", "hist", "rep"), None, None),
            P(("batch", "hist"), None),
            P("rep", None),
            P(("batch", "hist"), None),
        ),
        out_specs=(P(), P(("batch", "hist", "rep"), None), P(("batch", "hist"), None)),
        check_vma=False,
    )
```

```python
import functools
import math

import jax
import jax.numpy as jnp
from jax import lax
from jax.experimental import pallas as pl
from jax.experimental.pallas import tpu as pltpu
from jax.sharding import PartitionSpec as P

ALPHA = 0.1
BETA = math.log(1.5)
OWN = ("batch", "hist")
F32 = jnp.float32
BF16 = jnp.bfloat16
GELU_C = math.sqrt(2.0 / math.pi)
GELU_A = 0.044715
VMEM = pl.BlockSpec(memory_space=pltpu.VMEM)
SMEM = pl.BlockSpec(memory_space=pltpu.SMEM)
MIB = 1 << 20


def dot(a, b, left=1, right=0):
    return lax.dot_general(a, b, (((left,), (right,)), ((), ())), preferred_element_type=F32)


def split(v):
    high = v.astype(BF16)
    return high, (v - high.astype(F32)).astype(BF16)


def dot3(a, b, left=1, right=0):
    return dot(a[0], b[0], left, right) + (dot(a[0], b[1], left, right) + dot(a[1], b[0], left, right))


def lanes(rows, columns):
    return lax.broadcasted_iota(jnp.int32, (rows, columns), 1)


def one_hot(column, count):
    return (column == lanes(column.shape[0], count)).astype(BF16)


def call(kernel, outs, args, scalars=0, scratch=(), limit=8, flops=0, aliases=None):
    count = sum(math.prod(o[0]) for o in outs) * 4 + sum(math.prod(a.shape) for a in args) * 4
    return pl.pallas_call(
        kernel,
        out_shape=[jax.ShapeDtypeStruct(*o) for o in outs],
        in_specs=[SMEM] * scalars + [VMEM] * (len(args) - scalars),
        out_specs=[VMEM] * len(outs),
        scratch_shapes=list(scratch),
        input_output_aliases=aliases or {},
        compiler_params=pltpu.CompilerParams(vmem_limit_bytes=limit * MIB),
        cost_estimate=pl.CostEstimate(flops=flops, bytes_accessed=count, transcendentals=0),
    )(*args)


def gather_kernel(idx_ref, cold_ref, out_ref):
    owners, per = idx_ref.shape
    high, low = split(cold_ref[...])
    pick = jnp.concatenate(
        [one_hot(idx_ref[:, s : s + 1], cold_ref.shape[0]) for s in range(per)], axis=0
    )
    found = dot(pick, high) + dot(pick, low)
    for s in range(per):
        for l in range(4):
            out_ref[pl.ds(s * 4 + l, owners, stride=per * 4), :] = found[
                s * owners : (s + 1) * owners, l * 128 : (l + 1) * 128
            ]


def prepare_kernel(
    core_ref, nbr_ref, ew_ref, node_ref, init_ref, mine_ref, other_ref,
    part_ref, high_ref, low_ref, pick_ref, *, halo_count,
):
    rows = node_ref.shape[0]
    core = core_ref[0]
    nbr = nbr_ref[...]
    ew = ew_ref[...]
    ids = lanes(rows, rows)
    tile = jnp.zeros((rows, rows), F32)
    for k in range(2, nbr.shape[1]):
        tile = tile + jnp.where(nbr[:, k : k + 1] == ids, ew[:, k : k + 1], 0.0)
    tiles = split(tile)
    high_ref[...] = tiles[0]
    low_ref[...] = tiles[1]
    half = mine_ref.shape[0]
    hot = nbr[:, 1:2] - (rows + halo_count)
    picked = jnp.zeros((rows, node_ref.shape[1]), F32)
    for ref, start in ((mine_ref, core * half), (other_ref, (1 - core) * half)):
        choose = one_hot(hot - start, half)
        for part in split(ref[...]):
            picked = picked + dot(choose, part)
    agg = dot3(tiles, split(node_ref[...])) + ew[:, 1:2] * picked
    part_ref[...] = (1.0 - ALPHA) * agg + ALPHA * init_ref[...]
    place = nbr[:, :1] - rows
    pick_ref[...] = one_hot((place & 1) * (halo_count // 2) + (place >> 1), halo_count)


def layer_kernel(
    halo_ref, pick_ref, ew_ref, part_ref, weight_ref, out_ref, high_ref, low_ref, u_ref
):
    owners = halo_ref.shape[0] // 8
    halo = jnp.concatenate(
        [
            jnp.concatenate(
                [halo_ref[pl.ds(s * 4 + l, owners, stride=8), :] for l in range(4)], axis=1
            )
            for s in range(2)
        ],
        axis=0,
    )
    pick = pick_ref[...]
    high, low = split(halo)
    z = part_ref[...] + ((1.0 - ALPHA) * ew_ref[:, :1]) * (dot(pick, high) + dot(pick, low))
    zs = split(z)
    high_ref[...] = zs[0]
    low_ref[...] = zs[1]
    u = (1.0 - BETA) * z + BETA * dot3(zs, split(weight_ref[...]))
    u_ref[...] = u
    embed = (0.5 * u) * (1.0 + jnp.tanh(GELU_C * (u + GELU_A * (u * u * u))))
    groups = out_ref.shape[0]
    top = lax.broadcasted_iota(jnp.int32, (groups, 2, 8, 128), 2) < 4
    for pair in range(2):
        x, y = (
            embed[:, l * 128 : (l + 1) * 128].reshape(groups, 2, 8, 128)
            for l in (2 * pair, 2 * pair + 1)
        )
        even = jnp.where(top, x, pltpu.roll(y, 4, 2))
        odd = jnp.where(top, pltpu.roll(x, 4, 2), y)
        for h in range(2):
            out_ref[:, 2 * h, 8 * pair : 8 * pair + 8, :] = even[:, h]
            out_ref[:, 2 * h + 1, 8 * pair : 8 * pair + 8, :] = odd[:, h]


def weight_kernel(
    core_ref, u_ref, high_ref, low_ref, cot_ref, keep_ref, give_ref, du_ref, term_ref
):
    u = u_ref[...]
    square = u * u
    bent = jnp.tanh(GELU_C * (u + GELU_A * (square * u)))
    slope = 0.5 * (1.0 + bent) + (0.5 * u) * (1.0 - bent * bent) * (
        GELU_C * (1.0 + (3.0 * GELU_A) * square)
    )
    du = cot_ref[...] * slope
    du_ref[...] = du
    term_ref[...] = dot3((high_ref[...], low_ref[...]), split(du), 0, 0)
    half = term_ref.shape[0] // 2
    core = core_ref[0]
    keep_ref[...] = term_ref[pl.ds(pl.multiple_of(core * half, half), half), :]
    give_ref[...] = term_ref[pl.ds(pl.multiple_of((1 - core) * half, half), half), :]


def scatter_kernel(me_ref, *refs):
    terms, outs, total_ref = refs[: -1 - 4], refs[-1 - 4 : -1], refs[-1]
    total_ref[...] = functools.reduce(lambda x, y: x + y, [t[...] for t in terms])
    size = outs[0].shape[0]
    for shift, out in enumerate(outs):
        at = jnp.bitwise_xor(me_ref[0], shift) * size
        out[...] = total_ref[pl.ds(pl.multiple_of(at, size), size), :]


def total_kernel(*refs):
    terms = [t[...] for t in refs[:-1]]
    while len(terms) > 1:
        terms = [x + y for x, y in zip(terms[::2], terms[1::2])]
    refs[-1][...] = terms[0]


def join_kernel(me_ref, *refs, scale=None):
    size = refs[0].shape[0]
    for shift, part in enumerate(refs[:-1]):
        at = jnp.bitwise_xor(me_ref[0], shift) * size
        value = part[...] if scale is None else part[...] * scale
        refs[-1][pl.ds(pl.multiple_of(at, size), size), :] = value


def backward_kernel(du_ref, weight_ref, high_ref, low_ref, out_ref):
    du = du_ref[...]
    dz = (1.0 - BETA) * du + BETA * dot3(split(du), split(weight_ref[...]), 1, 1)
    out_ref[...] = (1.0 - ALPHA) * dot3((high_ref[...], low_ref[...]), split(dz), 0, 0)


def history_kernel(core_ref, dest_ref, mine_ref, other_ref, cold_ref, out_ref, high_ref, low_ref):
    core = core_ref[0]
    owners = mine_ref.shape[0] // 16
    rows = 4 * owners
    for r, ref in enumerate((mine_ref, other_ref)):
        for s in range(4):
            for l in range(4):
                high, low = split(ref[pl.ds(4 * l + s, owners, stride=16), :])
                at = pl.ds(r * rows + s * owners, owners)
                high_ref[at, l * 128 : (l + 1) * 128] = high
                low_ref[at, l * 128 : (l + 1) * 128] = low
    dest = jnp.concatenate(
        [dest_ref[pl.ds(core, 1), :], dest_ref[pl.ds(1 - core, 1), :]], axis=1
    )
    step = 256
    for start in range(0, cold_ref.shape[0], step):
        ids = lax.broadcasted_iota(jnp.int32, (step, 2 * rows), 0) + start
        hit = jnp.where(ids == dest, 1.0, 0.0)
        count = jnp.sum(hit, axis=1, keepdims=True)
        place = hit.astype(BF16)
        written = dot(place, high_ref[...]) + dot(place, low_ref[...])
        at = pl.ds(start, step)
        out_ref[at, :] = jnp.where(count > 0.5, written, cold_ref[at, :])


def exchange(v):
    return lax.all_to_all(v, OWN, split_axis=0, concat_axis=0, tiled=True)


def swap(v):
    return lax.ppermute(v, "rep", [(0, 1), (1, 0)])


def move(v, axis, mask):
    count = lax.axis_size(axis)
    return lax.ppermute(v, axis, [(i, i ^ mask) for i in range(count)])


def scatter(me, axis, unit, *terms):
    size = terms[0].shape[0] // 4
    piece = ((size, terms[0].shape[1]), F32)
    outs = call(
        scatter_kernel,
        [piece] * 4,
        (me,) + terms,
        scalars=1,
        scratch=[pltpu.VMEM(terms[0].shape, F32)],
    )
    return [outs[0]] + [move(outs[shift], axis, shift * unit) for shift in (1, 2, 3)]


def total(*terms):
    return call(total_kernel, [(terms[0].shape, F32)], terms)[0]


def join(me, parts, scale=None):
    rows, width = parts[0].shape
    return call(
        functools.partial(join_kernel, scale=scale),
        [((rows * len(parts), width), F32)],
        (me,) + tuple(parts),
        scalars=1,
    )[0]


def gather(me, axis, unit, v):
    return join(me, [v] + [move(v, axis, shift * unit) for shift in (1, 2, 3)])


def body(
    node_input,
    initial,
    cotangent,
    weight,
    edge_weight,
    neighbors,
    halo_rows,
    cold_history,
    hot_history,
    dest_rows,
):
    rows, width = node_input.shape
    owners = lax.axis_size(OWN)
    halo_count = owners * halo_rows.shape[2]
    core = lax.axis_index("rep").astype(jnp.int32).reshape(1)
    full = (rows, width)
    wanted = exchange(halo_rows[0])
    part, high, low, pick = call(
        lambda *r: prepare_kernel(*r, halo_count=halo_count),
        [(full, F32), ((rows, rows), BF16), ((rows, rows), BF16), ((rows, halo_count), BF16)],
        (core, neighbors, edge_weight, node_input, initial, hot_history, swap(hot_history)),
        scalars=1,
        limit=60,
        flops=6 * 10**9,
    )
    (found,) = call(
        gather_kernel,
        [((halo_count * 4, 128), F32)],
        (wanted, cold_history),
        limit=60,
        flops=10**9,
    )
    halo, part = lax.optimization_barrier((exchange(found), part))
    outgoing, z_high, z_low, u = call(
        layer_kernel,
        [((owners // 4, 4, 16, 128), F32), (full, BF16), (full, BF16), (full, F32)],
        (halo, pick, edge_weight, part, weight),
        limit=60,
        flops=2 * 10**9,
    )
    arrived = exchange(outgoing.reshape(owners * 16, 128))
    half = (rows // 2, width)
    keep, give, du = call(
        weight_kernel,
        [(half, F32), (half, F32), (full, F32)],
        (core, u, z_high, z_low, cotangent),
        scalars=1,
        scratch=[pltpu.VMEM((width, width), F32)],
        limit=60,
        flops=10**9,
    )
    (grad_input,) = call(
        backward_kernel, [(full, F32)], (du, weight, high, low), limit=60, flops=2 * 10**9
    )
    at_x = lax.axis_index("hist").astype(jnp.int32).reshape(1)
    batch = lax.axis_index("batch").astype(jnp.int32).reshape(1)
    depth = lax.axis_size("batch") // 4
    at_y = batch // depth
    parts = scatter(at_x, "hist", 1, keep, swap(give))
    parts = scatter(at_y, "batch", depth, *parts)
    summed = total(*parts)
    summed = total(summed, *[move(summed, "batch", mask) for mask in (2, 4, 6)])
    arrived, summed, grad_input = lax.optimization_barrier((arrived, summed, grad_input))
    dest = jnp.transpose(dest_rows.reshape(2, owners, 4), (0, 2, 1)).reshape(2, rows)
    (new_history,) = call(
        history_kernel,
        [(cold_history.shape, F32)],
        (core, dest, arrived, swap(arrived), cold_history),
        scalars=1,
        scratch=[pltpu.VMEM((2 * rows, width), BF16), pltpu.VMEM((2 * rows, width), BF16)],
        limit=24,
        flops=4 * 10**9,
    )
    summed = total(summed, move(summed, "batch", 1))
    summed = gather(at_y, "batch", depth, summed)
    summed = gather(at_x, "hist", 1, summed)
    all_nodes = rows * lax.axis_size(("batch", "hist", "rep"))
    grad_weight = join(core, [summed, swap(summed)], BETA / math.sqrt(all_nodes))
    return (grad_weight, grad_input, new_history)


def solution(mesh):
    return jax.shard_map(
        body,
        mesh=mesh,
        in_specs=(
            P(("batch", "hist", "rep"), None),
            P(("batch", "hist", "rep"), None),
            P(("batch", "hist", "rep"), None),
            P(),
            P(("batch", "hist", "rep"), None),
            P(("batch", "hist", "rep"), None),
            P(("batch", "hist", "rep"), None, None),
            P(("batch", "hist"), None),
            P("rep", None),
            P(("batch", "hist"), None),
        ),
        out_specs=(P(), P(("batch", "hist", "rep"), None), P(("batch", "hist"), None)),
        check_vma=False,
    )
```

```python
import functools
import math

import jax
import jax.numpy as jnp
from jax import lax
from jax.experimental import pallas as pl
from jax.experimental.pallas import tpu as pltpu
from jax.sharding import PartitionSpec as P

ALPHA = 0.1
BETA = math.log(1.5)
OWN = ("batch", "hist")
F32 = jnp.float32
BF16 = jnp.bfloat16
GELU_C = math.sqrt(2.0 / math.pi)
GELU_A = 0.044715
VMEM = pl.BlockSpec(memory_space=pltpu.VMEM)
SMEM = pl.BlockSpec(memory_space=pltpu.SMEM)
HBM = pl.BlockSpec(memory_space=pltpu.HBM)
MIB = 1 << 20


def dot(a, b, left=1, right=0):
    return lax.dot_general(a, b, (((left,), (right,)), ((), ())), preferred_element_type=F32)


def split(v):
    high = v.astype(BF16)
    return high, (v - high.astype(F32)).astype(BF16)


def dot3(a, b, left=1, right=0):
    return dot(a[0], b[0], left, right) + (dot(a[0], b[1], left, right) + dot(a[1], b[0], left, right))


def lanes(rows, columns):
    return lax.broadcasted_iota(jnp.int32, (rows, columns), 1)


def one_hot(column, count):
    return (column == lanes(column.shape[0], count)).astype(BF16)


class Source:
    def __init__(self, ref, buffer, sem, rows=None):
        rows = rows or ref.shape[0]
        self.buffer, self.copies, self.shape = buffer, [], ref.shape
        for i in range(ref.shape[0] // rows):
            at = (pl.ds(i * rows, rows),) + (slice(None),) * (len(ref.shape) - 1)
            copy = pltpu.make_async_copy(ref.at[at], buffer.at[at], sem.at[i])
            copy.start()
            self.copies.append(copy)

    def __getitem__(self, index):
        for copy in self.copies:
            copy.wait()
        self.copies = []
        return self.buffer[index]

    def part(self, i):
        self.copies[i].wait()


class Sink:
    def __init__(self, ref, buffer, sem, rows=None):
        self.ref, self.buffer, self.sem = ref, buffer, sem
        self.rows, self.copies = rows or ref.shape[0], []
        self.shape = ref.shape

    def __setitem__(self, index, value):
        self.buffer[index] = value

    def push(self, i=0):
        at = (pl.ds(i * self.rows, self.rows),) + (slice(None),) * (len(self.shape) - 1)
        copy = pltpu.make_async_copy(self.buffer.at[at], self.ref.at[at], self.sem.at[i])
        copy.start()
        self.copies.append(copy)


def call(kernel, outs, args, spaces=None, scratch=(), limit=8, flops=0, rows=None):
    spaces = spaces or "v" * (len(args) + len(outs))
    shapes = [(a.shape, a.dtype) for a in args] + list(outs)
    where = {"s": SMEM, "v": VMEM, "h": HBM}
    remote = [i for i, space in enumerate(spaces) if space == "h"]
    buffers = [pltpu.VMEM(*shapes[i]) for i in remote]
    sems = [pltpu.SemaphoreType.DMA((shapes[i][0][0] // rows if rows else 1,)) for i in remote]

    def wrapped(*refs):
        refs, rest = list(refs[: len(shapes)]), refs[len(shapes) :]
        sinks = []
        for n, i in enumerate(remote):
            kind = Source if i < len(args) else Sink
            refs[i] = kind(refs[i], rest[n], rest[len(remote) + n], rows)
            if kind is Sink:
                sinks.append(refs[i])
        kernel(*refs, *rest[2 * len(remote) :])
        for sink in sinks:
            for copy in sink.copies:
                copy.wait()

    count = sum(math.prod(shape) * 4 for shape, _ in shapes)
    return pl.pallas_call(
        wrapped,
        out_shape=[jax.ShapeDtypeStruct(*o) for o in outs],
        in_specs=[where[c] for c in spaces[: len(args)]],
        out_specs=[where[c] for c in spaces[len(args) :]],
        scratch_shapes=buffers + sems + list(scratch),
        compiler_params=pltpu.CompilerParams(vmem_limit_bytes=limit * MIB),
        cost_estimate=pl.CostEstimate(flops=flops, bytes_accessed=count, transcendentals=0),
    )(*args)


def gather_kernel(idx_ref, cold_ref, out_ref):
    owners, per = idx_ref.shape
    step = cold_ref.shape[0] // len(cold_ref.copies)
    found = jnp.zeros((per * owners, cold_ref.shape[1]), F32)
    for block in range(len(cold_ref.copies)):
        cold_ref.part(block)
        high, low = split(cold_ref.buffer[block * step : (block + 1) * step, :])
        pick = jnp.concatenate(
            [one_hot(idx_ref[:, s : s + 1] - block * step, step) for s in range(per)], axis=0
        )
        found = found + (dot(pick, high) + dot(pick, low))
    for s in range(per):
        for l in range(4):
            out_ref[pl.ds(s * 4 + l, owners, stride=per * 4), :] = found[
                s * owners : (s + 1) * owners, l * 128 : (l + 1) * 128
            ]


def hot_kernel(core_ref, nbr_ref, ew_ref, mine_ref, other_ref, out_ref, *, start):
    core = core_ref[0]
    half = mine_ref.shape[0]
    hot = nbr_ref[...].T[:, 1:2] - start
    picked = jnp.zeros(out_ref.shape, F32)
    for ref, base in ((mine_ref, core * half), (other_ref, (1 - core) * half)):
        choose = one_hot(hot - base, half)
        for part in split(ref[...]):
            picked = picked + dot(choose, part)
    out_ref[...] = ew_ref[...].T[:, 1:2] * picked
    out_ref.push()


def local_kernel(
    nbr_ref, ew_ref, node_ref, init_ref, hot_ref, part_ref, high_ref, low_ref, pick_ref
):
    rows = node_ref.shape[0]
    halo_count = pick_ref.shape[1]
    nbr = nbr_ref[...].T
    ew = ew_ref[...].T
    ids = lanes(rows, rows)
    tile = jnp.zeros((rows, rows), F32)
    for k in range(2, nbr.shape[1]):
        tile = tile + jnp.where(nbr[:, k : k + 1] == ids, ew[:, k : k + 1], 0.0)
    tiles = split(tile)
    high_ref[...] = tiles[0]
    low_ref[...] = tiles[1]
    high_ref.push()
    low_ref.push()
    agg = dot3(tiles, split(node_ref[...])) + hot_ref[...]
    part_ref[...] = (1.0 - ALPHA) * agg + ALPHA * init_ref[...]
    part_ref.push()
    place = nbr[:, :1] - rows
    pick_ref[...] = one_hot((place & 1) * (halo_count // 2) + (place >> 1), halo_count)
    pick_ref.push()


def layer_kernel(
    core_ref, halo_ref, pick_ref, ew_ref, part_ref, weight_ref, cot_ref,
    out_ref, keep_ref, give_ref, du_ref, term_ref,
):
    owners = halo_ref.shape[0] // 8
    halo = jnp.concatenate(
        [
            jnp.concatenate(
                [halo_ref[pl.ds(s * 4 + l, owners, stride=8), :] for l in range(4)], axis=1
            )
            for s in range(2)
        ],
        axis=0,
    )
    pick = pick_ref[...]
    high, low = split(halo)
    ew = ew_ref[...].T[:, :1]
    z = part_ref[...] + ((1.0 - ALPHA) * ew) * (dot(pick, high) + dot(pick, low))
    zs = split(z)
    u = (1.0 - BETA) * z + BETA * dot3(zs, split(weight_ref[...]))
    square = u * u
    bent = jnp.tanh(GELU_C * (u + GELU_A * (square * u)))
    embed = (0.5 * u) * (1.0 + bent)
    slope = 0.5 * (1.0 + bent) + (0.5 * u) * (1.0 - bent * bent) * (
        GELU_C * (1.0 + (3.0 * GELU_A) * square)
    )
    du = cot_ref[...] * slope
    du_ref[...] = du
    du_ref.push()
    groups = out_ref.shape[0]
    top = lax.broadcasted_iota(jnp.int32, (groups, 2, 8, 128), 2) < 4
    for pair in range(2):
        x, y = (
            embed[:, l * 128 : (l + 1) * 128].reshape(groups, 2, 8, 128)
            for l in (2 * pair, 2 * pair + 1)
        )
        even = jnp.where(top, x, pltpu.roll(y, 4, 2))
        odd = jnp.where(top, pltpu.roll(x, 4, 2), y)
        for h in range(2):
            out_ref[:, 2 * h, 8 * pair : 8 * pair + 8, :] = even[:, h]
            out_ref[:, 2 * h + 1, 8 * pair : 8 * pair + 8, :] = odd[:, h]
    out_ref.push()
    term_ref[...] = dot3(zs, split(du), 0, 0)
    half = term_ref.shape[0] // 2
    core = core_ref[0]
    keep_ref[...] = term_ref[pl.ds(pl.multiple_of(core * half, half), half), :]
    give_ref[...] = term_ref[pl.ds(pl.multiple_of((1 - core) * half, half), half), :]


def scatter_kernel(me_ref, *refs):
    terms, outs, total_ref = refs[: -1 - 4], refs[-1 - 4 : -1], refs[-1]
    total_ref[...] = functools.reduce(lambda x, y: x + y, [t[...] for t in terms])
    size = outs[0].shape[0]
    for shift, out in enumerate(outs):
        at = jnp.bitwise_xor(me_ref[0], shift) * size
        out[...] = total_ref[pl.ds(pl.multiple_of(at, size), size), :]


def total_kernel(*refs):
    terms = [t[...] for t in refs[:-1]]
    while len(terms) > 1:
        terms = [x + y for x, y in zip(terms[::2], terms[1::2])]
    refs[-1][...] = terms[0]


def join_kernel(me_ref, *refs, scale=None):
    size = refs[0].shape[0]
    for shift, part in enumerate(refs[:-1]):
        at = jnp.bitwise_xor(me_ref[0], shift) * size
        value = part[...] if scale is None else part[...] * scale
        refs[-1][pl.ds(pl.multiple_of(at, size), size), :] = value


def backward_kernel(du_ref, weight_ref, high_ref, low_ref, out_ref):
    du = du_ref[...]
    dz = (1.0 - BETA) * du + BETA * dot3(split(du), split(weight_ref[...]), 1, 1)
    out_ref[...] = (1.0 - ALPHA) * dot3((high_ref[...], low_ref[...]), split(dz), 0, 0)
    out_ref.push()


def history_kernel(which_ref, dest_ref, recv_ref, base_ref, out_ref, high_ref, low_ref):
    owners = recv_ref.shape[0] // 16
    for s in range(4):
        for l in range(4):
            high, low = split(recv_ref[pl.ds(4 * l + s, owners, stride=16), :])
            at = slice(s * owners, (s + 1) * owners)
            high_ref[at, l * 128 : (l + 1) * 128] = high
            low_ref[at, l * 128 : (l + 1) * 128] = low
    dest = dest_ref[pl.ds(which_ref[0], 1), :]
    step = out_ref.rows
    for block in range(out_ref.shape[0] // step):
        ids = lax.broadcasted_iota(jnp.int32, (step, dest.shape[1]), 0) + block * step
        hit = jnp.where(ids == dest, 1.0, 0.0)
        count = jnp.sum(hit, axis=1, keepdims=True)
        place = hit.astype(BF16)
        written = dot(place, high_ref[...]) + dot(place, low_ref[...])
        at = slice(block * step, (block + 1) * step)
        base_ref.part(block)
        out_ref[at, :] = jnp.where(count > 0.5, written, base_ref.buffer[at, :])
        out_ref.push(block)


def write_rows(which, dest, recv, base):
    rows, width = dest.shape[1], base.shape[1]
    return call(
        history_kernel,
        [(base.shape, F32)],
        (which, dest, recv, base),
        spaces="svvhh",
        scratch=[pltpu.VMEM((rows, width), BF16), pltpu.VMEM((rows, width), BF16)],
        limit=52,
        flops=2 * 10**9,
        rows=256,
    )[0]


def exchange(v):
    return lax.all_to_all(v, OWN, split_axis=0, concat_axis=0, tiled=True)


def swap(v):
    return lax.ppermute(v, "rep", [(0, 1), (1, 0)])


def move(v, axis, mask):
    count = lax.axis_size(axis)
    return lax.ppermute(v, axis, [(i, i ^ mask) for i in range(count)])


def scatter(me, *terms):
    size = terms[0].shape[0] // 4
    return call(
        scatter_kernel,
        [((size, terms[0].shape[1]), F32)] * 4,
        (me,) + terms,
        spaces="s" + "v" * (len(terms) + 4),
        scratch=[pltpu.VMEM(terms[0].shape, F32)],
    )


def trade(pieces, axis, unit):
    return [pieces[0]] + [move(pieces[shift], axis, shift * unit) for shift in (1, 2, 3)]


def total(*terms):
    return call(total_kernel, [(terms[0].shape, F32)], terms)[0]


def join(me, parts, scale=None):
    rows, width = parts[0].shape
    return call(
        functools.partial(join_kernel, scale=scale),
        [((rows * len(parts), width), F32)],
        (me,) + tuple(parts),
        spaces="s" + "v" * (len(parts) + 1),
    )[0]


def together(*values):
    return lax.optimization_barrier(values)


def body(
    node_input,
    initial,
    cotangent,
    weight,
    edge_weight,
    neighbors,
    halo_rows,
    cold_history,
    hot_history,
    dest_rows,
):
    rows, width = node_input.shape
    owners = lax.axis_size(OWN)
    halo_count = owners * halo_rows.shape[2]
    core = lax.axis_index("rep").astype(jnp.int32).reshape(1)
    at_x = lax.axis_index("hist").astype(jnp.int32).reshape(1)
    depth = lax.axis_size("batch") // 4
    at_y = lax.div(lax.axis_index("batch").astype(jnp.int32), jnp.int32(depth)).reshape(1)
    full = (rows, width)
    half = (rows // 2, width)
    nbr = neighbors.T
    ew = edge_weight.T
    dest = jnp.transpose(dest_rows.reshape(2, owners, 4), (0, 2, 1)).reshape(2, rows)

    wanted = exchange(halo_rows[0])
    (hot,) = call(
        functools.partial(hot_kernel, start=rows + halo_count),
        [(full, F32)],
        (core, nbr, ew, hot_history, swap(hot_history)),
        spaces="svvhhh",
        limit=60,
        flops=4 * 10**9,
    )
    wanted, hot, dest = together(wanted, hot, dest)
    (found,) = call(
        gather_kernel,
        [((halo_count * 4, 128), F32)],
        (wanted, cold_history),
        spaces="vhv",
        rows=256,
        limit=60,
        flops=10**9,
    )
    halo = exchange(found)
    part, high, low, pick = call(
        local_kernel,
        [(full, F32), ((rows, rows), BF16), ((rows, rows), BF16), ((rows, halo_count), BF16)],
        (nbr, ew, node_input, initial, hot),
        spaces="vvhhhhhhh",
        limit=60,
        flops=2 * 10**9,
    )
    halo, part = together(halo, part)
    outgoing, keep, give, du = call(
        layer_kernel,
        [((owners // 4, 4, 16, 128), F32), (half, F32), (half, F32), (full, F32)],
        (core, halo, pick, ew, part, weight, cotangent),
        spaces="svhvhhhhvvh",
        scratch=[pltpu.VMEM((width, width), F32)],
        limit=52,
        flops=3 * 10**9,
    )
    pieces = scatter(at_x, keep, swap(give))
    outgoing, *pieces = together(outgoing, *pieces)
    arrived = exchange(outgoing.reshape(owners * 16, 128))
    pieces = scatter(at_y, *trade(pieces, "hist", 1))
    summed = total(*trade(pieces, "batch", depth))
    (grad_input,) = call(
        backward_kernel,
        [(full, F32)],
        (du, weight, high, low),
        spaces="hhhhh",
        limit=60,
        flops=2 * 10**9,
    )
    summed = together(summed, *[move(summed, "batch", mask) for mask in (2, 4, 6)], grad_input)
    grad_input = summed[-1]
    summed = total(*summed[:-1])
    summed = total(summed, move(summed, "batch", 1))
    arrived, summed = together(arrived, summed)
    arrived_other = swap(arrived)
    parts = trade([summed] * 4, "batch", depth)
    history = write_rows(core, dest, arrived, cold_history)
    *parts, history = together(*parts, history)
    summed = join(at_y, parts)
    parts = trade([summed] * 4, "hist", 1)
    history = write_rows(1 - core, dest, arrived_other, history)
    *parts, history = together(*parts, history)
    summed = join(at_x, parts)
    all_nodes = rows * lax.axis_size(("batch", "hist", "rep"))
    grad_weight = join(core, [summed, swap(summed)], BETA / math.sqrt(all_nodes))
    return (grad_weight, grad_input, history)


def solution(mesh):
    return jax.shard_map(
        body,
        mesh=mesh,
        in_specs=(
            P(("batch", "hist", "rep"), None),
            P(("batch", "hist", "rep"), None),
            P(("batch", "hist", "rep"), None),
            P(),
            P(("batch", "hist", "rep"), None),
            P(("batch", "hist", "rep"), None),
            P(("batch", "hist", "rep"), None, None),
            P(("batch", "hist"), None),
            P("rep", None),
            P(("batch", "hist"), None),
        ),
        out_specs=(P(), P(("batch", "hist", "rep"), None), P(("batch", "hist"), None)),
        check_vma=False,
    )
```

```python
import functools
import math

import jax
import jax.numpy as jnp
from jax import lax
from jax.experimental import pallas as pl
from jax.experimental.pallas import tpu as pltpu
from jax.sharding import PartitionSpec as P

ALPHA = 0.1
BETA = math.log(1.5)
OWN = ("batch", "hist")
F32 = jnp.float32
BF16 = jnp.bfloat16
GELU_C = math.sqrt(2.0 / math.pi)
GELU_A = 0.044715
VMEM = pl.BlockSpec(memory_space=pltpu.VMEM)
SMEM = pl.BlockSpec(memory_space=pltpu.SMEM)
HBM = pl.BlockSpec(memory_space=pltpu.HBM)
MIB = 1 << 20


def dot(a, b, left=1, right=0):
    return lax.dot_general(a, b, (((left,), (right,)), ((), ())), preferred_element_type=F32)


def split(v):
    high = v.astype(BF16)
    return high, (v - high.astype(F32)).astype(BF16)


def dot3(a, b, left=1, right=0):
    return dot(a[0], b[0], left, right) + (dot(a[0], b[1], left, right) + dot(a[1], b[0], left, right))


def lanes(rows, columns):
    return lax.broadcasted_iota(jnp.int32, (rows, columns), 1)


def one_hot(column, count):
    return (column == lanes(column.shape[0], count)).astype(BF16)


class Source:
    def __init__(self, ref, buffer, sem, rows=None):
        rows = rows or ref.shape[0]
        self.buffer, self.copies, self.shape = buffer, [], ref.shape
        for i in range(ref.shape[0] // rows):
            at = (pl.ds(i * rows, rows),) + (slice(None),) * (len(ref.shape) - 1)
            copy = pltpu.make_async_copy(ref.at[at], buffer.at[at], sem.at[i])
            copy.start()
            self.copies.append(copy)

    def __getitem__(self, index):
        for copy in self.copies:
            copy.wait()
        self.copies = []
        return self.buffer[index]

    def part(self, i):
        self.copies[i].wait()


class Sink:
    def __init__(self, ref, buffer, sem, rows=None):
        self.ref, self.buffer, self.sem = ref, buffer, sem
        self.rows, self.copies = rows or ref.shape[0], []
        self.shape = ref.shape

    def __setitem__(self, index, value):
        self.buffer[index] = value

    def push(self, i=0):
        at = (pl.ds(i * self.rows, self.rows),) + (slice(None),) * (len(self.shape) - 1)
        copy = pltpu.make_async_copy(self.buffer.at[at], self.ref.at[at], self.sem.at[i])
        copy.start()
        self.copies.append(copy)


def call(kernel, outs, args, spaces=None, scratch=(), limit=8, flops=0, rows=None):
    spaces = spaces or "v" * (len(args) + len(outs))
    shapes = [(a.shape, a.dtype) for a in args] + list(outs)
    where = {"s": SMEM, "v": VMEM, "h": HBM}
    remote = [i for i, space in enumerate(spaces) if space == "h"]
    buffers = [pltpu.VMEM(*shapes[i]) for i in remote]
    sems = [pltpu.SemaphoreType.DMA((shapes[i][0][0] // rows if rows else 1,)) for i in remote]

    def wrapped(*refs):
        refs, rest = list(refs[: len(shapes)]), refs[len(shapes) :]
        sinks = []
        for n, i in enumerate(remote):
            kind = Source if i < len(args) else Sink
            refs[i] = kind(refs[i], rest[n], rest[len(remote) + n], rows)
            if kind is Sink:
                sinks.append(refs[i])
        kernel(*refs, *rest[2 * len(remote) :])
        for sink in sinks:
            for copy in sink.copies:
                copy.wait()

    count = sum(math.prod(shape) * 4 for shape, _ in shapes)
    return pl.pallas_call(
        wrapped,
        out_shape=[jax.ShapeDtypeStruct(*o) for o in outs],
        in_specs=[where[c] for c in spaces[: len(args)]],
        out_specs=[where[c] for c in spaces[len(args) :]],
        scratch_shapes=buffers + sems + list(scratch),
        compiler_params=pltpu.CompilerParams(vmem_limit_bytes=limit * MIB),
        cost_estimate=pl.CostEstimate(flops=flops, bytes_accessed=count, transcendentals=0),
    )(*args)


def gather_kernel(idx_ref, cold_ref, out_ref):
    owners, per = idx_ref.shape
    step = cold_ref.shape[0] // len(cold_ref.copies)
    found = jnp.zeros((per * owners, cold_ref.shape[1]), F32)
    for block in range(len(cold_ref.copies)):
        cold_ref.part(block)
        high, low = split(cold_ref.buffer[block * step : (block + 1) * step, :])
        pick = jnp.concatenate(
            [one_hot(idx_ref[:, s : s + 1] - block * step, step) for s in range(per)], axis=0
        )
        found = found + (dot(pick, high) + dot(pick, low))
    for s in range(per):
        for l in range(4):
            out_ref[pl.ds(s * 4 + l, owners, stride=per * 4), :] = found[
                s * owners : (s + 1) * owners, l * 128 : (l + 1) * 128
            ]


def prepare_kernel(
    core_ref, nbr_ref, ew_ref, mine_ref, other_ref, node_ref, init_ref,
    part_ref, high_ref, low_ref, pick_ref,
):
    rows = node_ref.shape[0]
    halo_count = pick_ref.shape[1]
    half = mine_ref.shape[0]
    core = core_ref[0]
    nbr = nbr_ref[...].T
    ew = ew_ref[...].T
    place = nbr[:, :1] - rows
    pick_ref[...] = one_hot((place & 1) * (halo_count // 2) + (place >> 1), halo_count)
    pick_ref.push()
    ids = lanes(rows, rows)
    tile = jnp.zeros((rows, rows), F32)
    for k in range(2, nbr.shape[1]):
        tile = tile + jnp.where(nbr[:, k : k + 1] == ids, ew[:, k : k + 1], 0.0)
    tiles = split(tile)
    high_ref[...] = tiles[0]
    low_ref[...] = tiles[1]
    high_ref.push()
    low_ref.push()
    hot = nbr[:, 1:2] - (rows + halo_count)
    picked = jnp.zeros((rows, node_ref.shape[1]), F32)
    for ref, base in ((mine_ref, core * half), (other_ref, (1 - core) * half)):
        choose = one_hot(hot - base, half)
        for piece in split(ref[...]):
            picked = picked + dot(choose, piece)
    agg = dot3(tiles, split(node_ref[...])) + ew[:, 1:2] * picked
    part_ref[...] = (1.0 - ALPHA) * agg + ALPHA * init_ref[...]
    part_ref.push()


def layer_kernel(
    core_ref, halo_ref, pick_ref, ew_ref, part_ref, weight_ref, cot_ref,
    out_ref, keep_ref, give_ref, du_ref, term_ref,
):
    owners = halo_ref.shape[0] // 8
    halo = jnp.concatenate(
        [
            jnp.concatenate(
                [halo_ref[pl.ds(s * 4 + l, owners, stride=8), :] for l in range(4)], axis=1
            )
            for s in range(2)
        ],
        axis=0,
    )
    pick = pick_ref[...]
    high, low = split(halo)
    ew = ew_ref[...].T[:, :1]
    z = part_ref[...] + ((1.0 - ALPHA) * ew) * (dot(pick, high) + dot(pick, low))
    zs = split(z)
    u = (1.0 - BETA) * z + BETA * dot3(zs, split(weight_ref[...]))
    square = u * u
    bent = jnp.tanh(GELU_C * (u + GELU_A * (square * u)))
    embed = (0.5 * u) * (1.0 + bent)
    slope = 0.5 * (1.0 + bent) + (0.5 * u) * (1.0 - bent * bent) * (
        GELU_C * (1.0 + (3.0 * GELU_A) * square)
    )
    du = cot_ref[...] * slope
    du_ref[...] = du
    du_ref.push()
    groups = out_ref.shape[0]
    top = lax.broadcasted_iota(jnp.int32, (groups, 2, 8, 128), 2) < 4
    for pair in range(2):
        x, y = (
            embed[:, l * 128 : (l + 1) * 128].reshape(groups, 2, 8, 128)
            for l in (2 * pair, 2 * pair + 1)
        )
        even = jnp.where(top, x, pltpu.roll(y, 4, 2))
        odd = jnp.where(top, pltpu.roll(x, 4, 2), y)
        for h in range(2):
            out_ref[:, 2 * h, 8 * pair : 8 * pair + 8, :] = even[:, h]
            out_ref[:, 2 * h + 1, 8 * pair : 8 * pair + 8, :] = odd[:, h]
    out_ref.push()
    term_ref[...] = dot3(zs, split(du), 0, 0)
    half = term_ref.shape[0] // 2
    core = core_ref[0]
    keep_ref[...] = term_ref[pl.ds(pl.multiple_of(core * half, half), half), :]
    give_ref[...] = term_ref[pl.ds(pl.multiple_of((1 - core) * half, half), half), :]


def scatter_kernel(me_ref, *refs):
    terms, outs, total_ref = refs[: -1 - 4], refs[-1 - 4 : -1], refs[-1]
    total_ref[...] = functools.reduce(lambda x, y: x + y, [t[...] for t in terms])
    size = outs[0].shape[0]
    for shift, out in enumerate(outs):
        at = jnp.bitwise_xor(me_ref[0], shift) * size
        out[...] = total_ref[pl.ds(pl.multiple_of(at, size), size), :]


def total_kernel(*refs):
    terms = [t[...] for t in refs[:-1]]
    while len(terms) > 1:
        terms = [x + y for x, y in zip(terms[::2], terms[1::2])]
    refs[-1][...] = terms[0]


def join_kernel(me_ref, *refs, scale=None):
    size = refs[0].shape[0]
    for shift, part in enumerate(refs[:-1]):
        at = jnp.bitwise_xor(me_ref[0], shift) * size
        value = part[...] if scale is None else part[...] * scale
        refs[-1][pl.ds(pl.multiple_of(at, size), size), :] = value


def backward_kernel(du_ref, weight_ref, high_ref, low_ref, out_ref):
    du = du_ref[...]
    dz = (1.0 - BETA) * du + BETA * dot3(split(du), split(weight_ref[...]), 1, 1)
    out_ref[...] = (1.0 - ALPHA) * dot3((high_ref[...], low_ref[...]), split(dz), 0, 0)
    out_ref.push()


def history_kernel(
    core_ref, dest_ref, mine_ref, other_ref, base_ref, out_ref, high_ref, low_ref
):
    owners = mine_ref.shape[0] // 16
    rows = 4 * owners
    for r, ref in enumerate((mine_ref, other_ref)):
        for s in range(4):
            for l in range(4):
                high, low = split(ref[pl.ds(4 * l + s, owners, stride=16), :])
                at = slice(r * rows + s * owners, r * rows + (s + 1) * owners)
                high_ref[at, l * 128 : (l + 1) * 128] = high
                low_ref[at, l * 128 : (l + 1) * 128] = low
    core = core_ref[0]
    dest = jnp.concatenate(
        [dest_ref[pl.ds(core, 1), :], dest_ref[pl.ds(1 - core, 1), :]], axis=1
    )
    step = out_ref.rows
    for block in range(out_ref.shape[0] // step):
        ids = lax.broadcasted_iota(jnp.int32, (step, 2 * rows), 0) + block * step
        hit = jnp.where(ids == dest, 1.0, 0.0)
        count = jnp.sum(hit, axis=1, keepdims=True)
        place = hit.astype(BF16)
        written = dot(place, high_ref[...]) + dot(place, low_ref[...])
        at = slice(block * step, (block + 1) * step)
        base_ref.part(block)
        out_ref[at, :] = jnp.where(count > 0.5, written, base_ref.buffer[at, :])
        out_ref.push(block)


def write_rows(core, dest, mine, other, base):
    rows, width = 2 * dest.shape[1], base.shape[1]
    return call(
        history_kernel,
        [(base.shape, F32)],
        (core, dest, mine, other, base),
        spaces="svvvhh",
        scratch=[pltpu.VMEM((rows, width), BF16), pltpu.VMEM((rows, width), BF16)],
        limit=52,
        flops=4 * 10**9,
        rows=256,
    )[0]


def exchange(v):
    return lax.all_to_all(v, OWN, split_axis=0, concat_axis=0, tiled=True)


def swap(v):
    return lax.ppermute(v, "rep", [(0, 1), (1, 0)])


def move(v, axis, mask):
    count = lax.axis_size(axis)
    return lax.ppermute(v, axis, [(i, i ^ mask) for i in range(count)])


def scatter(me, *terms):
    size = terms[0].shape[0] // 4
    return call(
        scatter_kernel,
        [((size, terms[0].shape[1]), F32)] * 4,
        (me,) + terms,
        spaces="s" + "v" * (len(terms) + 4),
        scratch=[pltpu.VMEM(terms[0].shape, F32)],
    )


def trade(pieces, axis, unit):
    return [pieces[0]] + [move(pieces[shift], axis, shift * unit) for shift in (1, 2, 3)]


def total(*terms):
    return call(total_kernel, [(terms[0].shape, F32)], terms)[0]


def join(me, parts, scale=None):
    rows, width = parts[0].shape
    return call(
        functools.partial(join_kernel, scale=scale),
        [((rows * len(parts), width), F32)],
        (me,) + tuple(parts),
        spaces="s" + "v" * (len(parts) + 1),
    )[0]


def together(*values):
    return lax.optimization_barrier(values)


def body(
    node_input,
    initial,
    cotangent,
    weight,
    edge_weight,
    neighbors,
    halo_rows,
    cold_history,
    hot_history,
    dest_rows,
):
    rows, width = node_input.shape
    owners = lax.axis_size(OWN)
    halo_count = owners * halo_rows.shape[2]
    core = lax.axis_index("rep").astype(jnp.int32).reshape(1)
    at_x = lax.axis_index("hist").astype(jnp.int32).reshape(1)
    depth = lax.axis_size("batch") // 4
    at_y = lax.div(lax.axis_index("batch").astype(jnp.int32), jnp.int32(depth)).reshape(1)
    full = (rows, width)
    half = (rows // 2, width)
    nbr = neighbors.T
    ew = edge_weight.T
    dest = jnp.transpose(dest_rows.reshape(2, owners, 4), (0, 2, 1)).reshape(2, rows)

    wanted = exchange(halo_rows[0])
    (found,) = call(
        gather_kernel,
        [((halo_count * 4, 128), F32)],
        (wanted, cold_history),
        spaces="vhv",
        rows=256,
        limit=60,
        flops=10**9,
    )
    halo = exchange(found)
    part, high, low, pick = call(
        prepare_kernel,
        [(full, F32), ((rows, rows), BF16), ((rows, rows), BF16), ((rows, halo_count), BF16)],
        (core, nbr, ew, hot_history, swap(hot_history), node_input, initial),
        spaces="svvhhhhhhhh",
        limit=60,
        flops=6 * 10**9,
    )
    halo, part = together(halo, part)
    outgoing, keep, give, du = call(
        layer_kernel,
        [((owners // 4, 4, 16, 128), F32), (half, F32), (half, F32), (full, F32)],
        (core, halo, pick, ew, part, weight, cotangent),
        spaces="svhvhhhhvvh",
        scratch=[pltpu.VMEM((width, width), F32)],
        limit=52,
        flops=3 * 10**9,
    )
    got, dest = together(swap(give), dest)
    pieces = trade(scatter(at_x, keep, got), "hist", 1)
    (grad_input,) = call(
        backward_kernel,
        [(full, F32)],
        (du, weight, high, low),
        spaces="hhhhh",
        limit=60,
        flops=2 * 10**9,
    )
    *pieces, grad_input = together(*pieces, grad_input)
    pieces = trade(scatter(at_y, *pieces), "batch", depth)
    outgoing, grad_input = together(outgoing, grad_input)
    arrived = exchange(outgoing.reshape(owners * 16, 128))
    summed = total(*pieces)
    summed = total(summed, *[move(summed, "batch", mask) for mask in (2, 4, 6)])
    summed = total(summed, move(summed, "batch", 1))
    summed = join(at_y, trade([summed] * 4, "batch", depth))
    arrived, summed = together(arrived, summed)
    parts = trade([summed] * 4, "hist", 1)
    history = write_rows(core, dest, arrived, swap(arrived), cold_history)
    *parts, history = together(*parts, history)
    summed = join(at_x, parts)
    all_nodes = rows * lax.axis_size(("batch", "hist", "rep"))
    grad_weight = join(core, [summed, swap(summed)], BETA / math.sqrt(all_nodes))
    return (grad_weight, grad_input, history)


def solution(mesh):
    return jax.shard_map(
        body,
        mesh=mesh,
        in_specs=(
            P(("batch", "hist", "rep"), None),
            P(("batch", "hist", "rep"), None),
            P(("batch", "hist", "rep"), None),
            P(),
            P(("batch", "hist", "rep"), None),
            P(("batch", "hist", "rep"), None),
            P(("batch", "hist", "rep"), None, None),
            P(("batch", "hist"), None),
            P("rep", None),
            P(("batch", "hist"), None),
        ),
        out_specs=(P(), P(("batch", "hist", "rep"), None), P(("batch", "hist"), None)),
        check_vma=False,
    )
```

```python
import functools
import math

import jax
import jax.numpy as jnp
from jax import lax
from jax.experimental import pallas as pl
from jax.experimental.pallas import tpu as pltpu
from jax.sharding import PartitionSpec as P

ALPHA = 0.1
BETA = math.log(1.5)
OWN = ("batch", "hist")
F32 = jnp.float32
BF16 = jnp.bfloat16
GELU_C = math.sqrt(2.0 / math.pi)
GELU_A = 0.044715
VMEM = pl.BlockSpec(memory_space=pltpu.VMEM)
SMEM = pl.BlockSpec(memory_space=pltpu.SMEM)
HBM = pl.BlockSpec(memory_space=pltpu.HBM)
MIB = 1 << 20


def dot(a, b, left=1, right=0):
    return lax.dot_general(a, b, (((left,), (right,)), ((), ())), preferred_element_type=F32)


def split(v):
    high = v.astype(BF16)
    return high, (v - high.astype(F32)).astype(BF16)


def dot3(a, b, left=1, right=0):
    return dot(a[0], b[0], left, right) + (dot(a[0], b[1], left, right) + dot(a[1], b[0], left, right))


def lanes(rows, columns):
    return lax.broadcasted_iota(jnp.int32, (rows, columns), 1)


def one_hot(column, count):
    return (column == lanes(column.shape[0], count)).astype(BF16)


class Source:
    def __init__(self, ref, buffer, sem, rows=None):
        rows = rows or ref.shape[0]
        self.buffer, self.copies, self.shape = buffer, [], ref.shape
        for i in range(ref.shape[0] // rows):
            at = (pl.ds(i * rows, rows),) + (slice(None),) * (len(ref.shape) - 1)
            copy = pltpu.make_async_copy(ref.at[at], buffer.at[at], sem.at[i])
            copy.start()
            self.copies.append(copy)

    def __getitem__(self, index):
        for copy in self.copies:
            copy.wait()
        self.copies = []
        return self.buffer[index]

    def part(self, i):
        self.copies[i].wait()


class Sink:
    def __init__(self, ref, buffer, sem, rows=None):
        self.ref, self.buffer, self.sem = ref, buffer, sem
        self.rows, self.copies = rows or ref.shape[0], []
        self.shape = ref.shape

    def __setitem__(self, index, value):
        self.buffer[index] = value

    def push(self, i=0):
        at = (pl.ds(i * self.rows, self.rows),) + (slice(None),) * (len(self.shape) - 1)
        copy = pltpu.make_async_copy(self.buffer.at[at], self.ref.at[at], self.sem.at[i])
        copy.start()
        self.copies.append(copy)


def call(kernel, outs, args, spaces=None, scratch=(), limit=8, flops=0, rows=None):
    spaces = spaces or "v" * (len(args) + len(outs))
    shapes = [(a.shape, a.dtype) for a in args] + list(outs)
    where = {"s": SMEM, "v": VMEM, "h": HBM}
    remote = [i for i, space in enumerate(spaces) if space == "h"]
    buffers = [pltpu.VMEM(*shapes[i]) for i in remote]
    sems = [pltpu.SemaphoreType.DMA((shapes[i][0][0] // rows if rows else 1,)) for i in remote]

    def wrapped(*refs):
        refs, rest = list(refs[: len(shapes)]), refs[len(shapes) :]
        sinks = []
        for n, i in enumerate(remote):
            kind = Source if i < len(args) else Sink
            refs[i] = kind(refs[i], rest[n], rest[len(remote) + n], rows)
            if kind is Sink:
                sinks.append(refs[i])
        kernel(*refs, *rest[2 * len(remote) :])
        for sink in sinks:
            for copy in sink.copies:
                copy.wait()

    count = sum(math.prod(shape) * 4 for shape, _ in shapes)
    return pl.pallas_call(
        wrapped,
        out_shape=[jax.ShapeDtypeStruct(*o) for o in outs],
        in_specs=[where[c] for c in spaces[: len(args)]],
        out_specs=[where[c] for c in spaces[len(args) :]],
        scratch_shapes=buffers + sems + list(scratch),
        compiler_params=pltpu.CompilerParams(vmem_limit_bytes=limit * MIB),
        cost_estimate=pl.CostEstimate(flops=flops, bytes_accessed=count, transcendentals=0),
    )(*args)


def gather_kernel(idx_ref, cold_ref, out_ref):
    owners, per = idx_ref.shape
    step = cold_ref.shape[0] // len(cold_ref.copies)
    found = jnp.zeros((per * owners, cold_ref.shape[1]), F32)
    idx = jnp.concatenate([idx_ref[:, s : s + 1] for s in range(per)], axis=0)
    picks = [one_hot(idx - block * step, step) for block in range(len(cold_ref.copies))]
    for block, pick in enumerate(picks):
        cold_ref.part(block)
        high, low = split(cold_ref.buffer[block * step : (block + 1) * step, :])
        found = found + (dot(pick, high) + dot(pick, low))
    for s in range(per):
        for l in range(4):
            out_ref[pl.ds(s * 4 + l, owners, stride=per * 4), :] = found[
                s * owners : (s + 1) * owners, l * 128 : (l + 1) * 128
            ]


def prepare_kernel(
    core_ref, nbr_ref, ew_ref, mine_ref, other_ref, node_ref, init_ref,
    part_ref, high_ref, low_ref, *, halo_count,
):
    rows = node_ref.shape[0]
    half = mine_ref.shape[0]
    core = core_ref[0]
    nbr = nbr_ref[...].T
    ew = ew_ref[...].T
    ids = lanes(rows, rows)
    tile = jnp.zeros((rows, rows), F32)
    for k in range(2, nbr.shape[1]):
        tile = tile + jnp.where(nbr[:, k : k + 1] == ids, ew[:, k : k + 1], 0.0)
    tiles = split(tile)
    high_ref[...] = tiles[0]
    low_ref[...] = tiles[1]
    high_ref.push()
    low_ref.push()
    hot = nbr[:, 1:2] - (rows + halo_count)
    picked = jnp.zeros((rows, node_ref.shape[1]), F32)
    for ref, base in ((mine_ref, core * half), (other_ref, (1 - core) * half)):
        choose = one_hot(hot - base, half)
        for piece in split(ref[...]):
            picked = picked + dot(choose, piece)
    agg = dot3(tiles, split(node_ref[...])) + ew[:, 1:2] * picked
    part_ref[...] = (1.0 - ALPHA) * agg + ALPHA * init_ref[...]
    part_ref.push()


def layer_kernel(
    core_ref, halo_ref, nbr_ref, ew_ref, part_ref, weight_ref, cot_ref,
    out_ref, keep_ref, give_ref, du_ref, term_ref,
):
    owners = halo_ref.shape[0] // 8
    halo = jnp.concatenate(
        [
            jnp.concatenate(
                [halo_ref[pl.ds(s * 4 + l, owners, stride=8), :] for l in range(4)], axis=1
            )
            for s in range(2)
        ],
        axis=0,
    )
    place = nbr_ref[...].T[:, :1] - part_ref.shape[0]
    pick = one_hot((place & 1) * owners + (place >> 1), 2 * owners)
    high, low = split(halo)
    ew = ew_ref[...].T[:, :1]
    z = part_ref[...] + ((1.0 - ALPHA) * ew) * (dot(pick, high) + dot(pick, low))
    zs = split(z)
    u = (1.0 - BETA) * z + BETA * dot3(zs, split(weight_ref[...]))
    square = u * u
    bent = jnp.tanh(GELU_C * (u + GELU_A * (square * u)))
    embed = (0.5 * u) * (1.0 + bent)
    slope = 0.5 * (1.0 + bent) + (0.5 * u) * (1.0 - bent * bent) * (
        GELU_C * (1.0 + (3.0 * GELU_A) * square)
    )
    du = cot_ref[...] * slope
    du_ref[...] = du
    du_ref.push()
    groups = out_ref.shape[0]
    top = lax.broadcasted_iota(jnp.int32, (groups, 2, 8, 128), 2) < 4
    for pair in range(2):
        x, y = (
            embed[:, l * 128 : (l + 1) * 128].reshape(groups, 2, 8, 128)
            for l in (2 * pair, 2 * pair + 1)
        )
        even = jnp.where(top, x, pltpu.roll(y, 4, 2))
        odd = jnp.where(top, pltpu.roll(x, 4, 2), y)
        for h in range(2):
            out_ref[:, 2 * h, 8 * pair : 8 * pair + 8, :] = even[:, h]
            out_ref[:, 2 * h + 1, 8 * pair : 8 * pair + 8, :] = odd[:, h]
    out_ref.push()
    term_ref[...] = dot3(zs, split(du), 0, 0)
    half = term_ref.shape[0] // 2
    core = core_ref[0]
    keep_ref[...] = term_ref[pl.ds(pl.multiple_of(core * half, half), half), :]
    give_ref[...] = term_ref[pl.ds(pl.multiple_of((1 - core) * half, half), half), :]


def scatter_kernel(me_ref, *refs):
    terms, outs, total_ref = refs[: -1 - 4], refs[-1 - 4 : -1], refs[-1]
    total_ref[...] = functools.reduce(lambda x, y: x + y, [t[...] for t in terms])
    size = outs[0].shape[0]
    for shift, out in enumerate(outs):
        at = jnp.bitwise_xor(me_ref[0], shift) * size
        out[...] = total_ref[pl.ds(pl.multiple_of(at, size), size), :]


def total_kernel(*refs):
    terms = [t[...] for t in refs[:-1]]
    while len(terms) > 1:
        terms = [x + y for x, y in zip(terms[::2], terms[1::2])]
    refs[-1][...] = terms[0]


def join_kernel(me_ref, *refs, scale=None):
    size = refs[0].shape[0]
    for shift, part in enumerate(refs[:-1]):
        at = jnp.bitwise_xor(me_ref[0], shift) * size
        value = part[...] if scale is None else part[...] * scale
        refs[-1][pl.ds(pl.multiple_of(at, size), size), :] = value


def backward_kernel(du_ref, weight_ref, high_ref, low_ref, out_ref):
    du = du_ref[...]
    dz = (1.0 - BETA) * du + BETA * dot3(split(du), split(weight_ref[...]), 1, 1)
    out_ref[...] = (1.0 - ALPHA) * dot3((high_ref[...], low_ref[...]), split(dz), 0, 0)
    out_ref.push()


def history_kernel(which_ref, dest_ref, recv_ref, base_ref, out_ref, high_ref, low_ref):
    owners = recv_ref.shape[0] // 16
    for s in range(4):
        for l in range(4):
            high, low = split(recv_ref[pl.ds(4 * l + s, owners, stride=16), :])
            at = slice(s * owners, (s + 1) * owners)
            high_ref[at, l * 128 : (l + 1) * 128] = high
            low_ref[at, l * 128 : (l + 1) * 128] = low
    dest = dest_ref[pl.ds(which_ref[0], 1), :]
    step = out_ref.rows
    for block in range(out_ref.shape[0] // step):
        ids = lax.broadcasted_iota(jnp.int32, (step, dest.shape[1]), 0) + block * step
        hit = jnp.where(ids == dest, 1.0, 0.0)
        count = jnp.sum(hit, axis=1, keepdims=True)
        place = hit.astype(BF16)
        written = dot(place, high_ref[...]) + dot(place, low_ref[...])
        at = slice(block * step, (block + 1) * step)
        base_ref.part(block)
        out_ref[at, :] = jnp.where(count > 0.5, written, base_ref.buffer[at, :])
        out_ref.push(block)


def write_rows(which, dest, recv, base):
    rows, width = dest.shape[1], base.shape[1]
    return call(
        history_kernel,
        [(base.shape, F32)],
        (which, dest, recv, base),
        spaces="svvhh",
        scratch=[pltpu.VMEM((rows, width), BF16), pltpu.VMEM((rows, width), BF16)],
        limit=52,
        flops=2 * 10**9,
        rows=256,
    )[0]


def exchange(v):
    return lax.all_to_all(v, OWN, split_axis=0, concat_axis=0, tiled=True)


def swap(v):
    return lax.ppermute(v, "rep", [(0, 1), (1, 0)])


def move(v, axis, mask):
    count = lax.axis_size(axis)
    return lax.ppermute(v, axis, [(i, i ^ mask) for i in range(count)])


def scatter(me, *terms):
    size = terms[0].shape[0] // 4
    return call(
        scatter_kernel,
        [((size, terms[0].shape[1]), F32)] * 4,
        (me,) + terms,
        spaces="s" + "v" * (len(terms) + 4),
        scratch=[pltpu.VMEM(terms[0].shape, F32)],
    )


def trade(pieces, axis, unit):
    return [pieces[0]] + [move(pieces[shift], axis, shift * unit) for shift in (1, 2, 3)]


def total(*terms):
    return call(total_kernel, [(terms[0].shape, F32)], terms)[0]


def join(me, parts, scale=None):
    rows, width = parts[0].shape
    return call(
        functools.partial(join_kernel, scale=scale),
        [((rows * len(parts), width), F32)],
        (me,) + tuple(parts),
        spaces="s" + "v" * (len(parts) + 1),
    )[0]


def together(*values):
    return lax.optimization_barrier(values)


def body(
    node_input,
    initial,
    cotangent,
    weight,
    edge_weight,
    neighbors,
    halo_rows,
    cold_history,
    hot_history,
    dest_rows,
):
    rows, width = node_input.shape
    owners = lax.axis_size(OWN)
    halo_count = owners * halo_rows.shape[2]
    core = lax.axis_index("rep").astype(jnp.int32).reshape(1)
    at_x = lax.axis_index("hist").astype(jnp.int32).reshape(1)
    depth = lax.axis_size("batch") // 4
    at_y = lax.div(lax.axis_index("batch").astype(jnp.int32), jnp.int32(depth)).reshape(1)
    full = (rows, width)
    half = (rows // 2, width)
    nbr = neighbors.T
    ew = edge_weight.T
    dest = jnp.transpose(dest_rows.reshape(2, owners, 4), (0, 2, 1)).reshape(2, rows)

    wanted = exchange(halo_rows[0])
    (found,) = call(
        gather_kernel,
        [((halo_count * 4, 128), F32)],
        (wanted, cold_history),
        spaces="vhv",
        rows=256,
        limit=60,
        flops=10**9,
    )
    halo = exchange(found)
    part, high, low = call(
        functools.partial(prepare_kernel, halo_count=halo_count),
        [(full, F32), ((rows, rows), BF16), ((rows, rows), BF16)],
        (core, nbr, ew, hot_history, swap(hot_history), node_input, initial),
        spaces="svvhhhhhhh",
        limit=60,
        flops=6 * 10**9,
    )
    halo, part = together(halo, part)
    outgoing, keep, give, du = call(
        layer_kernel,
        [((owners // 4, 4, 16, 128), F32), (half, F32), (half, F32), (full, F32)],
        (core, halo, nbr, ew, part, weight, cotangent),
        spaces="svvvhhhhvvh",
        scratch=[pltpu.VMEM((width, width), F32)],
        limit=52,
        flops=3 * 10**9,
    )
    got, dest = together(swap(give), dest)
    pieces = trade(scatter(at_x, keep, got), "hist", 1)
    (grad_input,) = call(
        backward_kernel,
        [(full, F32)],
        (du, weight, high, low),
        spaces="hhhhh",
        limit=60,
        flops=2 * 10**9,
    )
    *pieces, grad_input = together(*pieces, grad_input)
    pieces = trade(scatter(at_y, *pieces), "batch", depth)
    arrived = exchange(outgoing.reshape(owners * 16, 128))
    summed = total(*pieces)
    summed = total(summed, *[move(summed, "batch", mask) for mask in (2, 4, 6)])
    summed = total(summed, move(summed, "batch", 1))
    arrived, summed = together(arrived, summed)
    arrived_other = swap(arrived)
    parts = trade([summed] * 4, "batch", depth)
    history = write_rows(core, dest, arrived, cold_history)
    *parts, history = together(*parts, history)
    summed = join(at_y, parts)
    parts = trade([summed] * 4, "hist", 1)
    history = write_rows(1 - core, dest, arrived_other, history)
    *parts, history = together(*parts, history)
    summed = join(at_x, parts)
    all_nodes = rows * lax.axis_size(("batch", "hist", "rep"))
    grad_weight = join(core, [summed, swap(summed)], BETA / math.sqrt(all_nodes))
    return (grad_weight, grad_input, history)


def solution(mesh):
    return jax.shard_map(
        body,
        mesh=mesh,
        in_specs=(
            P(("batch", "hist", "rep"), None),
            P(("batch", "hist", "rep"), None),
            P(("batch", "hist", "rep"), None),
            P(),
            P(("batch", "hist", "rep"), None),
            P(("batch", "hist", "rep"), None),
            P(("batch", "hist", "rep"), None, None),
            P(("batch", "hist"), None),
            P("rep", None),
            P(("batch", "hist"), None),
        ),
        out_specs=(P(), P(("batch", "hist", "rep"), None), P(("batch", "hist"), None)),
        check_vma=False,
    )
```

```python
import functools
import math

import jax
import jax.numpy as jnp
from jax import lax
from jax.experimental import pallas as pl
from jax.experimental.pallas import tpu as pltpu
from jax.sharding import PartitionSpec as P

ALPHA = 0.1
BETA = math.log(1.5)
OWN = ("batch", "hist")
F32 = jnp.float32
BF16 = jnp.bfloat16
GELU_C = math.sqrt(2.0 / math.pi)
GELU_A = 0.044715
VMEM = pl.BlockSpec(memory_space=pltpu.VMEM)
SMEM = pl.BlockSpec(memory_space=pltpu.SMEM)
HBM = pl.BlockSpec(memory_space=pltpu.HBM)
MIB = 1 << 20


def dot(a, b, left=1, right=0):
    return lax.dot_general(a, b, (((left,), (right,)), ((), ())), preferred_element_type=F32)


def split(v):
    high = v.astype(BF16)
    return high, (v - high.astype(F32)).astype(BF16)


def dot3(a, b, left=1, right=0):
    return dot(a[0], b[0], left, right) + (dot(a[0], b[1], left, right) + dot(a[1], b[0], left, right))


def lanes(rows, columns):
    return lax.broadcasted_iota(jnp.int32, (rows, columns), 1)


def one_hot(column, count):
    return (column == lanes(column.shape[0], count)).astype(BF16)


class Source:
    def __init__(self, ref, buffer, sem, rows=None):
        rows = rows or ref.shape[0]
        self.buffer, self.copies, self.shape = buffer, [], ref.shape
        for i in range(ref.shape[0] // rows):
            at = (pl.ds(i * rows, rows),) + (slice(None),) * (len(ref.shape) - 1)
            copy = pltpu.make_async_copy(ref.at[at], buffer.at[at], sem.at[i])
            copy.start()
            self.copies.append(copy)

    def __getitem__(self, index):
        for copy in self.copies:
            copy.wait()
        self.copies = []
        return self.buffer[index]

    def part(self, i):
        self.copies[i].wait()


class Sink:
    def __init__(self, ref, buffer, sem, rows=None):
        self.ref, self.buffer, self.sem = ref, buffer, sem
        self.rows, self.copies = rows or ref.shape[0], []
        self.shape = ref.shape

    def __setitem__(self, index, value):
        self.buffer[index] = value

    def push(self, i=0):
        at = (pl.ds(i * self.rows, self.rows),) + (slice(None),) * (len(self.shape) - 1)
        copy = pltpu.make_async_copy(self.buffer.at[at], self.ref.at[at], self.sem.at[i])
        copy.start()
        self.copies.append(copy)


def call(kernel, outs, args, spaces=None, scratch=(), limit=8, flops=0, rows=None):
    spaces = spaces or "v" * (len(args) + len(outs))
    shapes = [(a.shape, a.dtype) for a in args] + list(outs)
    where = {"s": SMEM, "v": VMEM, "h": HBM}
    remote = [i for i, space in enumerate(spaces) if space == "h"]
    buffers = [pltpu.VMEM(*shapes[i]) for i in remote]
    sems = [pltpu.SemaphoreType.DMA((shapes[i][0][0] // rows if rows else 1,)) for i in remote]

    def wrapped(*refs):
        refs, rest = list(refs[: len(shapes)]), refs[len(shapes) :]
        sinks = []
        for n, i in enumerate(remote):
            kind = Source if i < len(args) else Sink
            refs[i] = kind(refs[i], rest[n], rest[len(remote) + n], rows)
            if kind is Sink:
                sinks.append(refs[i])
        kernel(*refs, *rest[2 * len(remote) :])
        for sink in sinks:
            for copy in sink.copies:
                copy.wait()

    count = sum(math.prod(shape) * 4 for shape, _ in shapes)
    return pl.pallas_call(
        wrapped,
        out_shape=[jax.ShapeDtypeStruct(*o) for o in outs],
        in_specs=[where[c] for c in spaces[: len(args)]],
        out_specs=[where[c] for c in spaces[len(args) :]],
        scratch_shapes=buffers + sems + list(scratch),
        compiler_params=pltpu.CompilerParams(vmem_limit_bytes=limit * MIB),
        cost_estimate=pl.CostEstimate(flops=flops, bytes_accessed=count, transcendentals=0),
    )(*args)


def gather_kernel(idx_ref, cold_ref, out_ref):
    owners, per = idx_ref.shape
    step = cold_ref.shape[0] // len(cold_ref.copies)
    found = jnp.zeros((per * owners, cold_ref.shape[1]), F32)
    idx = jnp.concatenate([idx_ref[:, s : s + 1] for s in range(per)], axis=0)
    picks = [one_hot(idx - block * step, step) for block in range(len(cold_ref.copies))]
    for block, pick in enumerate(picks):
        cold_ref.part(block)
        high, low = split(cold_ref.buffer[block * step : (block + 1) * step, :])
        found = found + (dot(pick, high) + dot(pick, low))
    for s in range(per):
        for l in range(4):
            out_ref[pl.ds(s * 4 + l, owners, stride=per * 4), :] = found[
                s * owners : (s + 1) * owners, l * 128 : (l + 1) * 128
            ]


def prepare_kernel(
    core_ref, nbr_ref, ew_ref, mine_ref, other_ref, node_ref, init_ref,
    part_ref, high_ref, low_ref, *, halo_count,
):
    rows = node_ref.shape[0]
    half = mine_ref.shape[0]
    core = core_ref[0]
    nbr = nbr_ref[...].T
    ew = ew_ref[...].T
    ids = lanes(rows, rows)
    tile = jnp.zeros((rows, rows), F32)
    for k in range(2, nbr.shape[1]):
        tile = tile + jnp.where(nbr[:, k : k + 1] == ids, ew[:, k : k + 1], 0.0)
    tiles = split(tile)
    high_ref[...] = tiles[0]
    low_ref[...] = tiles[1]
    high_ref.push()
    low_ref.push()
    hot = nbr[:, 1:2] - (rows + halo_count)
    picked = jnp.zeros((rows, node_ref.shape[1]), F32)
    for ref, base in ((mine_ref, core * half), (other_ref, (1 - core) * half)):
        choose = one_hot(hot - base, half)
        for piece in split(ref[...]):
            picked = picked + dot(choose, piece)
    agg = dot3(tiles, split(node_ref[...])) + ew[:, 1:2] * picked
    part_ref[...] = (1.0 - ALPHA) * agg + ALPHA * init_ref[...]
    part_ref.push()


def layer_kernel(
    core_ref, halo_ref, nbr_ref, ew_ref, part_ref, weight_ref, cot_ref,
    out_ref, keep_ref, give_ref, du_ref, term_ref,
):
    owners = halo_ref.shape[0] // 8
    halo = jnp.concatenate(
        [
            jnp.concatenate(
                [halo_ref[pl.ds(s * 4 + l, owners, stride=8), :] for l in range(4)], axis=1
            )
            for s in range(2)
        ],
        axis=0,
    )
    place = nbr_ref[...].T[:, :1] - part_ref.shape[0]
    pick = one_hot((place & 1) * owners + (place >> 1), 2 * owners)
    high, low = split(halo)
    ew = ew_ref[...].T[:, :1]
    z = part_ref[...] + ((1.0 - ALPHA) * ew) * (dot(pick, high) + dot(pick, low))
    zs = split(z)
    u = (1.0 - BETA) * z + BETA * dot3(zs, split(weight_ref[...]))
    square = u * u
    bent = jnp.tanh(GELU_C * (u + GELU_A * (square * u)))
    embed = (0.5 * u) * (1.0 + bent)
    slope = 0.5 * (1.0 + bent) + (0.5 * u) * (1.0 - bent * bent) * (
        GELU_C * (1.0 + (3.0 * GELU_A) * square)
    )
    du = cot_ref[...] * slope
    du_ref[...] = du
    du_ref.push()
    groups = out_ref.shape[0]
    top = lax.broadcasted_iota(jnp.int32, (groups, 2, 8, 128), 2) < 4
    for pair in range(2):
        x, y = (
            embed[:, l * 128 : (l + 1) * 128].reshape(groups, 2, 8, 128)
            for l in (2 * pair, 2 * pair + 1)
        )
        even = jnp.where(top, x, pltpu.roll(y, 4, 2))
        odd = jnp.where(top, pltpu.roll(x, 4, 2), y)
        for h in range(2):
            out_ref[:, 2 * h, 8 * pair : 8 * pair + 8, :] = even[:, h]
            out_ref[:, 2 * h + 1, 8 * pair : 8 * pair + 8, :] = odd[:, h]
    out_ref.push()
    term_ref[...] = dot3(zs, split(du), 0, 0)
    half = term_ref.shape[0] // 2
    core = core_ref[0]
    keep_ref[...] = term_ref[pl.ds(pl.multiple_of(core * half, half), half), :]
    give_ref[...] = term_ref[pl.ds(pl.multiple_of((1 - core) * half, half), half), :]


def scatter_kernel(me_ref, *refs):
    terms, outs, total_ref = refs[: -1 - 4], refs[-1 - 4 : -1], refs[-1]
    total_ref[...] = functools.reduce(lambda x, y: x + y, [t[...] for t in terms])
    size = outs[0].shape[0]
    for shift, out in enumerate(outs):
        at = jnp.bitwise_xor(me_ref[0], shift) * size
        out[...] = total_ref[pl.ds(pl.multiple_of(at, size), size), :]


def total_kernel(*refs):
    terms = [t[...] for t in refs[:-1]]
    while len(terms) > 1:
        terms = [x + y for x, y in zip(terms[::2], terms[1::2])]
    refs[-1][...] = terms[0]


def join_kernel(me_ref, *refs, scale=None):
    size = refs[0].shape[0]
    for shift, part in enumerate(refs[:-1]):
        at = jnp.bitwise_xor(me_ref[0], shift) * size
        value = part[...] if scale is None else part[...] * scale
        refs[-1][pl.ds(pl.multiple_of(at, size), size), :] = value


def backward_kernel(du_ref, weight_ref, high_ref, low_ref, out_ref):
    du = du_ref[...]
    dz = (1.0 - BETA) * du + BETA * dot3(split(du), split(weight_ref[...]), 1, 1)
    out_ref[...] = (1.0 - ALPHA) * dot3((high_ref[...], low_ref[...]), split(dz), 0, 0)
    out_ref.push()


def history_kernel(which_ref, dest_ref, recv_ref, base_ref, out_ref, high_ref, low_ref):
    owners = recv_ref.shape[0] // 16
    for s in range(4):
        for l in range(4):
            high, low = split(recv_ref[pl.ds(4 * l + s, owners, stride=16), :])
            at = slice(s * owners, (s + 1) * owners)
            high_ref[at, l * 128 : (l + 1) * 128] = high
            low_ref[at, l * 128 : (l + 1) * 128] = low
    dest = dest_ref[pl.ds(which_ref[0], 1), :]
    step = out_ref.rows
    for block in range(out_ref.shape[0] // step):
        ids = lax.broadcasted_iota(jnp.int32, (step, dest.shape[1]), 0) + block * step
        hit = jnp.where(ids == dest, 1.0, 0.0)
        count = jnp.sum(hit, axis=1, keepdims=True)
        place = hit.astype(BF16)
        written = dot(place, high_ref[...]) + dot(place, low_ref[...])
        at = slice(block * step, (block + 1) * step)
        base_ref.part(block)
        out_ref[at, :] = jnp.where(count > 0.5, written, base_ref.buffer[at, :])
        out_ref.push(block)


def write_rows(which, dest, recv, base):
    rows, width = dest.shape[1], base.shape[1]
    return call(
        history_kernel,
        [(base.shape, F32)],
        (which, dest, recv, base),
        spaces="svvhh",
        scratch=[pltpu.VMEM((rows, width), BF16), pltpu.VMEM((rows, width), BF16)],
        limit=52,
        flops=2 * 10**9,
        rows=256,
    )[0]


def exchange(v):
    return lax.all_to_all(v, OWN, split_axis=0, concat_axis=0, tiled=True)


def swap(v):
    return lax.ppermute(v, "rep", [(0, 1), (1, 0)])


def move(v, axis, mask):
    count = lax.axis_size(axis)
    return lax.ppermute(v, axis, [(i, i ^ mask) for i in range(count)])


def scatter(me, *terms):
    size = terms[0].shape[0] // 4
    return call(
        scatter_kernel,
        [((size, terms[0].shape[1]), F32)] * 4,
        (me,) + terms,
        spaces="s" + "v" * (len(terms) + 4),
        scratch=[pltpu.VMEM(terms[0].shape, F32)],
    )


def trade(pieces, axis, unit):
    return [pieces[0]] + [move(pieces[shift], axis, shift * unit) for shift in (1, 2, 3)]


def total(*terms):
    return call(total_kernel, [(terms[0].shape, F32)], terms)[0]


def join(me, parts, scale=None):
    rows, width = parts[0].shape
    return call(
        functools.partial(join_kernel, scale=scale),
        [((rows * len(parts), width), F32)],
        (me,) + tuple(parts),
        spaces="s" + "v" * (len(parts) + 1),
    )[0]


def together(*values):
    return lax.optimization_barrier(values)


def body(
    node_input,
    initial,
    cotangent,
    weight,
    edge_weight,
    neighbors,
    halo_rows,
    cold_history,
    hot_history,
    dest_rows,
):
    rows, width = node_input.shape
    owners = lax.axis_size(OWN)
    halo_count = owners * halo_rows.shape[2]
    core = lax.axis_index("rep").astype(jnp.int32).reshape(1)
    at_x = lax.axis_index("hist").astype(jnp.int32).reshape(1)
    depth = lax.axis_size("batch") // 4
    at_y = lax.div(lax.axis_index("batch").astype(jnp.int32), jnp.int32(depth)).reshape(1)
    full = (rows, width)
    half = (rows // 2, width)
    nbr = neighbors.T
    ew = edge_weight.T
    dest = jnp.transpose(dest_rows.reshape(2, owners, 4), (0, 2, 1)).reshape(2, rows)

    wanted = exchange(halo_rows[0])
    (found,) = call(
        gather_kernel,
        [((halo_count * 4, 128), F32)],
        (wanted, cold_history),
        spaces="vhv",
        rows=256,
        limit=60,
        flops=10**9,
    )
    halo = exchange(found)
    part, high, low = call(
        functools.partial(prepare_kernel, halo_count=halo_count),
        [(full, F32), ((rows, rows), BF16), ((rows, rows), BF16)],
        (core, nbr, ew, hot_history, swap(hot_history), node_input, initial),
        spaces="svvhhhhhhh",
        limit=60,
        flops=6 * 10**9,
    )
    halo, part = together(halo, part)
    outgoing, keep, give, du = call(
        layer_kernel,
        [((owners // 4, 4, 16, 128), F32), (half, F32), (half, F32), (full, F32)],
        (core, halo, nbr, ew, part, weight, cotangent),
        spaces="svvvhhhhvvh",
        scratch=[pltpu.VMEM((width, width), F32)],
        limit=52,
        flops=3 * 10**9,
    )
    got, dest = together(swap(give), dest)
    pieces = trade(scatter(at_x, keep, got), "hist", 1)
    (grad_input,) = call(
        backward_kernel,
        [(full, F32)],
        (du, weight, high, low),
        spaces="hhhhh",
        limit=60,
        flops=2 * 10**9,
    )
    *pieces, grad_input = together(*pieces, grad_input)
    pieces = trade(scatter(at_y, *pieces), "batch", depth)
    arrived = exchange(outgoing.reshape(owners * 16, 128))
    summed = total(*pieces)
    mask = 1
    while mask < depth:
        summed = total(summed, move(summed, "batch", mask))
        mask *= 2
    arrived, summed = together(arrived, summed)
    arrived_other = swap(arrived)
    parts = trade([summed] * 4, "batch", depth)
    history = write_rows(core, dest, arrived, cold_history)
    *parts, history = together(*parts, history)
    summed = join(at_y, parts)
    parts = trade([summed] * 4, "hist", 1)
    history = write_rows(1 - core, dest, arrived_other, history)
    *parts, history = together(*parts, history)
    summed = join(at_x, parts)
    all_nodes = rows * lax.axis_size(("batch", "hist", "rep"))
    grad_weight = join(core, [summed, swap(summed)], BETA / math.sqrt(all_nodes))
    return (grad_weight, grad_input, history)


def solution(mesh):
    return jax.shard_map(
        body,
        mesh=mesh,
        in_specs=(
            P(("batch", "hist", "rep"), None),
            P(("batch", "hist", "rep"), None),
            P(("batch", "hist", "rep"), None),
            P(),
            P(("batch", "hist", "rep"), None),
            P(("batch", "hist", "rep"), None),
            P(("batch", "hist", "rep"), None, None),
            P(("batch", "hist"), None),
            P("rep", None),
            P(("batch", "hist"), None),
        ),
        out_specs=(P(), P(("batch", "hist", "rep"), None), P(("batch", "hist"), None)),
        check_vma=False,
    )
```

```python
import functools
import math

import jax
import jax.numpy as jnp
from jax import lax
from jax.experimental import pallas as pl
from jax.experimental.pallas import tpu as pltpu
from jax.sharding import Mesh
from jax.sharding import PartitionSpec as P

ALPHA = 0.1
BETA = math.log(1.5)
OWN = ("y", "z", "hist")
PLANE = ("y", "hist")
ALL = ("y", "z", "hist", "rep")
F32 = jnp.float32
BF16 = jnp.bfloat16
GELU_C = math.sqrt(2.0 / math.pi)
GELU_A = 0.044715
VMEM = pl.BlockSpec(memory_space=pltpu.VMEM)
SMEM = pl.BlockSpec(memory_space=pltpu.SMEM)
HBM = pl.BlockSpec(memory_space=pltpu.HBM)
MIB = 1 << 20


def dot(a, b, left=1, right=0):
    return lax.dot_general(a, b, (((left,), (right,)), ((), ())), preferred_element_type=F32)


def split(v):
    high = v.astype(BF16)
    return high, (v - high.astype(F32)).astype(BF16)


def dot3(a, b, left=1, right=0):
    return dot(a[0], b[0], left, right) + (dot(a[0], b[1], left, right) + dot(a[1], b[0], left, right))


def lanes(rows, columns):
    return lax.broadcasted_iota(jnp.int32, (rows, columns), 1)


def one_hot(column, count):
    return (column == lanes(column.shape[0], count)).astype(BF16)


class Source:
    def __init__(self, ref, buffer, sem, rows=None):
        rows = rows or ref.shape[0]
        self.buffer, self.copies, self.shape = buffer, [], ref.shape
        for i in range(ref.shape[0] // rows):
            at = (pl.ds(i * rows, rows),) + (slice(None),) * (len(ref.shape) - 1)
            copy = pltpu.make_async_copy(ref.at[at], buffer.at[at], sem.at[i])
            copy.start()
            self.copies.append(copy)

    def __getitem__(self, index):
        for copy in self.copies:
            copy.wait()
        self.copies = []
        return self.buffer[index]

    def part(self, i):
        self.copies[i].wait()


class Sink:
    def __init__(self, ref, buffer, sem, rows=None):
        self.ref, self.buffer, self.sem = ref, buffer, sem
        self.rows, self.copies = rows or ref.shape[0], []
        self.shape = ref.shape

    def __setitem__(self, index, value):
        self.buffer[index] = value

    def push(self, i=0):
        at = (pl.ds(i * self.rows, self.rows),) + (slice(None),) * (len(self.shape) - 1)
        copy = pltpu.make_async_copy(self.buffer.at[at], self.ref.at[at], self.sem.at[i])
        copy.start()
        self.copies.append(copy)


def call(kernel, outs, args, spaces=None, scratch=(), limit=8, flops=0, rows=None):
    spaces = spaces or "v" * (len(args) + len(outs))
    shapes = [(a.shape, a.dtype) for a in args] + list(outs)
    where = {"s": SMEM, "v": VMEM, "h": HBM}
    remote = [i for i, space in enumerate(spaces) if space == "h"]
    buffers = [pltpu.VMEM(*shapes[i]) for i in remote]
    sems = [pltpu.SemaphoreType.DMA((shapes[i][0][0] // rows if rows else 1,)) for i in remote]

    def wrapped(*refs):
        refs, rest = list(refs[: len(shapes)]), refs[len(shapes) :]
        sinks = []
        for n, i in enumerate(remote):
            kind = Source if i < len(args) else Sink
            refs[i] = kind(refs[i], rest[n], rest[len(remote) + n], rows)
            if kind is Sink:
                sinks.append(refs[i])
        kernel(*refs, *rest[2 * len(remote) :])
        for sink in sinks:
            for copy in sink.copies:
                copy.wait()

    count = sum(math.prod(shape) * 4 for shape, _ in shapes)
    return pl.pallas_call(
        wrapped,
        out_shape=[jax.ShapeDtypeStruct(*o) for o in outs],
        in_specs=[where[c] for c in spaces[: len(args)]],
        out_specs=[where[c] for c in spaces[len(args) :]],
        scratch_shapes=buffers + sems + list(scratch),
        compiler_params=pltpu.CompilerParams(vmem_limit_bytes=limit * MIB),
        cost_estimate=pl.CostEstimate(flops=flops, bytes_accessed=count, transcendentals=0),
    )(*args)


def gather_kernel(idx_ref, cold_ref, out_ref):
    owners, per = idx_ref.shape
    step = cold_ref.shape[0] // len(cold_ref.copies)
    found = jnp.zeros((per * owners, cold_ref.shape[1]), F32)
    idx = jnp.concatenate([idx_ref[:, s : s + 1] for s in range(per)], axis=0)
    picks = [one_hot(idx - block * step, step) for block in range(len(cold_ref.copies))]
    for block, pick in enumerate(picks):
        cold_ref.part(block)
        high, low = split(cold_ref.buffer[block * step : (block + 1) * step, :])
        found = found + (dot(pick, high) + dot(pick, low))
    for s in range(per):
        for l in range(4):
            out_ref[pl.ds(s * 4 + l, owners, stride=per * 4), :] = found[
                s * owners : (s + 1) * owners, l * 128 : (l + 1) * 128
            ]


def prepare_kernel(
    core_ref, nbr_ref, ew_ref, mine_ref, other_ref, node_ref, init_ref,
    part_ref, high_ref, low_ref, *, halo_count,
):
    rows = node_ref.shape[0]
    half = mine_ref.shape[0]
    core = core_ref[0]
    nbr = nbr_ref[...].T
    ew = ew_ref[...].T
    ids = lanes(rows, rows)
    tile = jnp.zeros((rows, rows), F32)
    for k in range(2, nbr.shape[1]):
        tile = tile + jnp.where(nbr[:, k : k + 1] == ids, ew[:, k : k + 1], 0.0)
    tiles = split(tile)
    high_ref[...] = tiles[0]
    low_ref[...] = tiles[1]
    high_ref.push()
    low_ref.push()
    hot = nbr[:, 1:2] - (rows + halo_count)
    picked = jnp.zeros((rows, node_ref.shape[1]), F32)
    for ref, base in ((mine_ref, core * half), (other_ref, (1 - core) * half)):
        choose = one_hot(hot - base, half)
        for piece in split(ref[...]):
            picked = picked + dot(choose, piece)
    agg = dot3(tiles, split(node_ref[...])) + ew[:, 1:2] * picked
    part_ref[...] = (1.0 - ALPHA) * agg + ALPHA * init_ref[...]
    part_ref.push()


def layer_kernel(
    core_ref, halo_ref, nbr_ref, ew_ref, part_ref, weight_ref, cot_ref,
    out_ref, keep_ref, give_ref, du_ref, term_ref,
):
    owners = halo_ref.shape[0] // 8
    halo = jnp.concatenate(
        [
            jnp.concatenate(
                [halo_ref[pl.ds(s * 4 + l, owners, stride=8), :] for l in range(4)], axis=1
            )
            for s in range(2)
        ],
        axis=0,
    )
    place = nbr_ref[...].T[:, :1] - part_ref.shape[0]
    pick = one_hot((place & 1) * owners + (place >> 1), 2 * owners)
    high, low = split(halo)
    ew = ew_ref[...].T[:, :1]
    z = part_ref[...] + ((1.0 - ALPHA) * ew) * (dot(pick, high) + dot(pick, low))
    zs = split(z)
    u = (1.0 - BETA) * z + BETA * dot3(zs, split(weight_ref[...]))
    square = u * u
    bent = jnp.tanh(GELU_C * (u + GELU_A * (square * u)))
    embed = (0.5 * u) * (1.0 + bent)
    slope = 0.5 * (1.0 + bent) + (0.5 * u) * (1.0 - bent * bent) * (
        GELU_C * (1.0 + (3.0 * GELU_A) * square)
    )
    du = cot_ref[...] * slope
    du_ref[...] = du
    du_ref.push()
    groups = out_ref.shape[0]
    top = lax.broadcasted_iota(jnp.int32, (groups, 2, 8, 128), 2) < 4
    for pair in range(2):
        x, y = (
            embed[:, l * 128 : (l + 1) * 128].reshape(groups, 2, 8, 128)
            for l in (2 * pair, 2 * pair + 1)
        )
        even = jnp.where(top, x, pltpu.roll(y, 4, 2))
        odd = jnp.where(top, pltpu.roll(x, 4, 2), y)
        for h in range(2):
            out_ref[:, 2 * h, 8 * pair : 8 * pair + 8, :] = even[:, h]
            out_ref[:, 2 * h + 1, 8 * pair : 8 * pair + 8, :] = odd[:, h]
    out_ref.push()
    term_ref[...] = dot3(zs, split(du), 0, 0)
    half = term_ref.shape[0] // 2
    core = core_ref[0]
    keep_ref[...] = term_ref[pl.ds(pl.multiple_of(core * half, half), half), :]
    give_ref[...] = term_ref[pl.ds(pl.multiple_of((1 - core) * half, half), half), :]


def scatter_kernel(me_ref, *refs):
    terms, outs, total_ref = refs[: -1 - 4], refs[-1 - 4 : -1], refs[-1]
    total_ref[...] = functools.reduce(lambda x, y: x + y, [t[...] for t in terms])
    size = outs[0].shape[0]
    for shift, out in enumerate(outs):
        at = jnp.bitwise_xor(me_ref[0], shift) * size
        out[...] = total_ref[pl.ds(pl.multiple_of(at, size), size), :]


def total_kernel(*refs):
    terms = [t[...] for t in refs[:-1]]
    while len(terms) > 1:
        terms = [x + y for x, y in zip(terms[::2], terms[1::2])]
    refs[-1][...] = terms[0]


def spread_kernel(mine_ref, other_ref, out_ref):
    out_ref[...] = jnp.broadcast_to((mine_ref[...] + other_ref[...])[None], out_ref.shape)


def assemble_kernel(core_ref, mine_ref, other_ref, out_ref, *, scale):
    half = out_ref.shape[0] // 2
    size = mine_ref.shape[1]
    for ref, which in ((mine_ref, core_ref[0]), (other_ref, 1 - core_ref[0])):
        for y in range(4):
            for x in range(4):
                at = which * half + (x * 4 + y) * size
                out_ref[pl.ds(pl.multiple_of(at, size), size), :] = ref[y * 4 + x] * scale


def backward_kernel(du_ref, weight_ref, high_ref, low_ref, out_ref):
    du = du_ref[...]
    dz = (1.0 - BETA) * du + BETA * dot3(split(du), split(weight_ref[...]), 1, 1)
    out_ref[...] = (1.0 - ALPHA) * dot3((high_ref[...], low_ref[...]), split(dz), 0, 0)
    out_ref.push()


def history_kernel(which_ref, dest_ref, recv_ref, base_ref, out_ref, high_ref, low_ref):
    owners = recv_ref.shape[0] // 16
    for s in range(4):
        for l in range(4):
            high, low = split(recv_ref[pl.ds(4 * l + s, owners, stride=16), :])
            at = slice(s * owners, (s + 1) * owners)
            high_ref[at, l * 128 : (l + 1) * 128] = high
            low_ref[at, l * 128 : (l + 1) * 128] = low
    dest = dest_ref[pl.ds(which_ref[0], 1), :]
    step = out_ref.rows
    for block in range(out_ref.shape[0] // step):
        ids = lax.broadcasted_iota(jnp.int32, (step, dest.shape[1]), 0) + block * step
        hit = jnp.where(ids == dest, 1.0, 0.0)
        count = jnp.sum(hit, axis=1, keepdims=True)
        place = hit.astype(BF16)
        written = dot(place, high_ref[...]) + dot(place, low_ref[...])
        at = slice(block * step, (block + 1) * step)
        base_ref.part(block)
        out_ref[at, :] = jnp.where(count > 0.5, written, base_ref.buffer[at, :])
        out_ref.push(block)


def write_rows(which, dest, recv, base):
    rows, width = dest.shape[1], base.shape[1]
    return call(
        history_kernel,
        [(base.shape, F32)],
        (which, dest, recv, base),
        spaces="svvhh",
        scratch=[pltpu.VMEM((rows, width), BF16), pltpu.VMEM((rows, width), BF16)],
        limit=52,
        flops=2 * 10**9,
        rows=256,
    )[0]


def exchange(v, axes=OWN):
    return lax.all_to_all(v, axes, split_axis=0, concat_axis=0, tiled=True)


def swap(v):
    return lax.ppermute(v, "rep", [(0, 1), (1, 0)])


def move(v, axis, mask):
    count = lax.axis_size(axis)
    return lax.ppermute(v, axis, [(i, i ^ mask) for i in range(count)])


def scatter(me, *terms):
    size = terms[0].shape[0] // 4
    return call(
        scatter_kernel,
        [((size, terms[0].shape[1]), F32)] * 4,
        (me,) + terms,
        spaces="s" + "v" * (len(terms) + 4),
        scratch=[pltpu.VMEM(terms[0].shape, F32)],
    )


def trade(pieces, axis):
    return [pieces[0]] + [move(pieces[shift], axis, shift) for shift in (1, 2, 3)]


def total(*terms):
    return call(total_kernel, [(terms[0].shape, F32)], terms)[0]


def together(*values):
    return lax.optimization_barrier(values)


def body(
    node_input,
    initial,
    cotangent,
    weight,
    edge_weight,
    neighbors,
    halo_rows,
    cold_history,
    hot_history,
    dest_rows,
):
    rows, width = node_input.shape
    owners = lax.axis_size(OWN)
    halo_count = owners * halo_rows.shape[2]
    core = lax.axis_index("rep").astype(jnp.int32).reshape(1)
    at_x = lax.axis_index("hist").astype(jnp.int32).reshape(1)
    at_y = lax.axis_index("y").astype(jnp.int32).reshape(1)
    full = (rows, width)
    half = (rows // 2, width)
    nbr = neighbors.T
    ew = edge_weight.T
    dest = jnp.transpose(dest_rows.reshape(2, owners, 4), (0, 2, 1)).reshape(2, rows)

    wanted = exchange(halo_rows[0])
    (found,) = call(
        gather_kernel,
        [((halo_count * 4, 128), F32)],
        (wanted, cold_history),
        spaces="vhv",
        rows=256,
        limit=60,
        flops=10**9,
    )
    halo = exchange(found)
    part, high, low = call(
        functools.partial(prepare_kernel, halo_count=halo_count),
        [(full, F32), ((rows, rows), BF16), ((rows, rows), BF16)],
        (core, nbr, ew, hot_history, swap(hot_history), node_input, initial),
        spaces="svvhhhhhhh",
        limit=60,
        flops=6 * 10**9,
    )
    halo, part = together(halo, part)
    outgoing, keep, give, du = call(
        layer_kernel,
        [((owners // 4, 4, 16, 128), F32), (half, F32), (half, F32), (full, F32)],
        (core, halo, nbr, ew, part, weight, cotangent),
        spaces="svvvhhhhvvh",
        scratch=[pltpu.VMEM((width, width), F32)],
        limit=52,
        flops=3 * 10**9,
    )
    got, dest = together(swap(give), dest)
    pieces = trade(scatter(at_x, keep, got), "hist")
    (grad_input,) = call(
        backward_kernel,
        [(full, F32)],
        (du, weight, high, low),
        spaces="hhhhh",
        limit=60,
        flops=2 * 10**9,
    )
    *pieces, grad_input = together(*pieces, grad_input)
    pieces = trade(scatter(at_y, *pieces), "y")
    arrived = exchange(outgoing.reshape(owners * 16, 128))
    summed = total(*pieces)
    mask = 1
    while 2 * mask < lax.axis_size("z"):
        summed = total(summed, move(summed, "z", mask))
        mask *= 2
    plane = lax.axis_size(PLANE)
    (spread,) = call(
        spread_kernel, [((plane,) + summed.shape, F32)], (summed, move(summed, "z", mask))
    )
    arrived, spread = together(arrived, spread)
    arrived_other = swap(arrived)
    gathered = exchange(spread, PLANE)
    history = write_rows(core, dest, arrived, cold_history)
    history = write_rows(1 - core, dest, arrived_other, history)
    gathered, history = together(gathered, history)
    all_nodes = rows * lax.axis_size(ALL)
    (grad_weight,) = call(
        functools.partial(assemble_kernel, scale=BETA / math.sqrt(all_nodes)),
        [((width, width), F32)],
        (core, gathered, swap(gathered)),
        spaces="svvv",
    )
    return (grad_weight, grad_input, history)


def solution(mesh):
    batch, hist, rep = mesh.devices.shape
    mesh = Mesh(mesh.devices.reshape(4, batch // 4, hist, rep), ALL)
    return jax.shard_map(
        body,
        mesh=mesh,
        in_specs=(
            P(ALL, None),
            P(ALL, None),
            P(ALL, None),
            P(),
            P(ALL, None),
            P(ALL, None),
            P(ALL, None, None),
            P(OWN, None),
            P("rep", None),
            P(OWN, None),
        ),
        out_specs=(P(), P(ALL, None), P(OWN, None)),
        check_vma=False,
    )
```

```python
import functools
import math

import jax
import jax.numpy as jnp
from jax import lax
from jax.experimental import pallas as pl
from jax.experimental.pallas import tpu as pltpu
from jax.sharding import Mesh
from jax.sharding import PartitionSpec as P

ALPHA = 0.1
BETA = math.log(1.5)
OWN = ("y", "z", "hist")
PLANE = ("y", "hist")
ALL = ("y", "z", "hist", "rep")
F32 = jnp.float32
BF16 = jnp.bfloat16
GELU_C = math.sqrt(2.0 / math.pi)
GELU_A = 0.044715
VMEM = pl.BlockSpec(memory_space=pltpu.VMEM)
SMEM = pl.BlockSpec(memory_space=pltpu.SMEM)
HBM = pl.BlockSpec(memory_space=pltpu.HBM)
MIB = 1 << 20


def dot(a, b, left=1, right=0):
    return lax.dot_general(a, b, (((left,), (right,)), ((), ())), preferred_element_type=F32)


def split(v):
    high = v.astype(BF16)
    return high, (v - high.astype(F32)).astype(BF16)


def dot3(a, b, left=1, right=0):
    return dot(a[0], b[0], left, right) + (dot(a[0], b[1], left, right) + dot(a[1], b[0], left, right))


def lanes(rows, columns):
    return lax.broadcasted_iota(jnp.int32, (rows, columns), 1)


def one_hot(column, count):
    return (column == lanes(column.shape[0], count)).astype(BF16)


class Source:
    def __init__(self, ref, buffer, sem, rows=None):
        rows = rows or ref.shape[0]
        self.buffer, self.copies, self.shape = buffer, [], ref.shape
        for i in range(ref.shape[0] // rows):
            at = (pl.ds(i * rows, rows),) + (slice(None),) * (len(ref.shape) - 1)
            copy = pltpu.make_async_copy(ref.at[at], buffer.at[at], sem.at[i])
            copy.start()
            self.copies.append(copy)

    def __getitem__(self, index):
        for copy in self.copies:
            copy.wait()
        self.copies = []
        return self.buffer[index]

    def part(self, i):
        self.copies[i].wait()


class Sink:
    def __init__(self, ref, buffer, sem, rows=None):
        self.ref, self.buffer, self.sem = ref, buffer, sem
        self.rows, self.copies = rows or ref.shape[0], []
        self.shape = ref.shape

    def __setitem__(self, index, value):
        self.buffer[index] = value

    def push(self, i=0):
        at = (pl.ds(i * self.rows, self.rows),) + (slice(None),) * (len(self.shape) - 1)
        copy = pltpu.make_async_copy(self.buffer.at[at], self.ref.at[at], self.sem.at[i])
        copy.start()
        self.copies.append(copy)


def call(kernel, outs, args, spaces=None, scratch=(), limit=8, flops=0, rows=None):
    spaces = spaces or "v" * (len(args) + len(outs))
    shapes = [(a.shape, a.dtype) for a in args] + list(outs)
    where = {"s": SMEM, "v": VMEM, "h": HBM}
    remote = [i for i, space in enumerate(spaces) if space == "h"]
    buffers = [pltpu.VMEM(*shapes[i]) for i in remote]
    sems = [pltpu.SemaphoreType.DMA((shapes[i][0][0] // rows if rows else 1,)) for i in remote]

    def wrapped(*refs):
        refs, rest = list(refs[: len(shapes)]), refs[len(shapes) :]
        sinks = []
        for n, i in enumerate(remote):
            kind = Source if i < len(args) else Sink
            refs[i] = kind(refs[i], rest[n], rest[len(remote) + n], rows)
            if kind is Sink:
                sinks.append(refs[i])
        kernel(*refs, *rest[2 * len(remote) :])
        for sink in sinks:
            for copy in sink.copies:
                copy.wait()

    count = sum(math.prod(shape) * 4 for shape, _ in shapes)
    return pl.pallas_call(
        wrapped,
        out_shape=[jax.ShapeDtypeStruct(*o) for o in outs],
        in_specs=[where[c] for c in spaces[: len(args)]],
        out_specs=[where[c] for c in spaces[len(args) :]],
        scratch_shapes=buffers + sems + list(scratch),
        compiler_params=pltpu.CompilerParams(vmem_limit_bytes=limit * MIB),
        cost_estimate=pl.CostEstimate(flops=flops, bytes_accessed=count, transcendentals=0),
    )(*args)


def gather_kernel(idx_ref, cold_ref, out_ref):
    owners, per = idx_ref.shape
    step = cold_ref.shape[0] // len(cold_ref.copies)
    found = jnp.zeros((per * owners, cold_ref.shape[1]), F32)
    idx = jnp.concatenate([idx_ref[:, s : s + 1] for s in range(per)], axis=0)
    picks = [one_hot(idx - block * step, step) for block in range(len(cold_ref.copies))]
    for block, pick in enumerate(picks):
        cold_ref.part(block)
        high, low = split(cold_ref.buffer[block * step : (block + 1) * step, :])
        found = found + (dot(pick, high) + dot(pick, low))
    for s in range(per):
        for l in range(4):
            out_ref[pl.ds(s * 4 + l, owners, stride=per * 4), :] = found[
                s * owners : (s + 1) * owners, l * 128 : (l + 1) * 128
            ]


def prepare_kernel(
    core_ref, nbr_ref, ew_ref, mine_ref, other_ref, node_ref, init_ref, weight_ref,
    part_ref, high_ref, low_ref, whigh_ref, wlow_ref, *, halo_count,
):
    rows = node_ref.shape[0]
    weights = split(weight_ref[...])
    whigh_ref[...] = weights[0]
    wlow_ref[...] = weights[1]
    whigh_ref.push()
    wlow_ref.push()
    half = mine_ref.shape[0]
    core = core_ref[0]
    nbr = nbr_ref[...].T
    ew = ew_ref[...].T
    ids = lanes(rows, rows)
    tile = jnp.zeros((rows, rows), F32)
    for k in range(2, nbr.shape[1]):
        tile = tile + jnp.where(nbr[:, k : k + 1] == ids, ew[:, k : k + 1], 0.0)
    tiles = split(tile)
    high_ref[...] = tiles[0]
    low_ref[...] = tiles[1]
    high_ref.push()
    low_ref.push()
    hot = nbr[:, 1:2] - (rows + halo_count)
    picked = jnp.zeros((rows, node_ref.shape[1]), F32)
    for ref, base in ((mine_ref, core * half), (other_ref, (1 - core) * half)):
        choose = one_hot(hot - base, half)
        for piece in split(ref[...]):
            picked = picked + dot(choose, piece)
    agg = dot3(tiles, split(node_ref[...])) + ew[:, 1:2] * picked
    part_ref[...] = (1.0 - ALPHA) * agg + ALPHA * init_ref[...]
    part_ref.push()


def layer_kernel(
    core_ref, halo_ref, nbr_ref, ew_ref, part_ref, whigh_ref, wlow_ref, cot_ref,
    out_ref, keep_ref, give_ref, du_ref,
    term_ref, work_ref, zhigh_ref, zlow_ref, dhigh_ref, dlow_ref,
):
    owners = halo_ref.shape[0] // 8
    rows = part_ref.shape[0]
    block, step = 128, 32
    halo = jnp.concatenate(
        [
            jnp.concatenate(
                [halo_ref[pl.ds(s * 4 + l, owners, stride=8), :] for l in range(4)], axis=1
            )
            for s in range(2)
        ],
        axis=0,
    )
    place = nbr_ref[...].T[:, :1] - rows
    pick = one_hot((place & 1) * owners + (place >> 1), 2 * owners)
    scale = (1.0 - ALPHA) * ew_ref[...].T[:, :1]
    high, low = split(halo)
    top = lax.broadcasted_iota(jnp.int32, (step // 16, 2, 8, 128), 2) < 4
    for start in range(0, rows, block):
        whole = slice(start, start + block)
        work_ref[whole, :] = dot(pick[whole], high) + dot(pick[whole], low)
        for first in range(start, start + block, step):
            at = slice(first, first + step)
            z = part_ref[at, :] + scale[at] * work_ref[at, :]
            zs = split(z)
            work_ref[at, :] = z
            zhigh_ref[at, :] = zs[0]
            zlow_ref[at, :] = zs[1]
    weights = whigh_ref[...], wlow_ref[...]
    for start in range(0, rows, block):
        whole = slice(start, start + block)
        mixed = dot3((zhigh_ref[whole, :], zlow_ref[whole, :]), weights)
        work_ref[whole, :] = (1.0 - BETA) * work_ref[whole, :] + BETA * mixed
        for first in range(start, start + block, step):
            at = slice(first, first + step)
            u = work_ref[at, :]
            square = u * u
            bent = jnp.tanh(GELU_C * (u + GELU_A * (square * u)))
            embed = (0.5 * u) * (1.0 + bent)
            slope = 0.5 * (1.0 + bent) + (0.5 * u) * (1.0 - bent * bent) * (
                GELU_C * (1.0 + (3.0 * GELU_A) * square)
            )
            du = cot_ref[at, :] * slope
            du_ref[at, :] = du
            ds = split(du)
            dhigh_ref[at, :] = ds[0]
            dlow_ref[at, :] = ds[1]
            group = slice(first // 16, (first + step) // 16)
            for pair in range(2):
                x, y = (
                    embed[:, l * 128 : (l + 1) * 128].reshape(step // 16, 2, 8, 128)
                    for l in (2 * pair, 2 * pair + 1)
                )
                even = jnp.where(top, x, pltpu.roll(y, 4, 2))
                odd = jnp.where(top, pltpu.roll(x, 4, 2), y)
                for h in range(2):
                    out_ref[group, 2 * h, 8 * pair : 8 * pair + 8, :] = even[:, h]
                    out_ref[group, 2 * h + 1, 8 * pair : 8 * pair + 8, :] = odd[:, h]
    out_ref.push()
    du_ref.push()
    term_ref[...] = dot3(
        (zhigh_ref[...], zlow_ref[...]), (dhigh_ref[...], dlow_ref[...]), 0, 0
    )
    half = term_ref.shape[0] // 2
    core = core_ref[0]
    keep_ref[...] = term_ref[pl.ds(pl.multiple_of(core * half, half), half), :]
    give_ref[...] = term_ref[pl.ds(pl.multiple_of((1 - core) * half, half), half), :]


def scatter_kernel(me_ref, *refs):
    terms, outs, total_ref = refs[: -1 - 4], refs[-1 - 4 : -1], refs[-1]
    total_ref[...] = functools.reduce(lambda x, y: x + y, [t[...] for t in terms])
    size = outs[0].shape[0]
    for shift, out in enumerate(outs):
        at = jnp.bitwise_xor(me_ref[0], shift) * size
        out[...] = total_ref[pl.ds(pl.multiple_of(at, size), size), :]


def total_kernel(*refs):
    terms = [t[...] for t in refs[:-1]]
    while len(terms) > 1:
        terms = [x + y for x, y in zip(terms[::2], terms[1::2])]
    refs[-1][...] = terms[0]


def spread_kernel(mine_ref, other_ref, out_ref):
    out_ref[...] = jnp.broadcast_to((mine_ref[...] + other_ref[...])[None], out_ref.shape)


def assemble_kernel(core_ref, mine_ref, other_ref, out_ref, *, scale):
    half = out_ref.shape[0] // 2
    size = mine_ref.shape[1]
    for ref, which in ((mine_ref, core_ref[0]), (other_ref, 1 - core_ref[0])):
        for y in range(4):
            for x in range(4):
                at = which * half + (x * 4 + y) * size
                out_ref[pl.ds(pl.multiple_of(at, size), size), :] = ref[y * 4 + x] * scale


def backward_kernel(du_ref, weight_ref, high_ref, low_ref, out_ref):
    du = du_ref[...]
    dz = (1.0 - BETA) * du + BETA * dot3(split(du), split(weight_ref[...]), 1, 1)
    out_ref[...] = (1.0 - ALPHA) * dot3((high_ref[...], low_ref[...]), split(dz), 0, 0)
    out_ref.push()


def history_kernel(which_ref, dest_ref, recv_ref, base_ref, out_ref, high_ref, low_ref):
    owners = recv_ref.shape[0] // 16
    for s in range(4):
        for l in range(4):
            high, low = split(recv_ref[pl.ds(4 * l + s, owners, stride=16), :])
            at = slice(s * owners, (s + 1) * owners)
            high_ref[at, l * 128 : (l + 1) * 128] = high
            low_ref[at, l * 128 : (l + 1) * 128] = low
    dest = dest_ref[pl.ds(which_ref[0], 1), :]
    step = out_ref.rows
    for block in range(out_ref.shape[0] // step):
        ids = lax.broadcasted_iota(jnp.int32, (step, dest.shape[1]), 0) + block * step
        hit = jnp.where(ids == dest, 1.0, 0.0)
        count = jnp.sum(hit, axis=1, keepdims=True)
        place = hit.astype(BF16)
        written = dot(place, high_ref[...]) + dot(place, low_ref[...])
        at = slice(block * step, (block + 1) * step)
        base_ref.part(block)
        out_ref[at, :] = jnp.where(count > 0.5, written, base_ref.buffer[at, :])
        out_ref.push(block)


def write_rows(which, dest, recv, base):
    rows, width = dest.shape[1], base.shape[1]
    return call(
        history_kernel,
        [(base.shape, F32)],
        (which, dest, recv, base),
        spaces="svvhh",
        scratch=[pltpu.VMEM((rows, width), BF16), pltpu.VMEM((rows, width), BF16)],
        limit=52,
        flops=2 * 10**9,
        rows=256,
    )[0]


def exchange(v, axes=OWN):
    return lax.all_to_all(v, axes, split_axis=0, concat_axis=0, tiled=True)


def swap(v):
    return lax.ppermute(v, "rep", [(0, 1), (1, 0)])


def move(v, axis, mask):
    count = lax.axis_size(axis)
    return lax.ppermute(v, axis, [(i, i ^ mask) for i in range(count)])


def scatter(me, *terms):
    size = terms[0].shape[0] // 4
    return call(
        scatter_kernel,
        [((size, terms[0].shape[1]), F32)] * 4,
        (me,) + terms,
        spaces="s" + "v" * (len(terms) + 4),
        scratch=[pltpu.VMEM(terms[0].shape, F32)],
    )


def trade(pieces, axis):
    return [pieces[0]] + [move(pieces[shift], axis, shift) for shift in (1, 2, 3)]


def total(*terms):
    return call(total_kernel, [(terms[0].shape, F32)], terms)[0]


def together(*values):
    return lax.optimization_barrier(values)


def body(
    node_input,
    initial,
    cotangent,
    weight,
    edge_weight,
    neighbors,
    halo_rows,
    cold_history,
    hot_history,
    dest_rows,
):
    rows, width = node_input.shape
    owners = lax.axis_size(OWN)
    halo_count = owners * halo_rows.shape[2]
    core = lax.axis_index("rep").astype(jnp.int32).reshape(1)
    at_x = lax.axis_index("hist").astype(jnp.int32).reshape(1)
    at_y = lax.axis_index("y").astype(jnp.int32).reshape(1)
    full = (rows, width)
    half = (rows // 2, width)
    nbr = neighbors.T
    ew = edge_weight.T
    dest = jnp.transpose(dest_rows.reshape(2, owners, 4), (0, 2, 1)).reshape(2, rows)

    wanted = exchange(halo_rows[0])
    (found,) = call(
        gather_kernel,
        [((halo_count * 4, 128), F32)],
        (wanted, cold_history),
        spaces="vhv",
        rows=256,
        limit=60,
        flops=10**9,
    )
    halo = exchange(found)
    square = ((width, width), BF16)
    part, high, low, *weights = call(
        functools.partial(prepare_kernel, halo_count=halo_count),
        [(full, F32), ((rows, rows), BF16), ((rows, rows), BF16), square, square],
        (core, nbr, ew, hot_history, swap(hot_history), node_input, initial, weight),
        spaces="svvhhhhhhhhhh",
        limit=60,
        flops=6 * 10**9,
    )
    halo, part = together(halo, part)
    outgoing, keep, give, du = call(
        layer_kernel,
        [((owners // 4, 4, 16, 128), F32), (half, F32), (half, F32), (full, F32)],
        (core, halo, nbr, ew, part, *weights, cotangent),
        spaces="svvvhhhhhvvh",
        scratch=[pltpu.VMEM((width, width), F32), pltpu.VMEM(full, F32)]
        + [pltpu.VMEM(full, BF16)] * 4,
        limit=52,
        flops=3 * 10**9,
    )
    got, dest = together(swap(give), dest)
    pieces = trade(scatter(at_x, keep, got), "hist")
    (grad_input,) = call(
        backward_kernel,
        [(full, F32)],
        (du, weight, high, low),
        spaces="hhhhh",
        limit=60,
        flops=2 * 10**9,
    )
    *pieces, grad_input = together(*pieces, grad_input)
    pieces = trade(scatter(at_y, *pieces), "y")
    arrived = exchange(outgoing.reshape(owners * 16, 128))
    summed = total(*pieces)
    mask = 1
    while 2 * mask < lax.axis_size("z"):
        summed = total(summed, move(summed, "z", mask))
        mask *= 2
    plane = lax.axis_size(PLANE)
    (spread,) = call(
        spread_kernel, [((plane,) + summed.shape, F32)], (summed, move(summed, "z", mask))
    )
    arrived, spread = together(arrived, spread)
    arrived_other = swap(arrived)
    gathered = exchange(spread, PLANE)
    history = write_rows(core, dest, arrived, cold_history)
    history = write_rows(1 - core, dest, arrived_other, history)
    gathered, history = together(gathered, history)
    all_nodes = rows * lax.axis_size(ALL)
    (grad_weight,) = call(
        functools.partial(assemble_kernel, scale=BETA / math.sqrt(all_nodes)),
        [((width, width), F32)],
        (core, gathered, swap(gathered)),
        spaces="svvv",
    )
    return (grad_weight, grad_input, history)


def solution(mesh):
    batch, hist, rep = mesh.devices.shape
    mesh = Mesh(mesh.devices.reshape(4, batch // 4, hist, rep), ALL)
    return jax.shard_map(
        body,
        mesh=mesh,
        in_specs=(
            P(ALL, None),
            P(ALL, None),
            P(ALL, None),
            P(),
            P(ALL, None),
            P(ALL, None),
            P(ALL, None, None),
            P(OWN, None),
            P("rep", None),
            P(OWN, None),
        ),
        out_specs=(P(), P(ALL, None), P(OWN, None)),
        check_vma=False,
    )
```

```python
import functools
import math

import jax
import jax.numpy as jnp
from jax import lax
from jax.experimental import pallas as pl
from jax.experimental.pallas import tpu as pltpu
from jax.sharding import Mesh
from jax.sharding import PartitionSpec as P

ALPHA = 0.1
BETA = math.log(1.5)
OWN = ("y", "z", "hist")
PLANE = ("y", "hist")
ALL = ("y", "z", "hist", "rep")
F32 = jnp.float32
BF16 = jnp.bfloat16
GELU_C = math.sqrt(2.0 / math.pi)
GELU_A = 0.044715
VMEM = pl.BlockSpec(memory_space=pltpu.VMEM)
SMEM = pl.BlockSpec(memory_space=pltpu.SMEM)
HBM = pl.BlockSpec(memory_space=pltpu.HBM)
MIB = 1 << 20


def dot(a, b, left=1, right=0):
    return lax.dot_general(a, b, (((left,), (right,)), ((), ())), preferred_element_type=F32)


def split(v):
    high = v.astype(BF16)
    return high, (v - high.astype(F32)).astype(BF16)


def dot3(a, b, left=1, right=0):
    return dot(a[0], b[0], left, right) + (dot(a[0], b[1], left, right) + dot(a[1], b[0], left, right))


def lanes(rows, columns):
    return lax.broadcasted_iota(jnp.int32, (rows, columns), 1)


def one_hot(column, count):
    return (column == lanes(column.shape[0], count)).astype(BF16)


class Source:
    def __init__(self, ref, buffer, sem, chunks=1):
        rows = ref.shape[0] // chunks
        self.buffer, self.copies, self.shape = buffer, [], ref.shape
        for i in range(chunks):
            at = (pl.ds(i * rows, rows),) + (slice(None),) * (len(ref.shape) - 1)
            copy = pltpu.make_async_copy(ref.at[at], buffer.at[at], sem.at[i])
            copy.start()
            self.copies.append(copy)

    def __getitem__(self, index):
        for i in range(len(self.copies)):
            self.part(i)
        return self.buffer[index]

    def part(self, i):
        if self.copies[i] is not None:
            self.copies[i].wait()
        self.copies[i] = None


class Sink:
    def __init__(self, ref, buffer, sem, chunks=1):
        self.ref, self.buffer, self.sem = ref, buffer, sem
        self.rows, self.copies = ref.shape[0] // chunks, []
        self.shape = ref.shape

    def __setitem__(self, index, value):
        self.buffer[index] = value

    def push(self, i=0):
        at = (pl.ds(i * self.rows, self.rows),) + (slice(None),) * (len(self.shape) - 1)
        copy = pltpu.make_async_copy(self.buffer.at[at], self.ref.at[at], self.sem.at[i])
        copy.start()
        self.copies.append(copy)


def call(kernel, outs, args, spaces=None, scratch=(), limit=8, flops=0, chunks=1):
    spaces = spaces or "v" * (len(args) + len(outs))
    shapes = [(a.shape, a.dtype) for a in args] + list(outs)
    where = {"s": SMEM, "v": VMEM, "h": HBM}
    remote = [i for i, space in enumerate(spaces) if space == "h"]
    buffers = [pltpu.VMEM(*shapes[i]) for i in remote]
    sems = [pltpu.SemaphoreType.DMA((chunks,)) for _ in remote]

    def wrapped(*refs):
        refs, rest = list(refs[: len(shapes)]), refs[len(shapes) :]
        sinks = []
        for n, i in enumerate(remote):
            kind = Source if i < len(args) else Sink
            refs[i] = kind(refs[i], rest[n], rest[len(remote) + n], chunks)
            if kind is Sink:
                sinks.append(refs[i])
        kernel(*refs, *rest[2 * len(remote) :])
        for sink in sinks:
            for copy in sink.copies:
                copy.wait()

    count = sum(math.prod(shape) * 4 for shape, _ in shapes)
    return pl.pallas_call(
        wrapped,
        out_shape=[jax.ShapeDtypeStruct(*o) for o in outs],
        in_specs=[where[c] for c in spaces[: len(args)]],
        out_specs=[where[c] for c in spaces[len(args) :]],
        scratch_shapes=buffers + sems + list(scratch),
        compiler_params=pltpu.CompilerParams(vmem_limit_bytes=limit * MIB),
        cost_estimate=pl.CostEstimate(flops=flops, bytes_accessed=count, transcendentals=0),
    )(*args)


def gather_kernel(idx_ref, cold_ref, out_ref):
    owners, per = idx_ref.shape
    high, low = split(cold_ref[...])
    pick = jnp.concatenate(
        [one_hot(idx_ref[:, s : s + 1], cold_ref.shape[0]) for s in range(per)], axis=0
    )
    found = dot(pick, high) + dot(pick, low)
    for s in range(per):
        for l in range(4):
            out_ref[pl.ds(s * 4 + l, owners, stride=per * 4), :] = found[
                s * owners : (s + 1) * owners, l * 128 : (l + 1) * 128
            ]


def prepare_kernel(
    core_ref, nbr_ref, ew_ref, mine_ref, other_ref, node_ref, init_ref,
    part_ref, high_ref, low_ref, *, halo_count,
):
    rows = node_ref.shape[0]
    half = mine_ref.shape[0]
    core = core_ref[0]
    nbr = nbr_ref[...].T
    ew = ew_ref[...].T
    ids = lanes(rows, rows)
    tile = jnp.zeros((rows, rows), F32)
    for k in range(2, nbr.shape[1]):
        tile = tile + jnp.where(nbr[:, k : k + 1] == ids, ew[:, k : k + 1], 0.0)
    tiles = split(tile)
    high_ref[...] = tiles[0]
    low_ref[...] = tiles[1]
    high_ref.push()
    low_ref.push()
    hot = nbr[:, 1:2] - (rows + halo_count)
    picked = jnp.zeros((rows, node_ref.shape[1]), F32)
    for ref, base in ((mine_ref, core * half), (other_ref, (1 - core) * half)):
        choose = one_hot(hot - base, half)
        for piece in split(ref[...]):
            picked = picked + dot(choose, piece)
    agg = dot3(tiles, split(node_ref[...])) + ew[:, 1:2] * picked
    part_ref[...] = (1.0 - ALPHA) * agg + ALPHA * init_ref[...]
    part_ref.push()


def layer_kernel(
    core_ref, halo_ref, nbr_ref, ew_ref, part_ref, weight_ref, cot_ref,
    out_ref, keep_ref, give_ref, du_ref,
    term_ref, work_ref, zhigh_ref, zlow_ref, dhigh_ref, dlow_ref,
):
    owners = halo_ref.shape[0] // 8
    rows = part_ref.shape[0]
    block, step = rows // 4, 32
    halo = jnp.concatenate(
        [
            jnp.concatenate(
                [halo_ref[pl.ds(s * 4 + l, owners, stride=8), :] for l in range(4)], axis=1
            )
            for s in range(2)
        ],
        axis=0,
    )
    place = nbr_ref[...].T[:, :1] - rows
    pick = one_hot((place & 1) * owners + (place >> 1), 2 * owners)
    scale = (1.0 - ALPHA) * ew_ref[...].T[:, :1]
    high, low = split(halo)
    top = lax.broadcasted_iota(jnp.int32, (step // 16, 2, 8, 128), 2) < 4
    for start in range(0, rows, block):
        whole = slice(start, start + block)
        work_ref[whole, :] = dot(pick[whole], high) + dot(pick[whole], low)
        part_ref.part(start // block)
        for first in range(start, start + block, step):
            at = slice(first, first + step)
            z = part_ref.buffer[at, :] + scale[at] * work_ref[at, :]
            zs = split(z)
            work_ref[at, :] = z
            zhigh_ref[at, :] = zs[0]
            zlow_ref[at, :] = zs[1]
    weights = split(weight_ref[...])
    for start in range(0, rows, block):
        whole = slice(start, start + block)
        mixed = dot3((zhigh_ref[whole, :], zlow_ref[whole, :]), weights)
        work_ref[whole, :] = (1.0 - BETA) * work_ref[whole, :] + BETA * mixed
        cot_ref.part(start // block)
        for first in range(start, start + block, step):
            at = slice(first, first + step)
            u = work_ref[at, :]
            square = u * u
            bent = jnp.tanh(GELU_C * (u + GELU_A * (square * u)))
            embed = (0.5 * u) * (1.0 + bent)
            slope = 0.5 * (1.0 + bent) + (0.5 * u) * (1.0 - bent * bent) * (
                GELU_C * (1.0 + (3.0 * GELU_A) * square)
            )
            du = cot_ref.buffer[at, :] * slope
            du_ref[at, :] = du
            ds = split(du)
            dhigh_ref[at, :] = ds[0]
            dlow_ref[at, :] = ds[1]
            group = slice(first // 16, (first + step) // 16)
            for pair in range(2):
                x, y = (
                    embed[:, l * 128 : (l + 1) * 128].reshape(step // 16, 2, 8, 128)
                    for l in (2 * pair, 2 * pair + 1)
                )
                even = jnp.where(top, x, pltpu.roll(y, 4, 2))
                odd = jnp.where(top, pltpu.roll(x, 4, 2), y)
                for h in range(2):
                    out_ref[group, 2 * h, 8 * pair : 8 * pair + 8, :] = even[:, h]
                    out_ref[group, 2 * h + 1, 8 * pair : 8 * pair + 8, :] = odd[:, h]
        out_ref.push(start // block)
        du_ref.push(start // block)
    term_ref[...] = dot3(
        (zhigh_ref[...], zlow_ref[...]), (dhigh_ref[...], dlow_ref[...]), 0, 0
    )
    half = term_ref.shape[0] // 2
    core = core_ref[0]
    keep_ref[...] = term_ref[pl.ds(pl.multiple_of(core * half, half), half), :]
    give_ref[...] = term_ref[pl.ds(pl.multiple_of((1 - core) * half, half), half), :]


def scatter_kernel(me_ref, *refs):
    terms, outs, total_ref = refs[: -1 - 4], refs[-1 - 4 : -1], refs[-1]
    total_ref[...] = functools.reduce(lambda x, y: x + y, [t[...] for t in terms])
    size = outs[0].shape[0]
    for shift, out in enumerate(outs):
        at = jnp.bitwise_xor(me_ref[0], shift) * size
        out[...] = total_ref[pl.ds(pl.multiple_of(at, size), size), :]


def total_kernel(*refs):
    terms = [t[...] for t in refs[:-1]]
    while len(terms) > 1:
        terms = [x + y for x, y in zip(terms[::2], terms[1::2])]
    refs[-1][...] = terms[0]


def spread_kernel(mine_ref, other_ref, out_ref):
    out_ref[...] = jnp.broadcast_to((mine_ref[...] + other_ref[...])[None], out_ref.shape)


def assemble_kernel(core_ref, mine_ref, other_ref, out_ref, *, scale):
    half = out_ref.shape[0] // 2
    size = mine_ref.shape[1]
    for ref, which in ((mine_ref, core_ref[0]), (other_ref, 1 - core_ref[0])):
        for y in range(4):
            for x in range(4):
                at = which * half + (x * 4 + y) * size
                out_ref[pl.ds(pl.multiple_of(at, size), size), :] = ref[y * 4 + x] * scale


def backward_kernel(du_ref, weight_ref, high_ref, low_ref, out_ref):
    du = du_ref[...]
    dz = (1.0 - BETA) * du + BETA * dot3(split(du), split(weight_ref[...]), 1, 1)
    out_ref[...] = (1.0 - ALPHA) * dot3((high_ref[...], low_ref[...]), split(dz), 0, 0)
    out_ref.push()


def history_kernel(which_ref, dest_ref, recv_ref, base_ref, out_ref, high_ref, low_ref):
    owners = recv_ref.shape[0] // 16
    for s in range(4):
        for l in range(4):
            high, low = split(recv_ref[pl.ds(4 * l + s, owners, stride=16), :])
            at = slice(s * owners, (s + 1) * owners)
            high_ref[at, l * 128 : (l + 1) * 128] = high
            low_ref[at, l * 128 : (l + 1) * 128] = low
    dest = dest_ref[pl.ds(which_ref[0], 1), :]
    step = out_ref.rows
    for block in range(out_ref.shape[0] // step):
        ids = lax.broadcasted_iota(jnp.int32, (step, dest.shape[1]), 0) + block * step
        hit = jnp.where(ids == dest, 1.0, 0.0)
        count = jnp.sum(hit, axis=1, keepdims=True)
        place = hit.astype(BF16)
        written = dot(place, high_ref[...]) + dot(place, low_ref[...])
        at = slice(block * step, (block + 1) * step)
        base_ref.part(block)
        out_ref[at, :] = jnp.where(count > 0.5, written, base_ref.buffer[at, :])
        out_ref.push(block)


def write_rows(which, dest, recv, base):
    rows, width = dest.shape[1], base.shape[1]
    return call(
        history_kernel,
        [(base.shape, F32)],
        (which, dest, recv, base),
        spaces="svvhh",
        scratch=[pltpu.VMEM((rows, width), BF16), pltpu.VMEM((rows, width), BF16)],
        limit=52,
        flops=2 * 10**9,
        chunks=5,
    )[0]


def exchange(v, axes=OWN):
    return lax.all_to_all(v, axes, split_axis=0, concat_axis=0, tiled=True)


def swap(v):
    return lax.ppermute(v, "rep", [(0, 1), (1, 0)])


def move(v, axis, mask):
    count = lax.axis_size(axis)
    return lax.ppermute(v, axis, [(i, i ^ mask) for i in range(count)])


def scatter(me, *terms):
    size = terms[0].shape[0] // 4
    return call(
        scatter_kernel,
        [((size, terms[0].shape[1]), F32)] * 4,
        (me,) + terms,
        spaces="s" + "v" * (len(terms) + 4),
        scratch=[pltpu.VMEM(terms[0].shape, F32)],
    )


def trade(pieces, axis):
    return [pieces[0]] + [move(pieces[shift], axis, shift) for shift in (1, 2, 3)]


def total(*terms):
    return call(total_kernel, [(terms[0].shape, F32)], terms)[0]


def together(*values):
    return lax.optimization_barrier(values)


def body(
    node_input,
    initial,
    cotangent,
    weight,
    edge_weight,
    neighbors,
    halo_rows,
    cold_history,
    hot_history,
    dest_rows,
):
    rows, width = node_input.shape
    owners = lax.axis_size(OWN)
    halo_count = owners * halo_rows.shape[2]
    core = lax.axis_index("rep").astype(jnp.int32).reshape(1)
    at_x = lax.axis_index("hist").astype(jnp.int32).reshape(1)
    at_y = lax.axis_index("y").astype(jnp.int32).reshape(1)
    full = (rows, width)
    half = (rows // 2, width)
    nbr = neighbors.T
    ew = edge_weight.T
    dest = jnp.transpose(dest_rows.reshape(2, owners, 4), (0, 2, 1)).reshape(2, rows)

    wanted = exchange(halo_rows[0])
    (found,) = call(
        gather_kernel,
        [((halo_count * 4, 128), F32)],
        (wanted, cold_history),
        limit=16,
        flops=10**9,
    )
    halo = exchange(found)
    part, high, low = call(
        functools.partial(prepare_kernel, halo_count=halo_count),
        [(full, F32), ((rows, rows), BF16), ((rows, rows), BF16)],
        (core, nbr, ew, hot_history, swap(hot_history), node_input, initial),
        spaces="svvhhhhhhh",
        limit=60,
        flops=6 * 10**9,
    )
    halo, part = together(halo, part)
    outgoing, keep, give, du = call(
        layer_kernel,
        [((owners // 4, 4, 16, 128), F32), (half, F32), (half, F32), (full, F32)],
        (core, halo, nbr, ew, part, weight, cotangent),
        spaces="svvvhhhhvvh",
        chunks=4,
        scratch=[pltpu.VMEM((width, width), F32), pltpu.VMEM(full, F32)]
        + [pltpu.VMEM(full, BF16)] * 4,
        limit=52,
        flops=3 * 10**9,
    )
    got, dest = together(swap(give), dest)
    pieces = trade(scatter(at_x, keep, got), "hist")
    (grad_input,) = call(
        backward_kernel,
        [(full, F32)],
        (du, weight, high, low),
        spaces="hhhhh",
        limit=60,
        flops=2 * 10**9,
    )
    *pieces, grad_input = together(*pieces, grad_input)
    pieces = trade(scatter(at_y, *pieces), "y")
    arrived = exchange(outgoing.reshape(owners * 16, 128))
    summed = total(*pieces)
    mask = 1
    while 2 * mask < lax.axis_size("z"):
        summed = total(summed, move(summed, "z", mask))
        mask *= 2
    plane = lax.axis_size(PLANE)
    (spread,) = call(
        spread_kernel, [((plane,) + summed.shape, F32)], (summed, move(summed, "z", mask))
    )
    arrived, spread = together(arrived, spread)
    arrived_other = swap(arrived)
    gathered = exchange(spread, PLANE)
    history = write_rows(core, dest, arrived, cold_history)
    history = write_rows(1 - core, dest, arrived_other, history)
    gathered, history = together(gathered, history)
    all_nodes = rows * lax.axis_size(ALL)
    (grad_weight,) = call(
        functools.partial(assemble_kernel, scale=BETA / math.sqrt(all_nodes)),
        [((width, width), F32)],
        (core, gathered, swap(gathered)),
        spaces="svvv",
    )
    return (grad_weight, grad_input, history)


def solution(mesh):
    batch, hist, rep = mesh.devices.shape
    mesh = Mesh(mesh.devices.reshape(4, batch // 4, hist, rep), ALL)
    return jax.shard_map(
        body,
        mesh=mesh,
        in_specs=(
            P(ALL, None),
            P(ALL, None),
            P(ALL, None),
            P(),
            P(ALL, None),
            P(ALL, None),
            P(ALL, None, None),
            P(OWN, None),
            P("rep", None),
            P(OWN, None),
        ),
        out_specs=(P(), P(ALL, None), P(OWN, None)),
        check_vma=False,
    )
```

```python
import functools
import math

import jax
import jax.numpy as jnp
from jax import lax
from jax.experimental import pallas as pl
from jax.experimental.pallas import tpu as pltpu
from jax.sharding import Mesh
from jax.sharding import PartitionSpec as P

ALPHA = 0.1
BETA = math.log(1.5)
OWN = ("y", "z", "hist")
PLANE = ("y", "hist")
ALL = ("y", "z", "hist", "rep")
F32 = jnp.float32
BF16 = jnp.bfloat16
GELU_C = math.sqrt(2.0 / math.pi)
GELU_A = 0.044715
VMEM = pl.BlockSpec(memory_space=pltpu.VMEM)
SMEM = pl.BlockSpec(memory_space=pltpu.SMEM)
HBM = pl.BlockSpec(memory_space=pltpu.HBM)
MIB = 1 << 20


def dot(a, b, left=1, right=0):
    return lax.dot_general(a, b, (((left,), (right,)), ((), ())), preferred_element_type=F32)


def split(v):
    high = v.astype(BF16)
    return high, (v - high.astype(F32)).astype(BF16)


def dot3(a, b, left=1, right=0):
    return dot(a[0], b[0], left, right) + (dot(a[0], b[1], left, right) + dot(a[1], b[0], left, right))


def lanes(rows, columns):
    return lax.broadcasted_iota(jnp.int32, (rows, columns), 1)


def one_hot(column, count):
    return (column == lanes(column.shape[0], count)).astype(BF16)


class Source:
    def __init__(self, ref, buffer, sem, chunks=1):
        rows = ref.shape[0] // chunks
        self.buffer, self.copies, self.shape = buffer, [], ref.shape
        for i in range(chunks):
            at = (pl.ds(i * rows, rows),) + (slice(None),) * (len(ref.shape) - 1)
            copy = pltpu.make_async_copy(ref.at[at], buffer.at[at], sem.at[i])
            copy.start()
            self.copies.append(copy)

    def __getitem__(self, index):
        for i in range(len(self.copies)):
            self.part(i)
        return self.buffer[index]

    def part(self, i):
        if self.copies[i] is not None:
            self.copies[i].wait()
        self.copies[i] = None


class Sink:
    def __init__(self, ref, buffer, sem, chunks=1):
        self.ref, self.buffer, self.sem = ref, buffer, sem
        self.rows, self.copies = ref.shape[0] // chunks, []
        self.shape = ref.shape

    def __setitem__(self, index, value):
        self.buffer[index] = value

    def push(self, i=0):
        at = (pl.ds(i * self.rows, self.rows),) + (slice(None),) * (len(self.shape) - 1)
        copy = pltpu.make_async_copy(self.buffer.at[at], self.ref.at[at], self.sem.at[i])
        copy.start()
        self.copies.append(copy)


def call(kernel, outs, args, spaces=None, scratch=(), limit=8, flops=0, chunks=1):
    spaces = spaces or "v" * (len(args) + len(outs))
    shapes = [(a.shape, a.dtype) for a in args] + list(outs)
    where = {"s": SMEM, "v": VMEM, "h": HBM}
    remote = [i for i, space in enumerate(spaces) if space == "h"]
    buffers = [pltpu.VMEM(*shapes[i]) for i in remote]
    sems = [pltpu.SemaphoreType.DMA((chunks,)) for _ in remote]

    def wrapped(*refs):
        refs, rest = list(refs[: len(shapes)]), refs[len(shapes) :]
        sinks = []
        for n, i in enumerate(remote):
            kind = Source if i < len(args) else Sink
            refs[i] = kind(refs[i], rest[n], rest[len(remote) + n], chunks)
            if kind is Sink:
                sinks.append(refs[i])
        kernel(*refs, *rest[2 * len(remote) :])
        for sink in sinks:
            for copy in sink.copies:
                copy.wait()

    count = sum(math.prod(shape) * 4 for shape, _ in shapes)
    return pl.pallas_call(
        wrapped,
        out_shape=[jax.ShapeDtypeStruct(*o) for o in outs],
        in_specs=[where[c] for c in spaces[: len(args)]],
        out_specs=[where[c] for c in spaces[len(args) :]],
        scratch_shapes=buffers + sems + list(scratch),
        compiler_params=pltpu.CompilerParams(vmem_limit_bytes=limit * MIB),
        cost_estimate=pl.CostEstimate(flops=flops, bytes_accessed=count, transcendentals=0),
    )(*args)


def gather_kernel(idx_ref, cold_ref, out_ref):
    owners, per = idx_ref.shape
    high, low = split(cold_ref[...])
    pick = jnp.concatenate(
        [one_hot(idx_ref[:, s : s + 1], cold_ref.shape[0]) for s in range(per)], axis=0
    )
    found = dot(pick, high) + dot(pick, low)
    for s in range(per):
        for l in range(4):
            out_ref[pl.ds(s * 4 + l, owners, stride=per * 4), :] = found[
                s * owners : (s + 1) * owners, l * 128 : (l + 1) * 128
            ]


def prepare_kernel(
    core_ref, nbr_ref, ew_ref, mine_ref, other_ref, node_ref, init_ref,
    part_ref, high_ref, low_ref, *, halo_count,
):
    rows = node_ref.shape[0]
    half = mine_ref.shape[0]
    core = core_ref[0]
    nbr = nbr_ref[...].T
    ew = ew_ref[...].T
    ids = lanes(rows, rows)
    tile = jnp.zeros((rows, rows), F32)
    for k in range(2, nbr.shape[1]):
        tile = tile + jnp.where(nbr[:, k : k + 1] == ids, ew[:, k : k + 1], 0.0)
    tiles = split(tile)
    high_ref[...] = tiles[0]
    low_ref[...] = tiles[1]
    high_ref.push()
    low_ref.push()
    hot = nbr[:, 1:2] - (rows + halo_count)
    picked = jnp.zeros((rows, node_ref.shape[1]), F32)
    for ref, base in ((mine_ref, core * half), (other_ref, (1 - core) * half)):
        choose = one_hot(hot - base, half)
        for piece in split(ref[...]):
            picked = picked + dot(choose, piece)
    agg = dot3(tiles, split(node_ref[...])) + ew[:, 1:2] * picked
    part_ref[...] = (1.0 - ALPHA) * agg + ALPHA * init_ref[...]
    part_ref.push()


def layer_kernel(
    core_ref, halo_ref, nbr_ref, ew_ref, part_ref, weight_ref, cot_ref,
    out_ref, keep_ref, give_ref, du_ref,
    term_ref, work_ref, zhigh_ref, zlow_ref, dhigh_ref, dlow_ref,
):
    owners = halo_ref.shape[0] // 8
    rows = part_ref.shape[0]
    block, step = rows // 4, 32
    halo = jnp.concatenate(
        [
            jnp.concatenate(
                [halo_ref[pl.ds(s * 4 + l, owners, stride=8), :] for l in range(4)], axis=1
            )
            for s in range(2)
        ],
        axis=0,
    )
    place = nbr_ref[...].T[:, :1] - rows
    pick = one_hot((place & 1) * owners + (place >> 1), 2 * owners)
    scale = (1.0 - ALPHA) * ew_ref[...].T[:, :1]
    high, low = split(halo)
    top = lax.broadcasted_iota(jnp.int32, (step // 16, 2, 8, 128), 2) < 4
    for start in range(0, rows, block):
        whole = slice(start, start + block)
        work_ref[whole, :] = dot(pick[whole], high) + dot(pick[whole], low)
        part_ref.part(start // block)
        for first in range(start, start + block, step):
            at = slice(first, first + step)
            z = part_ref.buffer[at, :] + scale[at] * work_ref[at, :]
            zs = split(z)
            work_ref[at, :] = z
            zhigh_ref[at, :] = zs[0]
            zlow_ref[at, :] = zs[1]
    weights = split(weight_ref[...])
    for start in range(0, rows, block):
        whole = slice(start, start + block)
        mixed = dot3((zhigh_ref[whole, :], zlow_ref[whole, :]), weights)
        work_ref[whole, :] = (1.0 - BETA) * work_ref[whole, :] + BETA * mixed
        cot_ref.part(start // block)
        for first in range(start, start + block, step):
            at = slice(first, first + step)
            u = work_ref[at, :]
            square = u * u
            bent = jnp.tanh(GELU_C * (u + GELU_A * (square * u)))
            embed = (0.5 * u) * (1.0 + bent)
            slope = 0.5 * (1.0 + bent) + (0.5 * u) * (1.0 - bent * bent) * (
                GELU_C * (1.0 + (3.0 * GELU_A) * square)
            )
            du = cot_ref.buffer[at, :] * slope
            du_ref[at, :] = du
            ds = split(du)
            dhigh_ref[at, :] = ds[0]
            dlow_ref[at, :] = ds[1]
            group = slice(first // 16, (first + step) // 16)
            for pair in range(2):
                x, y = (
                    embed[:, l * 128 : (l + 1) * 128].reshape(step // 16, 2, 8, 128)
                    for l in (2 * pair, 2 * pair + 1)
                )
                even = jnp.where(top, x, pltpu.roll(y, 4, 2))
                odd = jnp.where(top, pltpu.roll(x, 4, 2), y)
                for h in range(2):
                    out_ref[group, 2 * h, 8 * pair : 8 * pair + 8, :] = even[:, h]
                    out_ref[group, 2 * h + 1, 8 * pair : 8 * pair + 8, :] = odd[:, h]
        out_ref.push(start // block)
        du_ref.push(start // block)
    term_ref[...] = dot3(
        (zhigh_ref[...], zlow_ref[...]), (dhigh_ref[...], dlow_ref[...]), 0, 0
    )
    half = term_ref.shape[0] // 2
    core = core_ref[0]
    keep_ref[...] = term_ref[pl.ds(pl.multiple_of(core * half, half), half), :]
    give_ref[...] = term_ref[pl.ds(pl.multiple_of((1 - core) * half, half), half), :]


def scatter_kernel(me_ref, *refs):
    terms, outs, total_ref = refs[: -1 - 4], refs[-1 - 4 : -1], refs[-1]
    total_ref[...] = functools.reduce(lambda x, y: x + y, [t[...] for t in terms])
    size = outs[0].shape[0]
    for shift, out in enumerate(outs):
        at = jnp.bitwise_xor(me_ref[0], shift) * size
        out[...] = total_ref[pl.ds(pl.multiple_of(at, size), size), :]


def total_kernel(*refs):
    terms = [t[...] for t in refs[:-1]]
    while len(terms) > 1:
        terms = [x + y for x, y in zip(terms[::2], terms[1::2])]
    refs[-1][...] = terms[0]


def spread_kernel(mine_ref, other_ref, out_ref):
    out_ref[...] = jnp.broadcast_to((mine_ref[...] + other_ref[...])[None], out_ref.shape)


def assemble_kernel(core_ref, mine_ref, other_ref, out_ref, *, scale):
    half = out_ref.shape[0] // 2
    size = mine_ref.shape[1]
    for ref, which in ((mine_ref, core_ref[0]), (other_ref, 1 - core_ref[0])):
        for y in range(4):
            for x in range(4):
                at = which * half + (x * 4 + y) * size
                out_ref[pl.ds(pl.multiple_of(at, size), size), :] = ref[y * 4 + x] * scale


def backward_kernel(du_ref, weight_ref, high_ref, low_ref, out_ref):
    du = du_ref[...]
    dz = (1.0 - BETA) * du + BETA * dot3(split(du), split(weight_ref[...]), 1, 1)
    out_ref[...] = (1.0 - ALPHA) * dot3((high_ref[...], low_ref[...]), split(dz), 0, 0)
    out_ref.push()


def history_kernel(which_ref, dest_ref, recv_ref, base_ref, out_ref, high_ref, low_ref):
    owners = recv_ref.shape[0] // 16
    for s in range(4):
        for l in range(4):
            high, low = split(recv_ref[pl.ds(4 * l + s, owners, stride=16), :])
            at = slice(s * owners, (s + 1) * owners)
            high_ref[at, l * 128 : (l + 1) * 128] = high
            low_ref[at, l * 128 : (l + 1) * 128] = low
    dest = dest_ref[pl.ds(which_ref[0], 1), :]
    step = out_ref.rows
    for block in range(out_ref.shape[0] // step):
        ids = lax.broadcasted_iota(jnp.int32, (step, dest.shape[1]), 0) + block * step
        hit = jnp.where(ids == dest, 1.0, 0.0)
        count = jnp.sum(hit, axis=1, keepdims=True)
        place = hit.astype(BF16)
        written = dot(place, high_ref[...]) + dot(place, low_ref[...])
        at = slice(block * step, (block + 1) * step)
        base_ref.part(block)
        out_ref[at, :] = jnp.where(count > 0.5, written, base_ref.buffer[at, :])
        out_ref.push(block)


def write_rows(which, dest, recv, base):
    rows, width = dest.shape[1], base.shape[1]
    return call(
        history_kernel,
        [(base.shape, F32)],
        (which, dest, recv, base),
        spaces="svvhh",
        scratch=[pltpu.VMEM((rows, width), BF16), pltpu.VMEM((rows, width), BF16)],
        limit=52,
        flops=2 * 10**9,
        chunks=5,
    )[0]


def exchange(v, axes=OWN):
    return lax.all_to_all(v, axes, split_axis=0, concat_axis=0, tiled=True)


def swap(v):
    return lax.ppermute(v, "rep", [(0, 1), (1, 0)])


def move(v, axis, mask):
    count = lax.axis_size(axis)
    return lax.ppermute(v, axis, [(i, i ^ mask) for i in range(count)])


def scatter(me, *terms):
    size = terms[0].shape[0] // 4
    return call(
        scatter_kernel,
        [((size, terms[0].shape[1]), F32)] * 4,
        (me,) + terms,
        spaces="s" + "v" * (len(terms) + 4),
        scratch=[pltpu.VMEM(terms[0].shape, F32)],
    )


def trade(pieces, axis):
    return [pieces[0]] + [move(pieces[shift], axis, shift) for shift in (1, 2, 3)]


def total(*terms):
    return call(total_kernel, [(terms[0].shape, F32)], terms)[0]


def together(*values):
    return lax.optimization_barrier(values)


def body(
    node_input,
    initial,
    cotangent,
    weight,
    edge_weight,
    neighbors,
    halo_rows,
    cold_history,
    hot_history,
    dest_rows,
):
    rows, width = node_input.shape
    owners = lax.axis_size(OWN)
    halo_count = owners * halo_rows.shape[2]
    core = lax.axis_index("rep").astype(jnp.int32).reshape(1)
    at_x = lax.axis_index("hist").astype(jnp.int32).reshape(1)
    at_y = lax.axis_index("y").astype(jnp.int32).reshape(1)
    full = (rows, width)
    half = (rows // 2, width)
    nbr = neighbors.T
    ew = edge_weight.T
    dest = jnp.transpose(dest_rows.reshape(2, owners, 4), (0, 2, 1)).reshape(2, rows)

    wanted = exchange(halo_rows[0])
    (found,) = call(
        gather_kernel,
        [((halo_count * 4, 128), F32)],
        (wanted, cold_history),
        limit=16,
        flops=10**9,
    )
    halo = exchange(found)
    part, high, low = call(
        functools.partial(prepare_kernel, halo_count=halo_count),
        [(full, F32), ((rows, rows), BF16), ((rows, rows), BF16)],
        (core, nbr, ew, hot_history, swap(hot_history), node_input, initial),
        spaces="svvhhhhhhh",
        limit=60,
        flops=6 * 10**9,
    )
    halo, part = together(halo, part)
    outgoing, keep, give, du = call(
        layer_kernel,
        [((owners // 4, 4, 16, 128), F32), (half, F32), (half, F32), (full, F32)],
        (core, halo, nbr, ew, part, weight, cotangent),
        spaces="svvvhhhhvvh",
        chunks=4,
        scratch=[pltpu.VMEM((width, width), F32), pltpu.VMEM(full, F32)]
        + [pltpu.VMEM(full, BF16)] * 4,
        limit=52,
        flops=3 * 10**9,
    )
    got, dest = together(swap(give), dest)
    pieces = trade(scatter(at_x, keep, got), "hist")
    (grad_input,) = call(
        backward_kernel,
        [(full, F32)],
        (du, weight, high, low),
        spaces="hhhhh",
        limit=60,
        flops=2 * 10**9,
    )
    *pieces, grad_input = together(*pieces, grad_input)
    pieces = trade(scatter(at_y, *pieces), "y")
    arrived = exchange(outgoing.reshape(owners * 16, 128))
    summed = total(*pieces)
    mask = 1
    while 2 * mask < lax.axis_size("z"):
        summed = total(summed, move(summed, "z", mask))
        mask *= 2
    arrived, summed = together(arrived, summed)
    arrived_other = swap(arrived)
    moved = move(summed, "z", mask)
    history = write_rows(core, dest, arrived, cold_history)
    moved, history = together(moved, history)
    plane = lax.axis_size(PLANE)
    (spread,) = call(spread_kernel, [((plane,) + summed.shape, F32)], (summed, moved))
    gathered = exchange(spread, PLANE)
    history = write_rows(1 - core, dest, arrived_other, history)
    gathered, history = together(gathered, history)
    all_nodes = rows * lax.axis_size(ALL)
    (grad_weight,) = call(
        functools.partial(assemble_kernel, scale=BETA / math.sqrt(all_nodes)),
        [((width, width), F32)],
        (core, gathered, swap(gathered)),
        spaces="svvv",
    )
    return (grad_weight, grad_input, history)


def solution(mesh):
    batch, hist, rep = mesh.devices.shape
    mesh = Mesh(mesh.devices.reshape(4, batch // 4, hist, rep), ALL)
    return jax.shard_map(
        body,
        mesh=mesh,
        in_specs=(
            P(ALL, None),
            P(ALL, None),
            P(ALL, None),
            P(),
            P(ALL, None),
            P(ALL, None),
            P(ALL, None, None),
            P(OWN, None),
            P("rep", None),
            P(OWN, None),
        ),
        out_specs=(P(), P(ALL, None), P(OWN, None)),
        check_vma=False,
    )
```

```python
import functools
import math

import jax
import jax.numpy as jnp
from jax import lax
from jax.experimental import pallas as pl
from jax.experimental.pallas import tpu as pltpu
from jax.sharding import Mesh
from jax.sharding import PartitionSpec as P

ALPHA = 0.1
BETA = math.log(1.5)
OWN = ("y", "z", "hist")
PLANE = ("y", "hist")
ALL = ("y", "z", "hist", "rep")
F32 = jnp.float32
BF16 = jnp.bfloat16
GELU_C = math.sqrt(2.0 / math.pi)
GELU_A = 0.044715
VMEM = pl.BlockSpec(memory_space=pltpu.VMEM)
SMEM = pl.BlockSpec(memory_space=pltpu.SMEM)
HBM = pl.BlockSpec(memory_space=pltpu.HBM)
MIB = 1 << 20


def dot(a, b, left=1, right=0):
    return lax.dot_general(a, b, (((left,), (right,)), ((), ())), preferred_element_type=F32)


def split(v):
    high = v.astype(BF16)
    return high, (v - high.astype(F32)).astype(BF16)


def dot3(a, b, left=1, right=0):
    return dot(a[0], b[0], left, right) + (dot(a[0], b[1], left, right) + dot(a[1], b[0], left, right))


def lanes(rows, columns):
    return lax.broadcasted_iota(jnp.int32, (rows, columns), 1)


def one_hot(column, count):
    return (column == lanes(column.shape[0], count)).astype(BF16)


class Source:
    def __init__(self, ref, buffer, sem, chunks=1):
        rows = ref.shape[0] // chunks
        self.buffer, self.copies, self.shape = buffer, [], ref.shape
        for i in range(chunks):
            at = (pl.ds(i * rows, rows),) + (slice(None),) * (len(ref.shape) - 1)
            copy = pltpu.make_async_copy(ref.at[at], buffer.at[at], sem.at[i])
            copy.start()
            self.copies.append(copy)

    def __getitem__(self, index):
        for i in range(len(self.copies)):
            self.part(i)
        return self.buffer[index]

    def part(self, i):
        if self.copies[i] is not None:
            self.copies[i].wait()
        self.copies[i] = None


class Sink:
    def __init__(self, ref, buffer, sem, chunks=1):
        self.ref, self.buffer, self.sem = ref, buffer, sem
        self.rows, self.copies = ref.shape[0] // chunks, []
        self.shape = ref.shape

    def __setitem__(self, index, value):
        self.buffer[index] = value

    def push(self, i=0):
        at = (pl.ds(i * self.rows, self.rows),) + (slice(None),) * (len(self.shape) - 1)
        copy = pltpu.make_async_copy(self.buffer.at[at], self.ref.at[at], self.sem.at[i])
        copy.start()
        self.copies.append(copy)


def call(kernel, outs, args, spaces=None, scratch=(), limit=8, flops=0, chunks=1):
    spaces = spaces or "v" * (len(args) + len(outs))
    shapes = [(a.shape, a.dtype) for a in args] + list(outs)
    where = {"s": SMEM, "v": VMEM, "h": HBM}
    remote = [i for i, space in enumerate(spaces) if space == "h"]
    buffers = [pltpu.VMEM(*shapes[i]) for i in remote]
    sems = [pltpu.SemaphoreType.DMA((chunks,)) for _ in remote]

    def wrapped(*refs):
        refs, rest = list(refs[: len(shapes)]), refs[len(shapes) :]
        sinks = []
        for n, i in enumerate(remote):
            kind = Source if i < len(args) else Sink
            refs[i] = kind(refs[i], rest[n], rest[len(remote) + n], chunks)
            if kind is Sink:
                sinks.append(refs[i])
        kernel(*refs, *rest[2 * len(remote) :])
        for sink in sinks:
            for copy in sink.copies:
                copy.wait()

    count = sum(math.prod(shape) * 4 for shape, _ in shapes)
    return pl.pallas_call(
        wrapped,
        out_shape=[jax.ShapeDtypeStruct(*o) for o in outs],
        in_specs=[where[c] for c in spaces[: len(args)]],
        out_specs=[where[c] for c in spaces[len(args) :]],
        scratch_shapes=buffers + sems + list(scratch),
        compiler_params=pltpu.CompilerParams(vmem_limit_bytes=limit * MIB),
        cost_estimate=pl.CostEstimate(flops=flops, bytes_accessed=count, transcendentals=0),
    )(*args)


def gather_kernel(idx_ref, cold_ref, out_ref):
    owners, per = idx_ref.shape
    high, low = split(cold_ref[...])
    pick = jnp.concatenate(
        [one_hot(idx_ref[:, s : s + 1], cold_ref.shape[0]) for s in range(per)], axis=0
    )
    found = dot(pick, high) + dot(pick, low)
    for s in range(per):
        for l in range(4):
            out_ref[pl.ds(s * 4 + l, owners, stride=per * 4), :] = found[
                s * owners : (s + 1) * owners, l * 128 : (l + 1) * 128
            ]


def prepare_kernel(
    core_ref, nbr_ref, ew_ref, mine_ref, other_ref, node_ref, init_ref,
    part_ref, high_ref, low_ref, *, halo_count,
):
    rows = node_ref.shape[0]
    half = mine_ref.shape[0]
    core = core_ref[0]
    nbr = nbr_ref[...].T
    ew = ew_ref[...].T
    ids = lanes(rows, rows)
    tile = jnp.zeros((rows, rows), F32)
    for k in range(2, nbr.shape[1]):
        tile = tile + jnp.where(nbr[:, k : k + 1] == ids, ew[:, k : k + 1], 0.0)
    tiles = split(tile)
    high_ref[...] = tiles[0]
    low_ref[...] = tiles[1]
    high_ref.push()
    low_ref.push()
    hot = nbr[:, 1:2] - (rows + halo_count)
    picked = jnp.zeros((rows, node_ref.shape[1]), F32)
    for ref, base in ((mine_ref, core * half), (other_ref, (1 - core) * half)):
        choose = one_hot(hot - base, half)
        for piece in split(ref[...]):
            picked = picked + dot(choose, piece)
    agg = dot3(tiles, split(node_ref[...])) + ew[:, 1:2] * picked
    part_ref[...] = (1.0 - ALPHA) * agg + ALPHA * init_ref[...]
    part_ref.push()


def layer_kernel(
    core_ref, halo_ref, nbr_ref, ew_ref, part_ref, weight_ref, cot_ref,
    out_ref, keep_ref, give_ref, du_ref,
    term_ref, work_ref, zhigh_ref, zlow_ref, dhigh_ref, dlow_ref,
):
    owners = halo_ref.shape[0] // 8
    rows = part_ref.shape[0]
    block, step = rows // 4, 32
    halo = jnp.concatenate(
        [
            jnp.concatenate(
                [halo_ref[pl.ds(s * 4 + l, owners, stride=8), :] for l in range(4)], axis=1
            )
            for s in range(2)
        ],
        axis=0,
    )
    place = nbr_ref[...].T[:, :1] - rows
    pick = one_hot((place & 1) * owners + (place >> 1), 2 * owners)
    scale = (1.0 - ALPHA) * ew_ref[...].T[:, :1]
    high, low = split(halo)
    top = lax.broadcasted_iota(jnp.int32, (step // 16, 2, 8, 128), 2) < 4
    for start in range(0, rows, block):
        whole = slice(start, start + block)
        work_ref[whole, :] = dot(pick[whole], high) + dot(pick[whole], low)
        part_ref.part(start // block)
        for first in range(start, start + block, step):
            at = slice(first, first + step)
            z = part_ref.buffer[at, :] + scale[at] * work_ref[at, :]
            zs = split(z)
            work_ref[at, :] = z
            zhigh_ref[at, :] = zs[0]
            zlow_ref[at, :] = zs[1]
    weights = split(weight_ref[...])
    for start in range(0, rows, block):
        whole = slice(start, start + block)
        mixed = dot3((zhigh_ref[whole, :], zlow_ref[whole, :]), weights)
        work_ref[whole, :] = (1.0 - BETA) * work_ref[whole, :] + BETA * mixed
        cot_ref.part(start // block)
        for first in range(start, start + block, step):
            at = slice(first, first + step)
            u = work_ref[at, :]
            square = u * u
            bent = jnp.tanh(GELU_C * (u + GELU_A * (square * u)))
            embed = (0.5 * u) * (1.0 + bent)
            slope = 0.5 * (1.0 + bent) + (0.5 * u) * (1.0 - bent * bent) * (
                GELU_C * (1.0 + (3.0 * GELU_A) * square)
            )
            du = cot_ref.buffer[at, :] * slope
            du_ref[at, :] = du
            ds = split(du)
            dhigh_ref[at, :] = ds[0]
            dlow_ref[at, :] = ds[1]
            group = slice(first // 16, (first + step) // 16)
            for pair in range(2):
                x, y = (
                    embed[:, l * 128 : (l + 1) * 128].reshape(step // 16, 2, 8, 128)
                    for l in (2 * pair, 2 * pair + 1)
                )
                even = jnp.where(top, x, pltpu.roll(y, 4, 2))
                odd = jnp.where(top, pltpu.roll(x, 4, 2), y)
                for h in range(2):
                    out_ref[group, 2 * h, 8 * pair : 8 * pair + 8, :] = even[:, h]
                    out_ref[group, 2 * h + 1, 8 * pair : 8 * pair + 8, :] = odd[:, h]
        out_ref.push(start // block)
        du_ref.push(start // block)
    term_ref[...] = dot3(
        (zhigh_ref[...], zlow_ref[...]), (dhigh_ref[...], dlow_ref[...]), 0, 0
    )
    half = term_ref.shape[0] // 2
    core = core_ref[0]
    keep_ref[...] = term_ref[pl.ds(pl.multiple_of(core * half, half), half), :]
    give_ref[...] = term_ref[pl.ds(pl.multiple_of((1 - core) * half, half), half), :]


def scatter_kernel(me_ref, *refs):
    terms, outs, total_ref = refs[: -1 - 4], refs[-1 - 4 : -1], refs[-1]
    total_ref[...] = functools.reduce(lambda x, y: x + y, [t[...] for t in terms])
    size = outs[0].shape[0]
    for shift, out in enumerate(outs):
        at = jnp.bitwise_xor(me_ref[0], shift) * size
        out[...] = total_ref[pl.ds(pl.multiple_of(at, size), size), :]


def total_kernel(*refs):
    terms = [t[...] for t in refs[:-1]]
    while len(terms) > 1:
        terms = [x + y for x, y in zip(terms[::2], terms[1::2])]
    refs[-1][...] = terms[0]


def spread_kernel(mine_ref, other_ref, out_ref):
    out_ref[...] = jnp.broadcast_to((mine_ref[...] + other_ref[...])[None], out_ref.shape)


def assemble_kernel(core_ref, mine_ref, other_ref, out_ref, *, scale):
    half = out_ref.shape[0] // 2
    size = mine_ref.shape[1]
    for ref, which in ((mine_ref, core_ref[0]), (other_ref, 1 - core_ref[0])):
        for y in range(4):
            for x in range(4):
                at = which * half + (x * 4 + y) * size
                out_ref[pl.ds(pl.multiple_of(at, size), size), :] = ref[y * 4 + x] * scale


def backward_kernel(du_ref, weight_ref, high_ref, low_ref, out_ref):
    du = du_ref[...]
    dz = (1.0 - BETA) * du + BETA * dot3(split(du), split(weight_ref[...]), 1, 1)
    out_ref[...] = (1.0 - ALPHA) * dot3((high_ref[...], low_ref[...]), split(dz), 0, 0)
    out_ref.push()


def history_kernel(which_ref, dest_ref, recv_ref, base_ref, out_ref, high_ref, low_ref):
    owners = recv_ref.shape[0] // 16
    for s in range(4):
        for l in range(4):
            high, low = split(recv_ref[pl.ds(4 * l + s, owners, stride=16), :])
            at = slice(s * owners, (s + 1) * owners)
            high_ref[at, l * 128 : (l + 1) * 128] = high
            low_ref[at, l * 128 : (l + 1) * 128] = low
    dest = dest_ref[pl.ds(which_ref[0], 1), :]
    step = out_ref.rows
    for block in range(out_ref.shape[0] // step):
        ids = lax.broadcasted_iota(jnp.int32, (step, dest.shape[1]), 0) + block * step
        hit = jnp.where(ids == dest, 1.0, 0.0)
        count = jnp.sum(hit, axis=1, keepdims=True)
        place = hit.astype(BF16)
        written = dot(place, high_ref[...]) + dot(place, low_ref[...])
        at = slice(block * step, (block + 1) * step)
        base_ref.part(block)
        out_ref[at, :] = jnp.where(count > 0.5, written, base_ref.buffer[at, :])
        out_ref.push(block)


def write_rows(which, dest, recv, base):
    rows, width = dest.shape[1], base.shape[1]
    return call(
        history_kernel,
        [(base.shape, F32)],
        (which, dest, recv, base),
        spaces="svvhh",
        scratch=[pltpu.VMEM((rows, width), BF16), pltpu.VMEM((rows, width), BF16)],
        limit=52,
        flops=2 * 10**9,
        chunks=5,
    )[0]


def exchange(v, axes=OWN):
    return lax.all_to_all(v, axes, split_axis=0, concat_axis=0, tiled=True)


def swap(v):
    return lax.ppermute(v, "rep", [(0, 1), (1, 0)])


def move(v, axis, mask):
    count = lax.axis_size(axis)
    return lax.ppermute(v, axis, [(i, i ^ mask) for i in range(count)])


def scatter(me, *terms):
    size = terms[0].shape[0] // 4
    return call(
        scatter_kernel,
        [((size, terms[0].shape[1]), F32)] * 4,
        (me,) + terms,
        spaces="s" + "v" * (len(terms) + 4),
        scratch=[pltpu.VMEM(terms[0].shape, F32)],
    )


def trade(pieces, axis):
    return [pieces[0]] + [move(pieces[shift], axis, shift) for shift in (1, 2, 3)]


def total(*terms):
    return call(total_kernel, [(terms[0].shape, F32)], terms)[0]


def together(*values):
    return lax.optimization_barrier(values)


def body(
    node_input,
    initial,
    cotangent,
    weight,
    edge_weight,
    neighbors,
    halo_rows,
    cold_history,
    hot_history,
    dest_rows,
):
    rows, width = node_input.shape
    owners = lax.axis_size(OWN)
    halo_count = owners * halo_rows.shape[2]
    core = lax.axis_index("rep").astype(jnp.int32).reshape(1)
    at_x = lax.axis_index("hist").astype(jnp.int32).reshape(1)
    at_y = lax.axis_index("y").astype(jnp.int32).reshape(1)
    full = (rows, width)
    half = (rows // 2, width)
    nbr = neighbors.T
    ew = edge_weight.T
    dest = jnp.transpose(dest_rows.reshape(2, owners, 4), (0, 2, 1)).reshape(2, rows)

    wanted = exchange(halo_rows[0])
    (found,) = call(
        gather_kernel,
        [((halo_count * 4, 128), F32)],
        (wanted, cold_history),
        limit=16,
        flops=10**9,
    )
    halo = exchange(found)
    part, high, low = call(
        functools.partial(prepare_kernel, halo_count=halo_count),
        [(full, F32), ((rows, rows), BF16), ((rows, rows), BF16)],
        (core, nbr, ew, hot_history, swap(hot_history), node_input, initial),
        spaces="svvhhhhhhh",
        limit=60,
        flops=6 * 10**9,
    )
    halo, part = together(halo, part)
    outgoing, keep, give, du = call(
        layer_kernel,
        [((owners // 4, 4, 16, 128), F32), (half, F32), (half, F32), (full, F32)],
        (core, halo, nbr, ew, part, weight, cotangent),
        spaces="svvvhhhhvvh",
        chunks=4,
        scratch=[pltpu.VMEM((width, width), F32), pltpu.VMEM(full, F32)]
        + [pltpu.VMEM(full, BF16)] * 4,
        limit=52,
        flops=3 * 10**9,
    )
    got, dest = together(swap(give), dest)
    pieces = trade(scatter(at_x, keep, got), "hist")
    (grad_input,) = call(
        backward_kernel,
        [(full, F32)],
        (du, weight, high, low),
        spaces="hhhhh",
        limit=60,
        flops=2 * 10**9,
    )
    *pieces, grad_input = together(*pieces, grad_input)
    pieces = trade(scatter(at_y, *pieces), "y")
    arrived = exchange(outgoing.reshape(owners * 16, 128))
    summed = total(*pieces)
    mask = lax.axis_size("z") // 2
    while mask > 1:
        summed = total(summed, move(summed, "z", mask))
        mask //= 2
    plane = lax.axis_size(PLANE)
    (spread,) = call(
        spread_kernel, [((plane,) + summed.shape, F32)], (summed, move(summed, "z", mask))
    )
    arrived, spread = together(arrived, spread)
    arrived_other = swap(arrived)
    gathered = exchange(spread, PLANE)
    history = write_rows(core, dest, arrived, cold_history)
    history = write_rows(1 - core, dest, arrived_other, history)
    gathered, history = together(gathered, history)
    all_nodes = rows * lax.axis_size(ALL)
    (grad_weight,) = call(
        functools.partial(assemble_kernel, scale=BETA / math.sqrt(all_nodes)),
        [((width, width), F32)],
        (core, gathered, swap(gathered)),
        spaces="svvv",
    )
    return (grad_weight, grad_input, history)


def solution(mesh):
    batch, hist, rep = mesh.devices.shape
    mesh = Mesh(mesh.devices.reshape(4, batch // 4, hist, rep), ALL)
    return jax.shard_map(
        body,
        mesh=mesh,
        in_specs=(
            P(ALL, None),
            P(ALL, None),
            P(ALL, None),
            P(),
            P(ALL, None),
            P(ALL, None),
            P(ALL, None, None),
            P(OWN, None),
            P("rep", None),
            P(OWN, None),
        ),
        out_specs=(P(), P(ALL, None), P(OWN, None)),
        check_vma=False,
    )
```

```python
import functools
import math

import jax
import jax.numpy as jnp
from jax import lax
from jax.experimental import pallas as pl
from jax.experimental.pallas import tpu as pltpu
from jax.sharding import Mesh
from jax.sharding import PartitionSpec as P

ALPHA = 0.1
BETA = math.log(1.5)
OWN = ("y", "z", "hist")
PLANE = ("y", "hist")
ALL = ("y", "z", "hist", "rep")
F32 = jnp.float32
BF16 = jnp.bfloat16
GELU_C = math.sqrt(2.0 / math.pi)
GELU_A = 0.044715
VMEM = pl.BlockSpec(memory_space=pltpu.VMEM)
SMEM = pl.BlockSpec(memory_space=pltpu.SMEM)
HBM = pl.BlockSpec(memory_space=pltpu.HBM)
MIB = 1 << 20


def dot(a, b, left=1, right=0):
    return lax.dot_general(a, b, (((left,), (right,)), ((), ())), preferred_element_type=F32)


def split(v):
    high = v.astype(BF16)
    return high, (v - high.astype(F32)).astype(BF16)


def dot3(a, b, left=1, right=0):
    return dot(a[0], b[0], left, right) + (dot(a[0], b[1], left, right) + dot(a[1], b[0], left, right))


def lanes(rows, columns):
    return lax.broadcasted_iota(jnp.int32, (rows, columns), 1)


def one_hot(column, count):
    return (column == lanes(column.shape[0], count)).astype(BF16)


class Source:
    def __init__(self, ref, buffer, sem, chunks=1):
        rows = ref.shape[0] // chunks
        self.buffer, self.copies, self.shape = buffer, [], ref.shape
        for i in range(chunks):
            at = (pl.ds(i * rows, rows),) + (slice(None),) * (len(ref.shape) - 1)
            copy = pltpu.make_async_copy(ref.at[at], buffer.at[at], sem.at[i])
            copy.start()
            self.copies.append(copy)

    def __getitem__(self, index):
        for i in range(len(self.copies)):
            self.part(i)
        return self.buffer[index]

    def part(self, i):
        if self.copies[i] is not None:
            self.copies[i].wait()
        self.copies[i] = None


class Sink:
    def __init__(self, ref, buffer, sem, chunks=1):
        self.ref, self.buffer, self.sem = ref, buffer, sem
        self.rows, self.copies = ref.shape[0] // chunks, []
        self.shape = ref.shape

    def __setitem__(self, index, value):
        self.buffer[index] = value

    def push(self, i=0):
        at = (pl.ds(i * self.rows, self.rows),) + (slice(None),) * (len(self.shape) - 1)
        copy = pltpu.make_async_copy(self.buffer.at[at], self.ref.at[at], self.sem.at[i])
        copy.start()
        self.copies.append(copy)


def call(kernel, outs, args, spaces=None, scratch=(), limit=8, flops=0, chunks=1):
    spaces = spaces or "v" * (len(args) + len(outs))
    shapes = [(a.shape, a.dtype) for a in args] + list(outs)
    where = {"s": SMEM, "v": VMEM, "h": HBM}
    remote = [i for i, space in enumerate(spaces) if space == "h"]
    buffers = [pltpu.VMEM(*shapes[i]) for i in remote]
    sems = [pltpu.SemaphoreType.DMA((chunks,)) for _ in remote]

    def wrapped(*refs):
        refs, rest = list(refs[: len(shapes)]), refs[len(shapes) :]
        sinks = []
        for n, i in enumerate(remote):
            kind = Source if i < len(args) else Sink
            refs[i] = kind(refs[i], rest[n], rest[len(remote) + n], chunks)
            if kind is Sink:
                sinks.append(refs[i])
        kernel(*refs, *rest[2 * len(remote) :])
        for sink in sinks:
            for copy in sink.copies:
                copy.wait()

    count = sum(math.prod(shape) * 4 for shape, _ in shapes)
    return pl.pallas_call(
        wrapped,
        out_shape=[jax.ShapeDtypeStruct(*o) for o in outs],
        in_specs=[where[c] for c in spaces[: len(args)]],
        out_specs=[where[c] for c in spaces[len(args) :]],
        scratch_shapes=buffers + sems + list(scratch),
        compiler_params=pltpu.CompilerParams(vmem_limit_bytes=limit * MIB),
        cost_estimate=pl.CostEstimate(flops=flops, bytes_accessed=count, transcendentals=0),
    )(*args)


def gather_kernel(idx_ref, cold_ref, out_ref):
    owners, per = idx_ref.shape
    high, low = split(cold_ref[...])
    pick = jnp.concatenate(
        [one_hot(idx_ref[:, s : s + 1], cold_ref.shape[0]) for s in range(per)], axis=0
    )
    found = dot(pick, high) + dot(pick, low)
    for s in range(per):
        for l in range(4):
            out_ref[pl.ds(s * 4 + l, owners, stride=per * 4), :] = found[
                s * owners : (s + 1) * owners, l * 128 : (l + 1) * 128
            ]


def prepare_kernel(
    core_ref, nbr_ref, ew_ref, mine_ref, other_ref, node_ref, init_ref,
    part_ref, high_ref, low_ref, *, halo_count,
):
    rows = node_ref.shape[0]
    half = mine_ref.shape[0]
    core = core_ref[0]
    nbr = nbr_ref[...].T
    ew = ew_ref[...].T
    ids = lanes(rows, rows)
    tile = jnp.zeros((rows, rows), F32)
    for k in range(2, nbr.shape[1]):
        tile = tile + jnp.where(nbr[:, k : k + 1] == ids, ew[:, k : k + 1], 0.0)
    tiles = split(tile)
    high_ref[...] = tiles[0]
    low_ref[...] = tiles[1]
    high_ref.push()
    low_ref.push()
    hot = nbr[:, 1:2] - (rows + halo_count)
    picked = jnp.zeros((rows, node_ref.shape[1]), F32)
    for ref, base in ((mine_ref, core * half), (other_ref, (1 - core) * half)):
        choose = one_hot(hot - base, half)
        for piece in split(ref[...]):
            picked = picked + dot(choose, piece)
    agg = dot3(tiles, split(node_ref[...])) + ew[:, 1:2] * picked
    part_ref[...] = (1.0 - ALPHA) * agg + ALPHA * init_ref[...]
    part_ref.push()


def layer_kernel(
    core_ref, halo_ref, nbr_ref, ew_ref, part_ref, weight_ref, cot_ref,
    out_ref, keep_ref, give_ref, du_ref,
    term_ref, work_ref, zhigh_ref, zlow_ref, dhigh_ref, dlow_ref,
):
    owners = halo_ref.shape[0] // 8
    rows = part_ref.shape[0]
    block, step = rows // 4, 32
    halo = jnp.concatenate(
        [
            jnp.concatenate(
                [halo_ref[pl.ds(s * 4 + l, owners, stride=8), :] for l in range(4)], axis=1
            )
            for s in range(2)
        ],
        axis=0,
    )
    place = nbr_ref[...].T[:, :1] - rows
    pick = one_hot((place & 1) * owners + (place >> 1), 2 * owners)
    scale = (1.0 - ALPHA) * ew_ref[...].T[:, :1]
    high, low = split(halo)
    top = lax.broadcasted_iota(jnp.int32, (step // 16, 2, 8, 128), 2) < 4
    for start in range(0, rows, block):
        whole = slice(start, start + block)
        work_ref[whole, :] = dot(pick[whole], high) + dot(pick[whole], low)
        part_ref.part(start // block)
        for first in range(start, start + block, step):
            at = slice(first, first + step)
            z = part_ref.buffer[at, :] + scale[at] * work_ref[at, :]
            zs = split(z)
            work_ref[at, :] = z
            zhigh_ref[at, :] = zs[0]
            zlow_ref[at, :] = zs[1]
    weights = split(weight_ref[...])
    for start in range(0, rows, block):
        whole = slice(start, start + block)
        mixed = dot3((zhigh_ref[whole, :], zlow_ref[whole, :]), weights)
        work_ref[whole, :] = (1.0 - BETA) * work_ref[whole, :] + BETA * mixed
        cot_ref.part(start // block)
        for first in range(start, start + block, step):
            at = slice(first, first + step)
            u = work_ref[at, :]
            square = u * u
            bent = jnp.tanh(GELU_C * (u + GELU_A * (square * u)))
            embed = (0.5 * u) * (1.0 + bent)
            slope = 0.5 * (1.0 + bent) + (0.5 * u) * (1.0 - bent * bent) * (
                GELU_C * (1.0 + (3.0 * GELU_A) * square)
            )
            du = cot_ref.buffer[at, :] * slope
            du_ref[at, :] = du
            ds = split(du)
            dhigh_ref[at, :] = ds[0]
            dlow_ref[at, :] = ds[1]
            group = slice(first // 16, (first + step) // 16)
            for pair in range(2):
                x, y = (
                    embed[:, l * 128 : (l + 1) * 128].reshape(step // 16, 2, 8, 128)
                    for l in (2 * pair, 2 * pair + 1)
                )
                even = jnp.where(top, x, pltpu.roll(y, 4, 2))
                odd = jnp.where(top, pltpu.roll(x, 4, 2), y)
                for h in range(2):
                    out_ref[group, 2 * h, 8 * pair : 8 * pair + 8, :] = even[:, h]
                    out_ref[group, 2 * h + 1, 8 * pair : 8 * pair + 8, :] = odd[:, h]
        out_ref.push(start // block)
        du_ref.push(start // block)
    term_ref[...] = dot3(
        (zhigh_ref[...], zlow_ref[...]), (dhigh_ref[...], dlow_ref[...]), 0, 0
    )
    half = term_ref.shape[0] // 2
    core = core_ref[0]
    keep_ref[...] = term_ref[pl.ds(pl.multiple_of(core * half, half), half), :]
    give_ref[...] = term_ref[pl.ds(pl.multiple_of((1 - core) * half, half), half), :]


def scatter_kernel(me_ref, *refs):
    terms, outs, total_ref = refs[: -1 - 4], refs[-1 - 4 : -1], refs[-1]
    total_ref[...] = functools.reduce(lambda x, y: x + y, [t[...] for t in terms])
    size = outs[0].shape[0]
    for shift, out in enumerate(outs):
        at = jnp.bitwise_xor(me_ref[0], shift) * size
        out[...] = total_ref[pl.ds(pl.multiple_of(at, size), size), :]


def total_kernel(*refs):
    terms = [t[...] for t in refs[:-1]]
    while len(terms) > 1:
        terms = [x + y for x, y in zip(terms[::2], terms[1::2])]
    refs[-1][...] = terms[0]


def spread_kernel(mine_ref, other_ref, out_ref):
    out_ref[...] = jnp.broadcast_to((mine_ref[...] + other_ref[...])[None], out_ref.shape)


def assemble_kernel(core_ref, mine_ref, other_ref, out_ref, *, scale):
    half = out_ref.shape[0] // 2
    size = mine_ref.shape[1]
    for ref, which in ((mine_ref, core_ref[0]), (other_ref, 1 - core_ref[0])):
        for y in range(4):
            for x in range(4):
                at = which * half + (x * 4 + y) * size
                out_ref[pl.ds(pl.multiple_of(at, size), size), :] = ref[y * 4 + x] * scale


def backward_kernel(du_ref, weight_ref, high_ref, low_ref, out_ref):
    du = du_ref[...]
    dz = (1.0 - BETA) * du + BETA * dot3(split(du), split(weight_ref[...]), 1, 1)
    out_ref[...] = (1.0 - ALPHA) * dot3((high_ref[...], low_ref[...]), split(dz), 0, 0)
    out_ref.push()


def history_kernel(
    core_ref, dest_ref, mine_ref, other_ref, base_ref, out_ref, high_ref, low_ref
):
    owners = mine_ref.shape[0] // 16
    rows = 4 * owners
    for r, ref in enumerate((mine_ref, other_ref)):
        for s in range(4):
            for l in range(4):
                high, low = split(ref[pl.ds(4 * l + s, owners, stride=16), :])
                at = slice(r * rows + s * owners, r * rows + (s + 1) * owners)
                high_ref[at, l * 128 : (l + 1) * 128] = high
                low_ref[at, l * 128 : (l + 1) * 128] = low
    core = core_ref[0]
    dest = jnp.concatenate(
        [dest_ref[pl.ds(core, 1), :], dest_ref[pl.ds(1 - core, 1), :]], axis=1
    )
    step = out_ref.rows
    for block in range(out_ref.shape[0] // step):
        ids = lax.broadcasted_iota(jnp.int32, (step, 2 * rows), 0) + block * step
        hit = jnp.where(ids == dest, 1.0, 0.0)
        count = jnp.sum(hit, axis=1, keepdims=True)
        place = hit.astype(BF16)
        written = dot(place, high_ref[...]) + dot(place, low_ref[...])
        at = slice(block * step, (block + 1) * step)
        base_ref.part(block)
        out_ref[at, :] = jnp.where(count > 0.5, written, base_ref.buffer[at, :])
        out_ref.push(block)


def write_rows(core, dest, mine, other, base):
    rows, width = 2 * dest.shape[1], base.shape[1]
    return call(
        history_kernel,
        [(base.shape, F32)],
        (core, dest, mine, other, base),
        spaces="svvvhh",
        scratch=[pltpu.VMEM((rows, width), BF16), pltpu.VMEM((rows, width), BF16)],
        limit=52,
        flops=4 * 10**9,
        chunks=5,
    )[0]


def exchange(v, axes=OWN):
    return lax.all_to_all(v, axes, split_axis=0, concat_axis=0, tiled=True)


def swap(v):
    return lax.ppermute(v, "rep", [(0, 1), (1, 0)])


def move(v, axis, mask):
    count = lax.axis_size(axis)
    return lax.ppermute(v, axis, [(i, i ^ mask) for i in range(count)])


def scatter(me, *terms):
    size = terms[0].shape[0] // 4
    return call(
        scatter_kernel,
        [((size, terms[0].shape[1]), F32)] * 4,
        (me,) + terms,
        spaces="s" + "v" * (len(terms) + 4),
        scratch=[pltpu.VMEM(terms[0].shape, F32)],
    )


def trade(pieces, axis):
    return [pieces[0]] + [move(pieces[shift], axis, shift) for shift in (1, 2, 3)]


def total(*terms):
    return call(total_kernel, [(terms[0].shape, F32)], terms)[0]


def together(*values):
    return lax.optimization_barrier(values)


def body(
    node_input,
    initial,
    cotangent,
    weight,
    edge_weight,
    neighbors,
    halo_rows,
    cold_history,
    hot_history,
    dest_rows,
):
    rows, width = node_input.shape
    owners = lax.axis_size(OWN)
    halo_count = owners * halo_rows.shape[2]
    core = lax.axis_index("rep").astype(jnp.int32).reshape(1)
    at_x = lax.axis_index("hist").astype(jnp.int32).reshape(1)
    at_y = lax.axis_index("y").astype(jnp.int32).reshape(1)
    full = (rows, width)
    half = (rows // 2, width)
    nbr = neighbors.T
    ew = edge_weight.T
    dest = jnp.transpose(dest_rows.reshape(2, owners, 4), (0, 2, 1)).reshape(2, rows)

    wanted = exchange(halo_rows[0])
    (found,) = call(
        gather_kernel,
        [((halo_count * 4, 128), F32)],
        (wanted, cold_history),
        limit=16,
        flops=10**9,
    )
    halo = exchange(found)
    part, high, low = call(
        functools.partial(prepare_kernel, halo_count=halo_count),
        [(full, F32), ((rows, rows), BF16), ((rows, rows), BF16)],
        (core, nbr, ew, hot_history, swap(hot_history), node_input, initial),
        spaces="svvhhhhhhh",
        limit=60,
        flops=6 * 10**9,
    )
    halo, part = together(halo, part)
    outgoing, keep, give, du = call(
        layer_kernel,
        [((owners // 4, 4, 16, 128), F32), (half, F32), (half, F32), (full, F32)],
        (core, halo, nbr, ew, part, weight, cotangent),
        spaces="svvvhhhhvvh",
        chunks=4,
        scratch=[pltpu.VMEM((width, width), F32), pltpu.VMEM(full, F32)]
        + [pltpu.VMEM(full, BF16)] * 4,
        limit=52,
        flops=3 * 10**9,
    )
    got, dest = together(swap(give), dest)
    pieces = trade(scatter(at_x, keep, got), "hist")
    (grad_input,) = call(
        backward_kernel,
        [(full, F32)],
        (du, weight, high, low),
        spaces="hhhhh",
        limit=60,
        flops=2 * 10**9,
    )
    *pieces, grad_input = together(*pieces, grad_input)
    pieces = trade(scatter(at_y, *pieces), "y")
    arrived = exchange(outgoing.reshape(owners * 16, 128))
    summed = total(*pieces)
    mask = 1
    while 2 * mask < lax.axis_size("z"):
        summed = total(summed, move(summed, "z", mask))
        mask *= 2
    plane = lax.axis_size(PLANE)
    (spread,) = call(
        spread_kernel, [((plane,) + summed.shape, F32)], (summed, move(summed, "z", mask))
    )
    arrived, spread = together(arrived, spread)
    arrived_other = swap(arrived)
    gathered = exchange(spread, PLANE)
    history = write_rows(core, dest, arrived, arrived_other, cold_history)
    gathered, history = together(gathered, history)
    all_nodes = rows * lax.axis_size(ALL)
    (grad_weight,) = call(
        functools.partial(assemble_kernel, scale=BETA / math.sqrt(all_nodes)),
        [((width, width), F32)],
        (core, gathered, swap(gathered)),
        spaces="svvv",
    )
    return (grad_weight, grad_input, history)


def solution(mesh):
    batch, hist, rep = mesh.devices.shape
    mesh = Mesh(mesh.devices.reshape(4, batch // 4, hist, rep), ALL)
    return jax.shard_map(
        body,
        mesh=mesh,
        in_specs=(
            P(ALL, None),
            P(ALL, None),
            P(ALL, None),
            P(),
            P(ALL, None),
            P(ALL, None),
            P(ALL, None, None),
            P(OWN, None),
            P("rep", None),
            P(OWN, None),
        ),
        out_specs=(P(), P(ALL, None), P(OWN, None)),
        check_vma=False,
    )
```
